32 devices in a mesh: groups: 2 (over y), frame: 16 (over z, x, core).
Axes of the slice: x: 2, y: 2, z: 4, core: 2. Of those that a mesh axis runs over, the one named last changes fastest.
Arguments:
- queries: bfloat16 [8192, 1536], P(('groups', 'frame')), parts along dimension 0, may hold values from -14 to 14
- key_heads: bfloat16 [8192, 1536], P(('groups', 'frame')), parts along dimension 0, may hold values from -14 to 14
- value_heads: bfloat16 [8192, 1536], P(('groups', 'frame')), parts along dimension 0, may hold values from -6 to 6
- tile_lists: int32 [16, 8], P('frame'), may hold values from 0 to 1
Outputs:
- attended: bfloat16 [8192, 1536], P(('groups', 'frame')), parts along dimension 0
The draws below stay inside these ranges and needn't reach their ends.
There are 2 independent parts, one for each index of `groups`. The reference program is written for one: setup_inputs(seed, part) draws one part's arguments, and reference() takes and returns one part's arrays. A program takes and returns all parts, laid end to end along the dimension named above; an argument that names none is the same for every part. Nothing has to cross between parts.
Inputs may be any that keep to these rules, and one draw needn't show every extreme that they name: `tile_lists`: entry l of a frame's row names a block of the frame 2^l before it, entry 4 + l one of the frame 2^l after it; entries for frames outside the video are not read.
All inputs are finite; a program needn't handle non-finite values.
Results may differ from the reference program's by a relative error of at most 0.0049.
Values may be sent and summed in bfloat16 or wider, within the bound.
No kernel may reach another device: no remote copies, remote signals or barrier semaphores. Data moves between devices by JAX's collectives and lax.ppermute only.
A program may use at most 64 MiB of HBM per device.

```python
import math
import jax
import jax.numpy as jnp
from jax import lax

HEADS = 12
HD = 128
TILE = 128
TF = 2
LEVELS = 4
FRAMES = 16
TOKENS = 4096
HC = 1536


def pair_draw(key):
    shape = (TOKENS, HEADS * HD)
    query_base = 1.4 * jnp.clip(jax.random.normal(jax.random.fold_in(key, 11), shape, jnp.float32), -4.0, 4.0)
    key_base = 1.4 * jnp.clip(jax.random.normal(jax.random.fold_in(key, 12), shape, jnp.float32), -4.0, 4.0)
    return (query_base, key_base)


def draw_queries(key, part):
    return pair_draw(key)[0].astype(jnp.bfloat16)


def draw_key_heads(key, part):
    return pair_draw(key)[1].astype(jnp.bfloat16)


def place_ends(entries, stream_key, smallest, high):
    longest = entries.shape.index(max(entries.shape))
    spots = []
    for shift in (0, 1):
        where = [jax.random.randint(jax.random.fold_in(stream_key, axis), (), 0, length) for axis, length in enumerate(entries.shape)]
        where[longest] = (where[longest] + shift) % entries.shape[longest]
        spots.append(tuple(where))
    return entries.at[spots[0]].set(smallest).at[spots[1]].set(high)


def steps_of(rng, shape, split, least, largest):
    def one(dim, blocks):
        heights = jax.random.uniform(jax.random.fold_in(jax.random.fold_in(rng, 6), dim), (blocks,), jnp.float32, least / len(split), largest / len(split))
        return jnp.repeat(jnp.exp(heights), shape[dim] // blocks).reshape((-1,) + (1,) * (len(shape) - dim - 1))

    gain = one(*split[0])
    for cut in split[1:]:
        gain = gain * one(*cut)
    return gain


def centred(key, dims, scale, bound, shards=(), kind=jnp.bfloat16):
    result = scale * jax.random.normal(key, dims, jnp.float32)
    if shards:
        result = result * steps_of(key, dims, shards, -0.22, 0.18)
    return jnp.clip(result, -bound, bound).astype(kind)


def setup_inputs(seed: int = 0, part: int = 0) -> dict:
    seeds = jax.random.split(jax.random.key(seed), 5)
    own_keys = jax.random.split(jax.random.fold_in(seeds[4], part), 5)
    return {
        "queries": draw_queries(jax.random.fold_in(jax.random.fold_in(seeds[4], part), 71), part),
        "key_heads": draw_key_heads(jax.random.fold_in(jax.random.fold_in(seeds[4], part), 71), part),
        "value_heads": centred(own_keys[2], (TOKENS, HC), 1.5, 6.0, ((0, 16),)),
        "tile_lists": place_ends(jax.random.randint(seeds[3], (FRAMES, 2 * LEVELS), 0, TF), jax.random.fold_in(seeds[3], 1), 0, TF - 1).astype(jnp.int32),
    }


def attend_block(block_queries, block_keys, block_values, usable):
    scale = 1.0 / math.sqrt(HD)

    def one_head(head):
        offset = head * HD
        head_queries = lax.dynamic_slice_in_dim(block_queries, offset, HD, 1)
        head_keys = lax.dynamic_slice_in_dim(block_keys, offset, HD, 1)
        head_values = lax.dynamic_slice_in_dim(block_values, offset, HD, 1)
        scores = lax.dot_general(head_queries, head_keys, (((1,), (1,)), ((), ())), preferred_element_type=jnp.float32) * scale
        scores = jnp.where(usable[None, :], scores, -jnp.inf)
        peak = lax.optimization_barrier(jnp.max(scores, axis=1, keepdims=True))
        raised = jnp.exp(scores - peak)
        weights = (raised / lax.optimization_barrier(jnp.sum(raised, axis=1, keepdims=True))).astype(jnp.bfloat16)
        return jnp.dot(weights, head_values, preferred_element_type=jnp.float32).astype(jnp.bfloat16)
    per_head = lax.map(one_head, jnp.arange(HEADS, dtype=jnp.int32))
    return jnp.transpose(per_head, (1, 0, 2)).reshape(block_queries.shape[0], HEADS * HD)

def reference(queries, key_heads, value_heads, tile_lists):
    frame_len = TF * TILE
    width = HEADS * HD
    query_frames = queries.reshape(FRAMES, frame_len, width)
    key_frames = key_heads.reshape(FRAMES, frame_len, width)
    value_frames = value_heads.reshape(FRAMES, frame_len, width)

    def per_frame(frame_no):
        own_queries = lax.dynamic_index_in_dim(query_frames, frame_no, 0, keepdims=False)
        own_lists = lax.dynamic_index_in_dim(tile_lists, frame_no, 0, keepdims=False)
        key_parts = [lax.dynamic_index_in_dim(key_frames, frame_no, 0, keepdims=False)]
        value_parts = [lax.dynamic_index_in_dim(value_frames, frame_no, 0, keepdims=False)]
        usable_parts = [jnp.ones((frame_len,), dtype=bool)]
        for upward in (0, 1):
            for level in range(LEVELS):
                distance = 2 ** level
                if upward:
                    source = frame_no + distance
                else:
                    source = frame_no - distance
                inside = (source >= 0) & (source < FRAMES)
                clipped = jnp.clip(source, 0, FRAMES - 1).astype(jnp.int32)
                first_row = (own_lists[upward * LEVELS + level] * TILE).astype(jnp.int32)
                start_index = (clipped, first_row, jnp.int32(0))
                key_parts.append(lax.dynamic_slice(key_frames, start_index, (1, TILE, width))[0])
                value_parts.append(lax.dynamic_slice(value_frames, start_index, (1, TILE, width))[0])
                usable_parts.append(jnp.broadcast_to(inside, (TILE,)))
        return attend_block(own_queries, jnp.concatenate(key_parts, axis=0), jnp.concatenate(value_parts, axis=0), jnp.concatenate(usable_parts, axis=0))
    attended = lax.map(per_frame, jnp.arange(FRAMES, dtype=jnp.int32))
    return attended.reshape(FRAMES * frame_len, width)
```

```python
import functools
import math

import jax
import jax.numpy as jnp
from jax import lax
from jax.experimental import pallas as pl
from jax.experimental.pallas import tpu as pltpu
from jax.sharding import PartitionSpec as P

HD = 128
TILE = 128
STEP_HEADS = 2
LOG2_SCALE = math.log2(math.e) / math.sqrt(HD)


def attend_kernel(wide, tiles, carry_in, final, meta, *refs):
    refs = list(refs)
    q_ref = refs.pop(0)
    sources = []
    if wide:
        sources.append(((refs.pop(0),), (refs.pop(0),), None))
    for n, parts in enumerate(tiles):
        k_refs = [refs.pop(0) for _ in range(parts)]
        v_refs = [refs.pop(0) for _ in range(parts)]
        sources.append((k_refs, v_refs, n))
    if carry_in:
        acc_in, sum_in, max_in = refs.pop(0), refs.pop(0), refs.pop(0)
    rows = q_ref.shape[0]

    def load(some, cols):
        total = some[0][:, cols]
        for other in some[1:]:
            total = total + other[:, cols]
        return total

    def bias_of(n, count):
        if n is None:
            return jnp.zeros((1, count), jnp.float32)
        return jnp.full((1, count), jnp.where(meta[2 * n + 1] > 0, 0.0, -jnp.inf), jnp.float32)

    groups = [[s] for s in sources[:1]] if wide else []
    narrow = sources[1:] if wide else sources
    groups += [narrow[at : at + 2] for at in range(0, len(narrow), 2)]

    for head in range(STEP_HEADS):
        cols = slice(head * HD, (head + 1) * HD)
        query = q_ref[:, cols]
        scores, values = [], []
        for group in groups:
            key = [load(k, cols) for k, _, _ in group]
            value = [load(v, cols) for _, v, _ in group]
            key = key[0] if len(key) == 1 else jnp.concatenate(key, axis=0)
            value = value[0] if len(value) == 1 else jnp.concatenate(value, axis=0)
            part = lax.dot_general(
                query, key, (((1,), (1,)), ((), ())), preferred_element_type=jnp.float32
            )
            part = part * LOG2_SCALE
            if any(n is not None for _, _, n in group):
                bias = [bias_of(n, k[0].shape[0]) for k, _, n in group]
                part = part + (bias[0] if len(bias) == 1 else jnp.concatenate(bias, axis=1))
            scores.append(part)
            values.append(value)
        peak = functools.reduce(
            jnp.maximum, [jnp.max(part, axis=1, keepdims=True) for part in scores]
        )
        if carry_in:
            old = max_in[:, cols]
            peak = jnp.maximum(old, jnp.broadcast_to(peak, (rows, HD)))
            shrink = jnp.exp2(old - peak)
            acc = acc_in[:, cols] * shrink
            total = sum_in[:, cols] * shrink
        else:
            peak = jnp.broadcast_to(peak, (rows, HD))
            acc = total = None
        for part, value in zip(scores, values):
            count = part.shape[1]
            shift = peak if count == HD else jnp.concatenate([peak] * (count // HD), axis=1)
            weight = jnp.exp2(part - shift).astype(jnp.bfloat16)
            both = jnp.concatenate([value, jnp.ones_like(value)], axis=1)
            added = jnp.dot(weight, both, preferred_element_type=jnp.float32)
            acc = added[:, :HD] if acc is None else acc + added[:, :HD]
            total = added[:, HD:] if total is None else total + added[:, HD:]
        if final:
            refs[0][:, cols] = (acc / total).astype(jnp.bfloat16)
        else:
            refs[0][:, cols] = acc
            refs[1][:, cols] = total
            refs[2][:, cols] = peak


def attend(queries, own, tiles, carry, final):
    rows, width = queries.shape
    block = STEP_HEADS * HD
    meta = []
    for _, _, tile, usable in tiles:
        meta += [jnp.asarray(tile, jnp.int32), jnp.asarray(usable, jnp.int32)]
    meta = jnp.stack(meta) if meta else jnp.zeros((2,), jnp.int32)

    whole = pl.BlockSpec((rows, block), lambda step, meta: (0, step))
    operands, specs = [queries], [whole]
    keys_seen = 0
    if own is not None:
        operands += list(own)
        specs += [pl.BlockSpec((own[0].shape[0], block), lambda step, meta: (0, step))] * 2
        keys_seen += own[0].shape[0]
    for n, (keys, values, _, _) in enumerate(tiles):
        spec = pl.BlockSpec((TILE, block), functools.partial(lambda n, step, meta: (meta[2 * n], step), n))
        operands += list(keys) + list(values)
        specs += [spec] * (len(keys) + len(values))
        keys_seen += TILE
    if carry is not None:
        operands += list(carry)
        specs += [whole] * 3
    if final:
        out_shape = jax.ShapeDtypeStruct((rows, width), jnp.bfloat16)
        out_specs = whole
    else:
        out_shape = [jax.ShapeDtypeStruct((rows, width), jnp.float32)] * 3
        out_specs = [whole] * 3
    return pl.pallas_call(
        functools.partial(
            attend_kernel, own is not None, [len(t[0]) for t in tiles], carry is not None, final
        ),
        out_shape=out_shape,
        grid_spec=pltpu.PrefetchScalarGridSpec(
            num_scalar_prefetch=1,
            grid=(width // block,),
            in_specs=specs,
            out_specs=out_specs,
        ),
        compiler_params=pltpu.CompilerParams(vmem_limit_bytes=24 * 1024 * 1024),
        cost_estimate=pl.CostEstimate(
            flops=4 * rows * keys_seen * width,
            bytes_accessed=4 * keys_seen * width + 2 * rows * width,
            transcendentals=rows * keys_seen * (width // HD),
        ),
    )(meta, *operands)


def pick(array, tile):
    return lax.dynamic_slice_in_dim(array, tile * TILE, TILE, 0)


def send(array, route):
    return lax.ppermute(array, "frame", route)


def body_direct(queries, key_heads, value_heads, tile_lists):
    frames = lax.axis_size("frame")
    levels = frames.bit_length() - 1
    me = lax.axis_index("frame")
    lists = jnp.clip(lax.all_gather(tile_lists, "frame", tiled=True), 0, key_heads.shape[0] // TILE - 1)
    tiles = []
    for level in range(levels):
        for entry, distance in ((level, 1 << level), (levels + level, -(1 << level))):
            route = [(i, i + distance) for i in range(frames) if 0 <= i + distance < frames]
            wanted = lists[jnp.clip(me + distance, 0, frames - 1), entry]
            both = jnp.stack([pick(key_heads, wanted), pick(value_heads, wanted)])
            both = send(both, route)
            usable = (me - distance >= 0) & (me - distance < frames)
            tiles.append(([both[0]], [both[1]], 0, usable))
    return attend(queries, (key_heads, value_heads), tiles, None, True)


def body_planes(queries, key_heads, value_heads, tile_lists):
    frames = 16
    me = lax.axis_index("frame")
    spot = me % 4
    levels = 4
    every = range(frames)

    up = [(i, i + 4) for i in every if i + 4 < frames]
    down = [(i, i - 4) for i in every if i - 4 >= 0]
    across = [(i, i ^ 2) for i in every]
    beside = [(i, i ^ 1) for i in every]
    low_k = send(key_heads, up)
    high_k = send(key_heads, down)
    across_k = send(key_heads, across)
    low_v = send(value_heads, up)
    high_v = send(value_heads, down)
    across_v = send(value_heads, across)
    beside_k = send(key_heads, beside)
    beside_v = send(value_heads, beside)
    lists = jnp.clip(lax.all_gather(tile_lists, "frame", tiled=True), 0, key_heads.shape[0] // TILE - 1)

    def wanted(frame, entry):
        return lists[jnp.clip(frame, 0, frames - 1), entry]

    mine = lists[me]

    tile = wanted(me + 4, 3)
    far_low = send(
        jnp.stack([pick(low_k, tile), pick(low_v, tile)]), [(i, i + 4) for i in range(4, 12)]
    )
    tile = wanted(me - 4, levels + 3)
    far_high = send(
        jnp.stack([pick(high_k, tile), pick(high_v, tile)]), [(i, i - 4) for i in range(4, 12)]
    )
    right = spot >= 2
    tile = jnp.where(right, wanted(me - 2, 1), wanted(me + 2, levels + 1))
    two = send(
        jnp.stack(
            [
                jnp.where(right, pick(low_k, tile), pick(high_k, tile)),
                jnp.where(right, pick(low_v, tile), pick(high_v, tile)),
            ]
        ),
        across,
    )
    step = jnp.where(spot == 0, 1, jnp.where(spot == 3, -1, jnp.where(spot == 1, 3, -3)))
    entry = jnp.where((spot == 0) | (spot == 2), levels, 0)
    tile = wanted(me + step, entry)
    route = []
    for i in every:
        j = i + {0: 1, 3: -1, 1: 3, 2: -3}[i % 4]
        if 0 <= j < frames:
            route.append((i, j))
    one = send(jnp.stack([pick(across_k, tile), pick(across_v, tile)]), route)

    odd = spot % 2 == 1
    carry = attend(
        queries,
        (key_heads, value_heads),
        [([beside_k], [beside_v], jnp.where(odd, mine[0], mine[levels]), True)],
        None,
        False,
    )
    carry = attend(
        queries,
        None,
        [
            ([across_k], [across_v], jnp.where(right, mine[1], mine[levels + 1]), True),
            ([low_k], [low_v], mine[2], me >= 4),
            ([high_k], [high_v], mine[levels + 2], me + 4 < frames),
        ],
        carry,
        False,
    )
    two_there = jnp.where(right, me + 2 < frames, me - 2 >= 0)
    one_there = jnp.where(spot == 0, me >= 1, jnp.where(spot == 3, me + 1 < frames, True))
    return attend(
        queries,
        None,
        [
            ([two[0]], [two[1]], 0, two_there),
            ([one[0]], [one[1]], 0, one_there),
            ([far_low[0], far_high[0]], [far_low[1], far_high[1]], 0, True),
        ],
        carry,
        True,
    )


def solution(mesh):
    body = body_planes if mesh.shape["frame"] == 16 else body_direct
    in_specs = (
        P(("groups", "frame"), None),
        P(("groups", "frame"), None),
        P(("groups", "frame"), None),
        P("frame", None),
    )
    out_specs = P(("groups", "frame"), None)
    return jax.shard_map(body, mesh=mesh, in_specs=in_specs, out_specs=out_specs, check_vma=False)
```

```python
import functools
import math

import jax
import jax.numpy as jnp
from jax import lax
from jax.experimental import pallas as pl
from jax.experimental.pallas import tpu as pltpu
from jax.sharding import PartitionSpec as P

HD = 128
TILE = 128
NOTE_ROWS = 16
LOG2_SCALE = math.log2(math.e) / math.sqrt(HD)
VMEM_LIMIT = 24 * 1024 * 1024


def attend_kernel(plan, heads, carry_in, final, meta, *refs):
    refs = list(refs)
    q_ref = refs.pop(0)
    sources = []
    for parts, usable in plan:
        k_refs = [refs.pop(0) for _ in range(parts)]
        v_refs = [refs.pop(0) for _ in range(parts)]
        bias = None
        if usable is not None:
            bias = jnp.where(usable(meta), 0.0, -jnp.inf).astype(jnp.float32)
        sources.append((k_refs, v_refs, bias))
    if carry_in:
        acc_in, sum_in, max_in = refs.pop(0), refs.pop(0), refs.pop(0)
    outs = refs[-1:] if final else refs[-3:]
    rows = q_ref.shape[0]

    def load(some, cols):
        total = some[0][:, cols]
        for other in some[1:]:
            total = total + other[:, cols]
        return total

    groups = [[s] for s in sources if s[0][0].shape[0] > TILE]
    narrow = [s for s in sources if s[0][0].shape[0] == TILE]
    groups += [narrow[at : at + 2] for at in range(0, len(narrow), 2)]

    for head in range(heads):
        cols = slice(head * HD, (head + 1) * HD)
        query = q_ref[:, cols]
        scores, values = [], []
        for group in groups:
            key = jnp.concatenate([load(k, cols) for k, _, _ in group], axis=0)
            values.append(jnp.concatenate([load(v, cols) for _, v, _ in group], axis=0))
            part = lax.dot_general(
                query, key, (((1,), (1,)), ((), ())), preferred_element_type=jnp.float32
            )
            pieces = []
            at = 0
            for k, _, bias in group:
                for _ in range(k[0].shape[0] // TILE):
                    piece = part[:, at : at + TILE] * LOG2_SCALE
                    pieces.append(piece if bias is None else piece + bias)
                    at += TILE
            scores.append(pieces)
        peak = functools.reduce(jnp.maximum, [piece for pieces in scores for piece in pieces])
        peak = jnp.broadcast_to(jnp.max(peak, axis=1, keepdims=True), (rows, HD))
        acc = total = None
        if carry_in:
            old = max_in[:, cols]
            peak = jnp.maximum(old, peak)
            shrink = jnp.exp2(old - peak)
            acc = acc_in[:, cols] * shrink
            total = sum_in[:, cols] * shrink
        for pieces, value in zip(scores, values):
            weight = [jnp.exp2(piece - peak).astype(jnp.bfloat16) for piece in pieces]
            both = jnp.concatenate([value, jnp.ones_like(value)], axis=1)
            added = jnp.dot(
                jnp.concatenate(weight, axis=1), both, preferred_element_type=jnp.float32
            )
            acc = added[:, :HD] if acc is None else acc + added[:, :HD]
            total = added[:, HD:] if total is None else total + added[:, HD:]
        if final:
            outs[0][:, cols] = (acc / total).astype(jnp.bfloat16)
        else:
            outs[0][:, cols] = acc
            outs[1][:, cols] = total
            outs[2][:, cols] = peak


def attend(queries, meta, sources, first, steps, heads, carry=None, final=False, into=None):
    rows, width = queries.shape
    block = heads * HD

    def spec(count, row, column):
        return pl.BlockSpec((count, block), lambda step, meta: (row(meta), column + step))

    def zero(meta):
        return 0

    operands, specs = [queries], [spec(rows, zero, first)]
    plan, keys_seen = [], 0
    for keys, values, usable in sources:
        for array, count, row, column in list(keys) + list(values):
            operands.append(array)
            specs.append(spec(count, row, column))
        keys_seen += keys[0][1]
        plan.append((len(keys), usable))
    if carry is not None:
        operands += list(carry)
        specs += [spec(rows, zero, 0)] * 3
    aliases = {}
    if final:
        out_shape = jax.ShapeDtypeStruct((rows, width), jnp.bfloat16)
        out_specs = spec(rows, zero, first)
        if into is not None:
            aliases = {len(operands) + 1: 0}
            operands.append(into)
            specs.append(pl.BlockSpec(memory_space=pl.ANY))
    else:
        out_shape = [jax.ShapeDtypeStruct((rows, steps * block), jnp.float32)] * 3
        out_specs = [spec(rows, zero, 0)] * 3
    done = steps * block
    return pl.pallas_call(
        functools.partial(attend_kernel, plan, heads, carry is not None, final),
        out_shape=out_shape,
        grid_spec=pltpu.PrefetchScalarGridSpec(
            num_scalar_prefetch=1, grid=(steps,), in_specs=specs, out_specs=out_specs
        ),
        input_output_aliases=aliases,
        compiler_params=pltpu.CompilerParams(vmem_limit_bytes=VMEM_LIMIT),
        cost_estimate=pl.CostEstimate(
            flops=4 * rows * keys_seen * done,
            bytes_accessed=4 * keys_seen * done + 2 * rows * done,
            transcendentals=rows * keys_seen * (done // HD),
        ),
    )(meta, *operands)


def pack_kernel(first, meta, k_ref, v_ref, out_ref, note, sems):
    rows = k_ref.shape[0]
    width = out_ref.shape[1]
    copies = [
        pltpu.make_async_copy(
            ref.at[:, pl.ds(first, width)], out_ref.at[pl.ds(n * rows, rows)], sems.at[n]
        )
        for n, ref in enumerate((k_ref, v_ref))
    ]
    for copy in copies:
        copy.start()
    lane = lax.broadcasted_iota(jnp.int32, note.shape, 1)
    row = jnp.zeros(note.shape, jnp.float32)
    for entry in range(8):
        row = jnp.where(lane == entry, meta[entry].astype(jnp.float32), row)
    note[...] = row.astype(jnp.bfloat16)
    last = pltpu.make_async_copy(note, out_ref.at[pl.ds(2 * rows, NOTE_ROWS)], sems.at[2])
    last.start()
    for copy in copies:
        copy.wait()
    last.wait()


def pack(meta, keys, values, first, width):
    rows = keys.shape[0]
    whole = pl.BlockSpec(memory_space=pl.ANY)
    return pl.pallas_call(
        functools.partial(pack_kernel, first),
        out_shape=jax.ShapeDtypeStruct((2 * rows + NOTE_ROWS, width), jnp.bfloat16),
        in_specs=[pl.BlockSpec(memory_space=pltpu.SMEM), whole, whole],
        out_specs=whole,
        scratch_shapes=[
            pltpu.VMEM((NOTE_ROWS, width), jnp.bfloat16),
            pltpu.SemaphoreType.DMA((3,)),
        ],
        compiler_params=pltpu.CompilerParams(vmem_limit_bytes=VMEM_LIMIT),
        cost_estimate=pl.CostEstimate(flops=0, bytes_accessed=8 * rows * width, transcendentals=0),
    )(meta, keys, values)


def choose_kernel(meta, list_ref, low, high, over, wants, far_up, far_down, two, one, notes, sems):
    rows = 2 * TILE
    spot = meta[8] % 4
    right = spot >= 2
    reads = [
        pltpu.make_async_copy(
            ref.at[pl.ds(2 * rows, NOTE_ROWS), pl.ds(0, HD)], notes.at[n], sems.at[n]
        )
        for n, ref in enumerate((low, high, over))
    ]
    for read in reads:
        read.start()
    for read in reads:
        read.wait()

    def entry(n, at):
        shape = notes.shape[1:]
        here = (lax.broadcasted_iota(jnp.int32, shape, 1) == at) & (
            lax.broadcasted_iota(jnp.int32, shape, 0) == 0
        )
        value = jnp.sum(jnp.where(here, notes[n].astype(jnp.float32), 0.0))
        return jnp.clip(value.astype(jnp.int32), 0, 1)

    up_tile = entry(1, 3)
    down_tile = entry(0, 7)
    two_tile = entry(2, jnp.where(right, 1, 5))
    one_tile = jnp.clip(list_ref[0, jnp.where(spot % 2 == 0, 4, 0)], 0, 1)
    wants[0] = up_tile
    wants[1] = down_tile
    wants[2] = two_tile
    wants[3] = one_tile
    copy_tiles(right, up_tile, down_tile, two_tile, one_tile, low, high, over, far_up, far_down, two, one, sems)


def choose_again_kernel(meta, wants, low, high, over, far_up, far_down, two, one, sems):
    right = meta[8] % 4 >= 2
    copy_tiles(right, wants[0], wants[1], wants[2], wants[3], low, high, over, far_up, far_down, two, one, sems)


def copy_tiles(right, up_tile, down_tile, two_tile, one_tile, low, high, over, far_up, far_down, two, one, sems):
    rows = 2 * TILE

    def copies(src, tile, dst, sem):
        start = pl.multiple_of(tile * TILE, TILE)
        return [
            pltpu.make_async_copy(
                src.at[pl.ds(n * rows + start, TILE)], dst.at[pl.ds(n * TILE, TILE)], sems.at[sem + n]
            )
            for n in (0, 1)
        ]

    always = copies(low, up_tile, far_up, 3) + copies(high, down_tile, far_down, 5) + copies(over, one_tile, one, 7)
    for copy in always:
        copy.start()

    @pl.when(right)
    def _():
        for copy in copies(low, two_tile, two, 9):
            copy.start()

    @pl.when(jnp.logical_not(right))
    def _():
        for copy in copies(high, two_tile, two, 9):
            copy.start()

    for copy in always + copies(low, two_tile, two, 9):
        copy.wait()


def choose(meta, lists, wants, low, high, over):
    width = low.shape[1]
    scalar = pl.BlockSpec(memory_space=pltpu.SMEM)
    whole = pl.BlockSpec(memory_space=pl.ANY)
    sent = jax.ShapeDtypeStruct((2 * TILE, width), jnp.bfloat16)
    again = wants is not None
    outs = ([] if again else [jax.ShapeDtypeStruct((4,), jnp.int32)]) + [sent] * 4
    return pl.pallas_call(
        choose_again_kernel if again else choose_kernel,
        out_shape=outs,
        in_specs=[scalar, scalar] + [whole] * 3,
        out_specs=([] if again else [scalar]) + [whole] * 4,
        scratch_shapes=([] if again else [pltpu.VMEM((3, NOTE_ROWS, HD), jnp.bfloat16)])
        + [pltpu.SemaphoreType.DMA((11,))],
        compiler_params=pltpu.CompilerParams(vmem_limit_bytes=VMEM_LIMIT),
        cost_estimate=pl.CostEstimate(flops=0, bytes_accessed=32 * TILE * width, transcendentals=0),
    )(meta, wants if again else lists, low, high, over)


def send(array, route):
    return lax.ppermute(array, "frame", route)


def fixed(block):
    return lambda meta: block


def body_direct(queries, key_heads, value_heads, tile_lists):
    frames = lax.axis_size("frame")
    levels = frames.bit_length() - 1
    rows, width = key_heads.shape
    me = lax.axis_index("frame")
    lists = jnp.clip(lax.all_gather(tile_lists, "frame", tiled=True), 0, rows // TILE - 1)
    meta = me.astype(jnp.int32).reshape(1)
    sources = [([(key_heads, rows, fixed(0), 0)], [(value_heads, rows, fixed(0), 0)], None)]
    for level in range(levels):
        for entry, distance in ((level, 1 << level), (levels + level, -(1 << level))):
            route = [(i, i + distance) for i in range(frames) if 0 <= i + distance < frames]
            start = lists[jnp.clip(me + distance, 0, frames - 1), entry] * TILE
            both = [lax.dynamic_slice_in_dim(a, start, TILE, 0) for a in (key_heads, value_heads)]
            both = send(jnp.concatenate(both, axis=0), route)

            def usable(meta, distance=distance):
                return (meta[0] >= distance) & (meta[0] - distance < frames)

            sources.append(([(both, TILE, fixed(0), 0)], [(both, TILE, fixed(1), 0)], usable))
    return attend(queries, meta, sources, 0, width // (2 * HD), 2, final=True)


def body_planes(queries, key_heads, value_heads, tile_lists):
    frames = 16
    rows, width = key_heads.shape
    half = width // 2
    heads = 3
    steps = half // (heads * HD)
    every = range(frames)
    meta = jnp.concatenate(
        [jnp.clip(tile_lists[0], 0, rows // TILE - 1), lax.axis_index("frame").astype(jnp.int32).reshape(1)]
    )
    up = [(i, i + 4) for i in every if i + 4 < frames]
    down = [(i, i - 4) for i in every if i - 4 >= 0]
    across = [(i, i ^ 2) for i in every]
    beside = [(i, i ^ 1) for i in every]
    far_up = [(i, i + 4) for i in range(4, 12)]
    far_down = [(i, i - 4) for i in range(4, 12)]
    off_chip = [(i, i + (1, 3, -3, -1)[i % 4]) for i in every]
    off_chip = [(i, j) for i, j in off_chip if 0 <= j < frames]
    back = [(j, i) for i, j in off_chip]

    def right(meta):
        return meta[8] % 4 >= 2

    def beside_tile(meta):
        return jnp.where(meta[8] % 2 == 1, meta[0], meta[4])

    def across_tile(meta):
        return jnp.where(right(meta), meta[1], meta[5])

    def two_there(meta):
        return jnp.where(right(meta), meta[8] + 2 < frames, meta[8] >= 2)

    def one_there(meta):
        return (meta[8] >= 1) & (meta[8] < frames - 1)

    def tile_of(array, tile, usable=None):
        return (
            [(array, TILE, tile, 0)],
            [(array, TILE, lambda meta: tile(meta) + 2, 0)],
            usable,
        )

    def pair_of(arrays, usable=None):
        return [(a, TILE, fixed(0), 0) for a in arrays], [(a, TILE, fixed(1), 0) for a in arrays], usable

    lists = send(tile_lists, back)
    packs = [pack(meta, key_heads, value_heads, n * half, half) for n in (0, 1)]
    wants = None
    carries, finals = [], []
    for n, packed in enumerate(packs):
        low = send(packed, up)
        high = send(packed, down)
        over = send(packed, across)
        next_to = send(packed, beside)
        if wants is None:
            wants, far_low, far_high, two, one = choose(meta, lists, None, low, high, over)
        else:
            far_low, far_high, two, one = choose(meta, None, wants, low, high, over)
        far_low = send(far_low, far_up)
        far_high = send(far_high, far_down)
        two = send(two, across)
        one = send(one, off_chip)
        carry = attend(
            queries,
            meta,
            [
                ([(key_heads, rows, fixed(0), n * steps)], [(value_heads, rows, fixed(0), n * steps)], None),
                tile_of(next_to, beside_tile),
            ],
            n * steps,
            steps,
            heads,
        )
        carry = attend(
            queries,
            meta,
            [
                tile_of(over, across_tile),
                tile_of(low, lambda meta: meta[2], lambda meta: meta[8] >= 4),
                tile_of(high, lambda meta: meta[6], lambda meta: meta[8] + 4 < frames),
            ],
            n * steps,
            steps,
            heads,
            carry,
        )
        carries.append(carry)
        finals.append([pair_of([two], two_there), pair_of([one], one_there), pair_of([far_low, far_high])])
    out = None
    for n in (0, 1):
        out = attend(queries, meta, finals[n], n * steps, steps, heads, carries[n], True, out)
    return out


def solution(mesh):
    body = body_planes if mesh.shape["frame"] == 16 else body_direct
    in_specs = (
        P(("groups", "frame"), None),
        P(("groups", "frame"), None),
        P(("groups", "frame"), None),
        P("frame", None),
    )
    out_specs = P(("groups", "frame"), None)
    return jax.shard_map(body, mesh=mesh, in_specs=in_specs, out_specs=out_specs, check_vma=False)
```

```python
import functools
import math

import jax
import jax.numpy as jnp
from jax import lax
from jax.experimental import pallas as pl
from jax.experimental.pallas import tpu as pltpu
from jax.sharding import PartitionSpec as P

HD = 128
TILE = 128
NOTE_ROWS = 16
LOG2_SCALE = math.log2(math.e) / math.sqrt(HD)
VMEM_LIMIT = 24 * 1024 * 1024


def attend_kernel(plan, heads, carry_in, final, meta, *refs):
    refs = list(refs)
    q_ref = refs.pop(0)
    sources = []
    for parts, usable in plan:
        k_refs = [refs.pop(0) for _ in range(parts)]
        v_refs = [refs.pop(0) for _ in range(parts)]
        bias = None
        if usable is not None:
            bias = jnp.where(usable(meta), 0.0, -jnp.inf).astype(jnp.float32)
        sources.append((k_refs, v_refs, bias))
    if carry_in:
        acc_in, sum_in, max_in = refs.pop(0), refs.pop(0), refs.pop(0)
    outs = refs[-1:] if final else refs[-3:]
    rows = q_ref.shape[0]

    def load(some, cols):
        total = some[0][:, cols]
        for other in some[1:]:
            total = total + other[:, cols]
        return total

    groups = [[s] for s in sources if s[0][0].shape[0] > TILE]
    narrow = [s for s in sources if s[0][0].shape[0] == TILE]
    groups += [narrow[at : at + 2] for at in range(0, len(narrow), 2)]

    def columns(head):
        return slice(head * HD, (head + 1) * HD)

    def scores_of(head):
        cols = columns(head)
        scores = []
        for group in groups:
            key = jnp.concatenate([load(k, cols) for k, _, _ in group], axis=0)
            part = lax.dot_general(
                q_ref[:, cols], key, (((1,), (1,)), ((), ())), preferred_element_type=jnp.float32
            )
            pieces = []
            at = 0
            for k, _, bias in group:
                for _ in range(k[0].shape[0] // TILE):
                    piece = part[:, at : at + TILE] * LOG2_SCALE
                    pieces.append(piece if bias is None else piece + bias)
                    at += TILE
            scores.append(pieces)
        return scores

    def weigh(head, scores):
        peak = functools.reduce(jnp.maximum, [piece for pieces in scores for piece in pieces])
        peak = jnp.broadcast_to(jnp.max(peak, axis=1, keepdims=True), (rows, HD))
        if carry_in:
            peak = jnp.maximum(max_in[:, columns(head)], peak)
        weights = [
            jnp.concatenate([jnp.exp2(piece - peak).astype(jnp.bfloat16) for piece in pieces], axis=1)
            for pieces in scores
        ]
        return peak, weights

    def add_up(head, peak, weights):
        cols = columns(head)
        acc = total = None
        if carry_in:
            shrink = jnp.exp2(max_in[:, cols] - peak)
            acc = acc_in[:, cols] * shrink
            total = sum_in[:, cols] * shrink
        for group, weight in zip(groups, weights):
            value = jnp.concatenate([load(v, cols) for _, v, _ in group], axis=0)
            both = jnp.concatenate([value, jnp.ones_like(value)], axis=1)
            added = jnp.dot(weight, both, preferred_element_type=jnp.float32)
            acc = added[:, :HD] if acc is None else acc + added[:, :HD]
            total = added[:, HD:] if total is None else total + added[:, HD:]
        if final:
            outs[0][:, cols] = (acc / total).astype(jnp.bfloat16)
        else:
            outs[0][:, cols] = acc
            outs[1][:, cols] = total
            outs[2][:, cols] = peak

    scores = scores_of(0)
    last = None
    for head in range(heads):
        following = scores_of(head + 1) if head + 1 < heads else None
        weighed = weigh(head, scores)
        if last is not None:
            add_up(*last)
        last = (head, *weighed)
        scores = following
    add_up(*last)


def attend(queries, meta, sources, first, steps, heads, carry=None, final=False, into=None, held=0):
    rows, width = queries.shape
    block = heads * HD

    def spec(count, row, column):
        return pl.BlockSpec((count, block), lambda step, meta: (row(meta), column + step))

    def zero(meta):
        return 0

    operands, specs = [queries], [spec(rows, zero, first)]
    plan, keys_seen = [], 0
    for keys, values, usable in sources:
        for array, count, row, column in list(keys) + list(values):
            operands.append(array)
            specs.append(spec(count, row, column))
        keys_seen += keys[0][1]
        plan.append((len(keys), usable))
    if carry is not None:
        operands += list(carry)
        specs += [spec(rows, zero, held)] * 3
    aliases = {}
    if final:
        out_shape = jax.ShapeDtypeStruct((rows, width), jnp.bfloat16)
        out_specs = spec(rows, zero, first)
        if into is not None:
            aliases = {len(operands) + 1: 0}
            operands.append(into)
            specs.append(pl.BlockSpec(memory_space=pl.ANY))
    else:
        out_shape = [jax.ShapeDtypeStruct((rows, steps * block), jnp.float32)] * 3
        out_specs = [spec(rows, zero, 0)] * 3
    done = steps * block
    return pl.pallas_call(
        functools.partial(attend_kernel, plan, heads, carry is not None, final),
        out_shape=out_shape,
        grid_spec=pltpu.PrefetchScalarGridSpec(
            num_scalar_prefetch=1, grid=(steps,), in_specs=specs, out_specs=out_specs
        ),
        input_output_aliases=aliases,
        compiler_params=pltpu.CompilerParams(vmem_limit_bytes=VMEM_LIMIT),
        cost_estimate=pl.CostEstimate(
            flops=4 * rows * keys_seen * done,
            bytes_accessed=4 * keys_seen * done + 2 * rows * done,
            transcendentals=rows * keys_seen * (done // HD),
        ),
    )(meta, *operands)


def pack_kernel(first, meta, k_ref, v_ref, *refs):
    out_ref, note, sems = refs[-3:]
    rows = k_ref.shape[0]
    width = out_ref.shape[1]
    copies = [
        pltpu.make_async_copy(
            ref.at[:, pl.ds(first, width)], out_ref.at[pl.ds(n * rows, rows)], sems.at[n]
        )
        for n, ref in enumerate((k_ref, v_ref))
    ]
    for copy in copies:
        copy.start()
    lane = lax.broadcasted_iota(jnp.int32, note.shape, 1)
    row = jnp.zeros(note.shape, jnp.float32)
    for entry in range(8):
        row = jnp.where(lane == entry, meta[entry].astype(jnp.float32), row)
    note[...] = row.astype(jnp.bfloat16)
    last = pltpu.make_async_copy(note, out_ref.at[pl.ds(2 * rows, NOTE_ROWS)], sems.at[2])
    last.start()
    for copy in copies:
        copy.wait()
    last.wait()


def pack(meta, keys, values, first, width, after):
    rows = keys.shape[0]
    whole = pl.BlockSpec(memory_space=pl.ANY)
    source = pl.BlockSpec(memory_space=pltpu.HBM)
    return pl.pallas_call(
        functools.partial(pack_kernel, first),
        out_shape=jax.ShapeDtypeStruct((2 * rows + NOTE_ROWS, width), jnp.bfloat16),
        in_specs=[pl.BlockSpec(memory_space=pltpu.SMEM), source, source] + [whole] * len(after),
        out_specs=whole,
        scratch_shapes=[
            pltpu.VMEM((NOTE_ROWS, width), jnp.bfloat16),
            pltpu.SemaphoreType.DMA((3,)),
        ],
        compiler_params=pltpu.CompilerParams(vmem_limit_bytes=VMEM_LIMIT),
        cost_estimate=pl.CostEstimate(flops=0, bytes_accessed=8 * rows * width, transcendentals=0),
    )(meta, keys, values, *after)


def choose_kernel(meta, far_list, one_list, own, low, high, over, *refs):
    far, two, one, note, sems = refs[-5:]
    rows = 2 * TILE
    spot, plane = meta[8] % 4, meta[8] // 4
    right = spot >= 2
    read = pltpu.make_async_copy(
        over.at[pl.ds(2 * rows, NOTE_ROWS), pl.ds(0, HD)], note, sems.at[6]
    )
    read.start()

    def copies(src, tile, dst, sem):
        start = pl.multiple_of(tile * TILE, TILE)
        return [
            pltpu.make_async_copy(
                src.at[pl.ds(n * rows + start, TILE)], dst.at[pl.ds(n * TILE, TILE)], sems.at[sem + n]
            )
            for n in (0, 1)
        ]

    def start_if(condition, *args):
        @pl.when(condition)
        def _():
            for copy in copies(*args):
                copy.start()

    far_tile = jnp.clip(far_list[0, jnp.where(plane % 2 == 0, 3, 7)], 0, 1)
    start_if((plane == 0) | (plane == 3), own, far_tile, far, 0)
    start_if(plane == 1, high, far_tile, far, 0)
    start_if(plane == 2, low, far_tile, far, 0)
    one_tile = jnp.clip(one_list[0, jnp.where(spot % 2 == 0, 4, 0)], 0, 1)
    for copy in copies(over, one_tile, one, 2):
        copy.start()
    read.wait()
    here = (lax.broadcasted_iota(jnp.int32, note.shape, 1) == jnp.where(right, 1, 5)) & (
        lax.broadcasted_iota(jnp.int32, note.shape, 0) == 0
    )
    two_tile = jnp.sum(jnp.where(here, note[...].astype(jnp.float32), 0.0))
    two_tile = jnp.clip(two_tile.astype(jnp.int32), 0, 1)
    start_if(right, low, two_tile, two, 4)
    start_if(jnp.logical_not(right), high, two_tile, two, 4)
    for copy in copies(own, far_tile, far, 0) + copies(over, one_tile, one, 2) + copies(low, two_tile, two, 4):
        copy.wait()


def choose(meta, far_list, one_list, own, low, high, over, after):
    width = low.shape[1]
    scalar = pl.BlockSpec(memory_space=pltpu.SMEM)
    whole = pl.BlockSpec(memory_space=pl.ANY)
    return pl.pallas_call(
        choose_kernel,
        out_shape=[jax.ShapeDtypeStruct((2 * TILE, width), jnp.bfloat16)] * 3,
        in_specs=[scalar] * 3 + [whole] * (4 + len(after)),
        out_specs=[whole] * 3,
        scratch_shapes=[
            pltpu.VMEM((NOTE_ROWS, HD), jnp.bfloat16),
            pltpu.SemaphoreType.DMA((7,)),
        ],
        compiler_params=pltpu.CompilerParams(vmem_limit_bytes=VMEM_LIMIT),
        cost_estimate=pl.CostEstimate(flops=0, bytes_accessed=24 * TILE * width, transcendentals=0),
    )(meta, far_list, one_list, own, low, high, over, *after)


def send(array, route):
    return lax.ppermute(array, "frame", route)


def fixed(block):
    return lambda meta: block


def body_direct(queries, key_heads, value_heads, tile_lists):
    frames = lax.axis_size("frame")
    levels = frames.bit_length() - 1
    rows, width = key_heads.shape
    me = lax.axis_index("frame")
    lists = jnp.clip(lax.all_gather(tile_lists, "frame", tiled=True), 0, rows // TILE - 1)
    meta = me.astype(jnp.int32).reshape(1)
    sources = [([(key_heads, rows, fixed(0), 0)], [(value_heads, rows, fixed(0), 0)], None)]
    for level in range(levels):
        for entry, distance in ((level, 1 << level), (levels + level, -(1 << level))):
            route = [(i, i + distance) for i in range(frames) if 0 <= i + distance < frames]
            start = lists[jnp.clip(me + distance, 0, frames - 1), entry] * TILE
            both = [lax.dynamic_slice_in_dim(a, start, TILE, 0) for a in (key_heads, value_heads)]
            both = send(jnp.concatenate(both, axis=0), route)

            def usable(meta, distance=distance):
                return (meta[0] >= distance) & (meta[0] - distance < frames)

            sources.append(([(both, TILE, fixed(0), 0)], [(both, TILE, fixed(1), 0)], usable))
    return attend(queries, meta, sources, 0, width // (2 * HD), 2, final=True)


def body_planes(queries, key_heads, value_heads, tile_lists):
    frames = 16
    rows, width = key_heads.shape
    half = width // 2
    heads = 3
    steps = half // (heads * HD)
    every = range(frames)
    meta = jnp.concatenate(
        [jnp.clip(tile_lists[0], 0, rows // TILE - 1), lax.axis_index("frame").astype(jnp.int32).reshape(1)]
    )
    up = [(i, i + 4) for i in every if i + 4 < frames]
    down = [(i, i - 4) for i in every if i - 4 >= 0]
    across = [(i, i ^ 2) for i in every]
    beside = [(i, i ^ 1) for i in every]
    far = [(i, i + (8, -4, 4, -8)[i // 4]) for i in every]
    off_chip = [(i, i + (1, 3, -3, -1)[i % 4]) for i in every]
    off_chip = [(i, j) for i, j in off_chip if 0 <= j < frames]

    def right(meta):
        return meta[8] % 4 >= 2

    def beside_tile(meta):
        return jnp.where(meta[8] % 2 == 1, meta[0], meta[4])

    def across_tile(meta):
        return jnp.where(right(meta), meta[1], meta[5])

    def two_there(meta):
        return jnp.where(right(meta), meta[8] + 2 < frames, meta[8] >= 2)

    def one_there(meta):
        return (meta[8] >= 1) & (meta[8] < frames - 1)

    def tile_of(array, tile, usable=None):
        return (
            [(array, TILE, tile, 0)],
            [(array, TILE, lambda meta: tile(meta) + 2, 0)],
            usable,
        )

    def pair_of(arrays, usable=None):
        return [(a, TILE, fixed(0), 0) for a in arrays], [(a, TILE, fixed(1), 0) for a in arrays], usable

    def whole_of(n):
        return [(key_heads, rows, fixed(0), n)], [(value_heads, rows, fixed(0), n)], None

    def back(route):
        return [(j, i) for i, j in route]

    far_list = send(tile_lists, back(far))
    one_list = send(tile_lists, back(off_chip))
    first = pack(meta, key_heads, value_heads, 0, half, [far_list, one_list])
    begun = attend(queries, meta, [whole_of(0)], 0, 2 * steps, heads)
    second = pack(meta, key_heads, value_heads, half, half, [begun[0]])
    after = []
    middles, finals = [], []
    for n, packed in enumerate((first, second)):
        low = send(packed, up)
        high = send(packed, down)
        over = send(packed, across)
        next_to = send(packed, beside)
        to_far, to_two, to_one = choose(meta, far_list, one_list, packed, low, high, over, after)
        from_far = send(to_far, far)
        two = send(to_two, across)
        one = send(to_one, off_chip)
        middle = attend(
            queries,
            meta,
            [
                tile_of(next_to, beside_tile),
                tile_of(over, across_tile),
                tile_of(low, lambda meta: meta[2], lambda meta: meta[8] >= 4),
                tile_of(high, lambda meta: meta[6], lambda meta: meta[8] + 4 < frames),
            ],
            n * steps,
            steps,
            heads,
            begun,
            held=n * steps,
        )
        after = [middle[0]]
        middles.append(middle)
        finals.append([pair_of([two], two_there), pair_of([one], one_there), pair_of([from_far])])
    out = None
    for n in (0, 1):
        out = attend(queries, meta, finals[n], n * steps, steps, heads, middles[n], True, out)
    return out


def solution(mesh):
    body = body_planes if mesh.shape["frame"] == 16 else body_direct
    in_specs = (
        P(("groups", "frame"), None),
        P(("groups", "frame"), None),
        P(("groups", "frame"), None),
        P("frame", None),
    )
    out_specs = P(("groups", "frame"), None)
    return jax.shard_map(body, mesh=mesh, in_specs=in_specs, out_specs=out_specs, check_vma=False)
```

```python
import functools
import math

import jax
import jax.numpy as jnp
from jax import lax
from jax.experimental import pallas as pl
from jax.experimental.pallas import tpu as pltpu
from jax.sharding import PartitionSpec as P

HD = 128
TILE = 128
NOTE_ROWS = 16
LOG2_SCALE = math.log2(math.e) / math.sqrt(HD)
VMEM_LIMIT = 24 * 1024 * 1024


def attend_kernel(plan, heads, carry_in, final, meta, *refs):
    refs = list(refs)
    q_ref = refs.pop(0)
    sources = []
    for parts, usable in plan:
        k_refs = [refs.pop(0) for _ in range(parts)]
        v_refs = [refs.pop(0) for _ in range(parts)]
        bias = None
        if usable is not None:
            bias = jnp.where(usable(meta), 0.0, -jnp.inf).astype(jnp.float32)
        sources.append((k_refs, v_refs, bias))
    if carry_in:
        acc_in, sum_in, max_in = refs.pop(0), refs.pop(0), refs.pop(0)
    outs = refs[-1:] if final else refs[-3:]
    rows = q_ref.shape[0]

    def load(some, cols):
        total = some[0][:, cols]
        for other in some[1:]:
            total = total + other[:, cols]
        return total

    groups = [[s] for s in sources if s[0][0].shape[0] > TILE]
    narrow = [s for s in sources if s[0][0].shape[0] == TILE]
    groups += [narrow[at : at + 2] for at in range(0, len(narrow), 2)]

    def columns(head):
        return slice(head * HD, (head + 1) * HD)

    def scores_of(head):
        cols = columns(head)
        scores = []
        for group in groups:
            key = jnp.concatenate([load(k, cols) for k, _, _ in group], axis=0)
            part = lax.dot_general(
                q_ref[:, cols], key, (((1,), (1,)), ((), ())), preferred_element_type=jnp.float32
            )
            pieces = []
            at = 0
            for k, _, bias in group:
                for _ in range(k[0].shape[0] // TILE):
                    piece = part[:, at : at + TILE] * LOG2_SCALE
                    pieces.append(piece if bias is None else piece + bias)
                    at += TILE
            scores.append(pieces)
        return scores

    def weigh(head, scores):
        peak = functools.reduce(jnp.maximum, [piece for pieces in scores for piece in pieces])
        peak = jnp.broadcast_to(jnp.max(peak, axis=1, keepdims=True), (rows, HD))
        if carry_in:
            peak = jnp.maximum(max_in[:, columns(head)], peak)
        weights = [
            jnp.concatenate([jnp.exp2(piece - peak).astype(jnp.bfloat16) for piece in pieces], axis=1)
            for pieces in scores
        ]
        return peak, weights

    def add_up(head, peak, weights):
        cols = columns(head)
        acc = total = None
        if carry_in:
            shrink = jnp.exp2(max_in[:, cols] - peak)
            acc = acc_in[:, cols] * shrink
            total = sum_in[:, cols] * shrink
        for group, weight in zip(groups, weights):
            value = jnp.concatenate([load(v, cols) for _, v, _ in group], axis=0)
            both = jnp.concatenate([value, jnp.ones_like(value)], axis=1)
            added = jnp.dot(weight, both, preferred_element_type=jnp.float32)
            acc = added[:, :HD] if acc is None else acc + added[:, :HD]
            total = added[:, HD:] if total is None else total + added[:, HD:]
        if final:
            outs[0][:, cols] = (acc / total).astype(jnp.bfloat16)
        else:
            outs[0][:, cols] = acc
            outs[1][:, cols] = total
            outs[2][:, cols] = peak

    scores = scores_of(0)
    last = None
    for head in range(heads):
        following = scores_of(head + 1) if head + 1 < heads else None
        weighed = weigh(head, scores)
        if last is not None:
            add_up(*last)
        last = (head, *weighed)
        scores = following
    add_up(*last)


def attend(queries, meta, sources, first, steps, heads, carry=None, final=False, into=None, held=0):
    rows, width = queries.shape
    block = heads * HD

    def spec(count, row, column):
        return pl.BlockSpec((count, block), lambda step, meta: (row(meta), column + step))

    def zero(meta):
        return 0

    operands, specs = [queries], [spec(rows, zero, first)]
    plan, keys_seen = [], 0
    for keys, values, usable in sources:
        for array, count, row, column in list(keys) + list(values):
            operands.append(array)
            specs.append(spec(count, row, column))
        keys_seen += keys[0][1]
        plan.append((len(keys), usable))
    if carry is not None:
        operands += list(carry)
        specs += [spec(rows, zero, held)] * 3
    aliases = {}
    if final:
        out_shape = jax.ShapeDtypeStruct((rows, width), jnp.bfloat16)
        out_specs = spec(rows, zero, first)
        if into is not None:
            aliases = {len(operands) + 1: 0}
            operands.append(into)
            specs.append(pl.BlockSpec(memory_space=pl.ANY))
    else:
        out_shape = [jax.ShapeDtypeStruct((rows, steps * block), jnp.float32)] * 3
        out_specs = [spec(rows, zero, 0)] * 3
    done = steps * block
    return pl.pallas_call(
        functools.partial(attend_kernel, plan, heads, carry is not None, final),
        name="attend_last" if final else "attend_more" if carry is not None else "attend_own",
        out_shape=out_shape,
        grid_spec=pltpu.PrefetchScalarGridSpec(
            num_scalar_prefetch=1, grid=(steps,), in_specs=specs, out_specs=out_specs
        ),
        input_output_aliases=aliases,
        compiler_params=pltpu.CompilerParams(vmem_limit_bytes=VMEM_LIMIT),
        cost_estimate=pl.CostEstimate(
            flops=4 * rows * keys_seen * done,
            bytes_accessed=4 * keys_seen * done + 2 * rows * done,
            transcendentals=rows * keys_seen * (done // HD),
        ),
    )(meta, *operands)


SCALAR = pl.BlockSpec(memory_space=pltpu.SMEM)
WHOLE = pl.BlockSpec(memory_space=pl.ANY)


def move(name, build, operands, specs, out_shape, out_specs, copies, moved, scratch=()):
    return pl.pallas_call(
        build,
        name=name,
        out_shape=out_shape,
        in_specs=specs,
        out_specs=out_specs,
        scratch_shapes=[*scratch, pltpu.SemaphoreType.DMA((copies,))],
        compiler_params=pltpu.CompilerParams(vmem_limit_bytes=VMEM_LIMIT),
        cost_estimate=pl.CostEstimate(flops=0, bytes_accessed=moved, transcendentals=0),
    )(*operands)


def in_hbm(array):
    return pltpu.with_memory_space_constraint(array, pltpu.HBM)


def tile_copies(sources, tile, target, column, sems, at):
    width = target.shape[1] if column is None else column[1]
    to = 0 if column is None else column[0]
    return [
        pltpu.make_async_copy(
            ref.at[pl.ds(pl.multiple_of(row + tile * TILE, TILE), TILE), pl.ds(first, width)],
            target.at[pl.ds(n * TILE, TILE), pl.ds(to, width)],
            sems.at[at + n],
        )
        for n, (ref, row, first) in enumerate(sources)
    ]


def start_if(condition, copies):
    @pl.when(condition)
    def _():
        for copy in copies:
            copy.start()


def begin(tile_lists, me, beside_list, across_list, far_list, keys, values, width):
    rows, all_width = keys.shape
    tile_count = rows // TILE

    def build(list_ref, me_ref, beside_ref, across_ref, far_ref, k_ref, v_ref, *refs):
        meta, packed, to_beside, to_across, note, sems = refs
        me = me_ref[0]
        plane, right = me // 4, me % 4 >= 2

        def tile_at(ref, entry):
            return jnp.clip(ref[0, entry], 0, tile_count - 1)

        copies = [
            pltpu.make_async_copy(
                ref.at[:, pl.ds(0, width)], packed.at[pl.ds(n * rows, rows)], sems.at[n]
            )
            for n, ref in enumerate((k_ref, v_ref))
        ]
        own = ((k_ref, 0, 0), (v_ref, 0, 0))
        copies += tile_copies(own, tile_at(across_ref, jnp.where(right, 5, 1)), to_across, None, sems, 2)
        copies += tile_copies(own, tile_at(beside_ref, jnp.where(me % 2 == 0, 0, 4)), to_beside, None, sems, 4)
        for copy in copies:
            copy.start()
        lane = lax.broadcasted_iota(jnp.int32, note.shape, 1)
        row = jnp.zeros(note.shape, jnp.float32)
        for entry in range(8):
            row = jnp.where(lane == entry, tile_at(beside_ref, entry).astype(jnp.float32), row)
        note[...] = row.astype(jnp.bfloat16)
        copies.append(
            pltpu.make_async_copy(note, to_across.at[pl.ds(2 * TILE, NOTE_ROWS)], sems.at[6])
        )
        copies[-1].start()
        for entry in range(8):
            meta[entry] = tile_at(list_ref, entry)
        meta[8] = me
        meta[9] = tile_at(far_ref, jnp.where(plane % 2 == 0, 3, 7))
        meta[10] = tile_at(across_ref, jnp.where(right, 1, 5))
        for entry in range(11, 16):
            meta[entry] = 0
        for copy in copies:
            copy.wait()

    return move(
        "begin",
        build,
        (tile_lists, me, beside_list, across_list, far_list, in_hbm(keys), in_hbm(values)),
        [SCALAR] * 5 + [WHOLE] * 2,
        [
            jax.ShapeDtypeStruct((16,), jnp.int32),
            jax.ShapeDtypeStruct((2 * rows, width), jnp.bfloat16),
            jax.ShapeDtypeStruct((2 * TILE, all_width), jnp.bfloat16),
            jax.ShapeDtypeStruct((2 * TILE + NOTE_ROWS, all_width), jnp.bfloat16),
        ],
        [SCALAR, WHOLE, WHOLE, WHOLE],
        7,
        24 * TILE * all_width,
        [pltpu.VMEM((NOTE_ROWS, all_width), jnp.bfloat16)],
    )


def pack(keys, values, first, width, after):
    rows = keys.shape[0]

    def build(k_ref, v_ref, *refs):
        out_ref, sems = refs[-2:]
        copies = [
            pltpu.make_async_copy(
                ref.at[:, pl.ds(first, width)], out_ref.at[pl.ds(n * rows, rows)], sems.at[n]
            )
            for n, ref in enumerate((k_ref, v_ref))
        ]
        for copy in copies:
            copy.start()
        for copy in copies:
            copy.wait()

    return move(
        "pack",
        build,
        (in_hbm(keys), in_hbm(values), *after),
        [WHOLE] * (2 + len(after)),
        jax.ShapeDtypeStruct((2 * rows, width), jnp.bfloat16),
        WHOLE,
        2,
        8 * rows * width,
    )


def choose(meta, over, keys, values, first, low, high, after):
    rows, width = low.shape[0] // 2, low.shape[1]
    tile_count = rows // TILE

    def build(meta, over_ref, k_ref, v_ref, low, high, *refs):
        to_two, to_one, to_far, note, sems = refs[-5:]
        spot, plane = meta[8] % 4, meta[8] // 4
        right = spot >= 2
        read = pltpu.make_async_copy(
            over_ref.at[pl.ds(2 * TILE, NOTE_ROWS), pl.ds(0, HD)], note, sems.at[6]
        )
        read.start()
        own = ((k_ref, 0, first), (v_ref, 0, first))
        below = ((low, 0, 0), (low, rows, 0))
        above = ((high, 0, 0), (high, rows, 0))

        def copies(source, tile, target, at):
            return tile_copies(source, tile, target, None, sems, at)

        start_if((plane == 0) | (plane == 3), copies(own, meta[9], to_far, 0))
        start_if(plane == 1, copies(above, meta[9], to_far, 0))
        start_if(plane == 2, copies(below, meta[9], to_far, 0))
        start_if(right, copies(below, meta[10], to_two, 2))
        start_if(jnp.logical_not(right), copies(above, meta[10], to_two, 2))
        read.wait()
        here = (lax.broadcasted_iota(jnp.int32, note.shape, 1) == jnp.where(spot % 2 == 0, 4, 0)) & (
            lax.broadcasted_iota(jnp.int32, note.shape, 0) == 0
        )
        tile = jnp.sum(jnp.where(here, note[...].astype(jnp.float32), 0.0))
        tile = jnp.clip(tile.astype(jnp.int32), 0, tile_count - 1)
        start_if(spot == 0, copies(above, tile, to_one, 4))
        start_if(spot == 3, copies(below, tile, to_one, 4))
        start_if((spot == 1) | (spot == 2), copies(own, tile, to_one, 4))
        for at, target in ((0, to_far), (2, to_two), (4, to_one)):
            for copy in copies(own, 0, target, at):
                copy.wait()

    return move(
        "choose",
        build,
        (meta, over, in_hbm(keys), in_hbm(values), low, high, *after),
        [SCALAR] + [WHOLE] * (5 + len(after)),
        [jax.ShapeDtypeStruct((2 * TILE, width), jnp.bfloat16)] * 3,
        [WHOLE] * 3,
        7,
        24 * TILE * width,
        [pltpu.VMEM((NOTE_ROWS, HD), jnp.bfloat16)],
    )


def send(array, route):
    return lax.ppermute(array, "frame", route)


def fixed(block):
    return lambda meta: block


def body_direct(queries, key_heads, value_heads, tile_lists):
    frames = lax.axis_size("frame")
    levels = frames.bit_length() - 1
    rows, width = key_heads.shape
    me = lax.axis_index("frame")
    lists = jnp.clip(lax.all_gather(tile_lists, "frame", tiled=True), 0, rows // TILE - 1)
    meta = me.astype(jnp.int32).reshape(1)
    sources = [([(key_heads, rows, fixed(0), 0)], [(value_heads, rows, fixed(0), 0)], None)]
    for level in range(levels):
        for entry, distance in ((level, 1 << level), (levels + level, -(1 << level))):
            route = [(i, i + distance) for i in range(frames) if 0 <= i + distance < frames]
            start = lists[jnp.clip(me + distance, 0, frames - 1), entry] * TILE
            both = [lax.dynamic_slice_in_dim(a, start, TILE, 0) for a in (key_heads, value_heads)]
            both = send(jnp.concatenate(both, axis=0), route)

            def usable(meta, distance=distance):
                return (meta[0] >= distance) & (meta[0] - distance < frames)

            sources.append(([(both, TILE, fixed(0), 0)], [(both, TILE, fixed(1), 0)], usable))
    return attend(queries, meta, sources, 0, width // (2 * HD), 2, final=True)


def body_planes(queries, key_heads, value_heads, tile_lists):
    frames = 16
    rows, width = key_heads.shape
    tile_count = rows // TILE
    half = width // 2
    heads = 3
    steps = half // (heads * HD)
    every = range(frames)
    up = [(i, i + 4) for i in every if i + 4 < frames]
    down = [(i, i - 4) for i in every if i - 4 >= 0]
    beside = [(i, i ^ 1) for i in every]
    across = [(i, i ^ 2) for i in every]
    corner = [(i, i ^ 3) for i in every]
    far = [(i, i + (8, -4, 4, -8)[i // 4]) for i in every]

    def right(meta):
        return meta[8] % 4 >= 2

    def two_there(meta):
        return jnp.where(right(meta), meta[8] + 2 < frames, meta[8] >= 2)

    def one_there(meta):
        return (meta[8] >= 1) & (meta[8] < frames - 1)

    def own_frame():
        return [(key_heads, rows, fixed(0), 0)], [(value_heads, rows, fixed(0), 0)], None

    def tile_of(array, tile, usable):
        return [(array, TILE, tile, 0)], [(array, TILE, lambda meta: tile(meta) + tile_count, 0)], usable

    def sent_tile(array, column=0, usable=None):
        return [(array, TILE, fixed(0), column)], [(array, TILE, fixed(1), column)], usable

    me = lax.axis_index("frame").astype(jnp.int32).reshape(1)
    far_list = send(tile_lists, [(j, i) for i, j in far])
    beside_list = send(tile_lists, beside)
    across_list = send(tile_lists, across)
    meta, first, to_beside, to_across = begin(
        tile_lists, me, beside_list, across_list, far_list, key_heads, value_heads, half
    )
    over = send(to_across, across)
    low = [send(first, up)]
    high = [send(first, down)]
    next_to = send(to_beside, beside)
    begun = attend(queries, meta, [own_frame()], 0, 2 * steps, heads)
    second = pack(key_heads, value_heads, half, half, [begun[0]])
    low.append(send(second, up))
    high.append(send(second, down))

    after = []
    middles, finals = [], []
    for n in (0, 1):
        sent = choose(meta, over, key_heads, value_heads, n * half, low[n], high[n], after)
        two = send(sent[0], across)
        one = send(sent[1], corner)
        from_far = send(sent[2], far)
        middle = attend(
            queries,
            meta,
            [
                sent_tile(next_to, n * steps),
                sent_tile(over, n * steps),
                tile_of(low[n], lambda meta: meta[2], lambda meta: meta[8] >= 4),
                tile_of(high[n], lambda meta: meta[6], lambda meta: meta[8] + 4 < frames),
            ],
            n * steps,
            steps,
            heads,
            begun,
            held=n * steps,
        )
        after = [middle[0], two]
        middles.append(middle)
        finals.append([sent_tile(two, 0, two_there), sent_tile(one, 0, one_there), sent_tile(from_far)])
    out = None
    for n in (0, 1):
        out = attend(queries, meta, finals[n], n * steps, steps, heads, middles[n], True, out)
    return out


def solution(mesh):
    body = body_planes if mesh.shape["frame"] == 16 else body_direct
    in_specs = (
        P(("groups", "frame"), None),
        P(("groups", "frame"), None),
        P(("groups", "frame"), None),
        P("frame", None),
    )
    out_specs = P(("groups", "frame"), None)
    return jax.shard_map(body, mesh=mesh, in_specs=in_specs, out_specs=out_specs, check_vma=False)
```

```python
import functools
import math

import jax
import jax.numpy as jnp
from jax import lax
from jax.experimental import pallas as pl
from jax.experimental.pallas import tpu as pltpu
from jax.sharding import PartitionSpec as P

HD = 128
TILE = 128
NOTE_ROWS = 16
LOG2_SCALE = math.log2(math.e) / math.sqrt(HD)
VMEM_LIMIT = 24 * 1024 * 1024


def attend_kernel(plan, heads, carry_in, final, meta, *refs):
    refs = list(refs)
    q_ref = refs.pop(0)
    sources = []
    for parts, usable in plan:
        k_refs = [refs.pop(0) for _ in range(parts)]
        v_refs = [refs.pop(0) for _ in range(parts)]
        bias = None
        if usable is not None:
            bias = jnp.where(usable(meta), 0.0, -jnp.inf).astype(jnp.float32)
        sources.append((k_refs, v_refs, bias))
    if carry_in:
        acc_in, sum_in, max_in = refs.pop(0), refs.pop(0), refs.pop(0)
    outs = refs[-1:] if final else refs[-3:]
    rows = q_ref.shape[0]

    def load(some, cols):
        total = some[0][:, cols]
        for other in some[1:]:
            total = total + other[:, cols]
        return total

    groups = [[s] for s in sources if s[0][0].shape[0] > TILE]
    narrow = [s for s in sources if s[0][0].shape[0] == TILE]
    groups += [narrow[at : at + 2] for at in range(0, len(narrow), 2)]

    def columns(head):
        return slice(head * HD, (head + 1) * HD)

    def scores_of(head):
        cols = columns(head)
        scores = []
        for group in groups:
            key = jnp.concatenate([load(k, cols) for k, _, _ in group], axis=0)
            part = lax.dot_general(
                q_ref[:, cols], key, (((1,), (1,)), ((), ())), preferred_element_type=jnp.float32
            )
            pieces = []
            at = 0
            for k, _, bias in group:
                for _ in range(k[0].shape[0] // TILE):
                    piece = part[:, at : at + TILE] * LOG2_SCALE
                    pieces.append(piece if bias is None else piece + bias)
                    at += TILE
            scores.append(pieces)
        return scores

    def weigh(head, scores):
        peak = functools.reduce(jnp.maximum, [piece for pieces in scores for piece in pieces])
        peak = jnp.broadcast_to(jnp.max(peak, axis=1, keepdims=True), (rows, HD))
        if carry_in:
            peak = jnp.maximum(max_in[:, columns(head)], peak)
        weights = [
            jnp.concatenate([jnp.exp2(piece - peak).astype(jnp.bfloat16) for piece in pieces], axis=1)
            for pieces in scores
        ]
        return peak, weights

    def add_up(head, peak, weights):
        cols = columns(head)
        acc = total = None
        if carry_in:
            shrink = jnp.exp2(max_in[:, cols] - peak)
            acc = acc_in[:, cols] * shrink
            total = sum_in[:, cols] * shrink
        for group, weight in zip(groups, weights):
            value = jnp.concatenate([load(v, cols) for _, v, _ in group], axis=0)
            both = jnp.concatenate([value, jnp.ones_like(value)], axis=1)
            added = jnp.dot(weight, both, preferred_element_type=jnp.float32)
            acc = added[:, :HD] if acc is None else acc + added[:, :HD]
            total = added[:, HD:] if total is None else total + added[:, HD:]
        if final:
            outs[0][:, cols] = (acc / total).astype(jnp.bfloat16)
        else:
            outs[0][:, cols] = acc
            outs[1][:, cols] = total
            outs[2][:, cols] = peak

    scores = scores_of(0)
    last = None
    for head in range(heads):
        following = scores_of(head + 1) if head + 1 < heads else None
        weighed = weigh(head, scores)
        if last is not None:
            add_up(*last)
        last = (head, *weighed)
        scores = following
    add_up(*last)


def attend(queries, meta, sources, first, steps, heads, carry=None, final=False, into=None, held=0):
    rows, width = queries.shape
    block = heads * HD

    def spec(count, row, column):
        return pl.BlockSpec((count, block), lambda step, meta: (row(meta), column + step))

    def zero(meta):
        return 0

    operands, specs = [queries], [spec(rows, zero, first)]
    plan, keys_seen = [], 0
    for keys, values, usable in sources:
        for array, count, row, column in list(keys) + list(values):
            operands.append(array)
            specs.append(spec(count, row, column))
        keys_seen += keys[0][1]
        plan.append((len(keys), usable))
    if carry is not None:
        operands += list(carry)
        specs += [spec(rows, zero, held)] * 3
    aliases = {}
    if final:
        out_shape = jax.ShapeDtypeStruct((rows, width), jnp.bfloat16)
        out_specs = spec(rows, zero, first)
        if into is not None:
            aliases = {len(operands) + 1: 0}
            operands.append(into)
            specs.append(pl.BlockSpec(memory_space=pl.ANY))
    else:
        out_shape = [jax.ShapeDtypeStruct((rows, steps * block), jnp.float32)] * 3
        out_specs = [spec(rows, zero, 0)] * 3
    done = steps * block
    return pl.pallas_call(
        functools.partial(attend_kernel, plan, heads, carry is not None, final),
        name="attend_last" if final else "attend_more" if carry is not None else "attend_own",
        out_shape=out_shape,
        grid_spec=pltpu.PrefetchScalarGridSpec(
            num_scalar_prefetch=1, grid=(steps,), in_specs=specs, out_specs=out_specs
        ),
        input_output_aliases=aliases,
        compiler_params=pltpu.CompilerParams(vmem_limit_bytes=VMEM_LIMIT),
        cost_estimate=pl.CostEstimate(
            flops=4 * rows * keys_seen * done,
            bytes_accessed=4 * keys_seen * done + 2 * rows * done,
            transcendentals=rows * keys_seen * (done // HD),
        ),
    )(meta, *operands)


SCALAR = pl.BlockSpec(memory_space=pltpu.SMEM)
WHOLE = pl.BlockSpec(memory_space=pl.ANY)


def move(name, build, operands, specs, out_shape, out_specs, copies, moved, scratch=()):
    return pl.pallas_call(
        build,
        name=name,
        out_shape=out_shape,
        in_specs=specs,
        out_specs=out_specs,
        scratch_shapes=[*scratch, pltpu.SemaphoreType.DMA((copies,))],
        compiler_params=pltpu.CompilerParams(vmem_limit_bytes=VMEM_LIMIT),
        cost_estimate=pl.CostEstimate(flops=0, bytes_accessed=moved, transcendentals=0),
    )(*operands)


def in_hbm(array):
    return pltpu.with_memory_space_constraint(array, pltpu.HBM)


def tile_copies(sources, tile, target, column, sems, at):
    width = target.shape[1] if column is None else column[1]
    to = 0 if column is None else column[0]
    return [
        pltpu.make_async_copy(
            ref.at[pl.ds(pl.multiple_of(row + tile * TILE, TILE), TILE), pl.ds(first, width)],
            target.at[pl.ds(n * TILE, TILE), pl.ds(to, width)],
            sems.at[at + n],
        )
        for n, (ref, row, first) in enumerate(sources)
    ]


def start_if(condition, copies):
    @pl.when(condition)
    def _():
        for copy in copies:
            copy.start()


def tile_at(ref, entry, tile_count):
    return jnp.clip(ref[0, entry], 0, tile_count - 1)


def begin(me, beside_list, across_list, keys, values):
    rows, width = keys.shape
    tile_count = rows // TILE

    def build(me_ref, beside_ref, across_ref, k_ref, v_ref, to_beside, to_across, note, sems):
        me = me_ref[0]
        own = ((k_ref, 0, 0), (v_ref, 0, 0))
        tile = tile_at(across_ref, jnp.where(me % 4 >= 2, 5, 1), tile_count)
        copies = tile_copies(own, tile, to_across, None, sems, 0)
        tile = tile_at(beside_ref, jnp.where(me % 2 == 0, 0, 4), tile_count)
        copies += tile_copies(own, tile, to_beside, None, sems, 2)
        for copy in copies:
            copy.start()
        lane = lax.broadcasted_iota(jnp.int32, note.shape, 1)
        row = jnp.zeros(note.shape, jnp.float32)
        for entry in range(8):
            row = jnp.where(lane == entry, tile_at(beside_ref, entry, tile_count).astype(jnp.float32), row)
        note[...] = row.astype(jnp.bfloat16)
        copies.append(
            pltpu.make_async_copy(note, to_across.at[pl.ds(2 * TILE, NOTE_ROWS)], sems.at[4])
        )
        copies[-1].start()
        for copy in copies:
            copy.wait()

    return move(
        "begin",
        build,
        (me, beside_list, across_list, in_hbm(keys), in_hbm(values)),
        [SCALAR] * 3 + [WHOLE] * 2,
        [
            jax.ShapeDtypeStruct((2 * TILE, width), jnp.bfloat16),
            jax.ShapeDtypeStruct((2 * TILE + NOTE_ROWS, width), jnp.bfloat16),
        ],
        [WHOLE, WHOLE],
        5,
        16 * TILE * width,
        [pltpu.VMEM((NOTE_ROWS, width), jnp.bfloat16)],
    )


def pack_copies(k_ref, v_ref, first, packed, sems):
    rows, width = k_ref.shape[0], packed.shape[1]
    return [
        pltpu.make_async_copy(
            ref.at[:, pl.ds(first, width)], packed.at[pl.ds(n * rows, rows)], sems.at[n]
        )
        for n, ref in enumerate((k_ref, v_ref))
    ]


def pack(keys, values, width):
    rows = keys.shape[0]

    def build(k_ref, v_ref, packed, sems):
        copies = pack_copies(k_ref, v_ref, 0, packed, sems)
        for copy in copies:
            copy.start()
        for copy in copies:
            copy.wait()

    return move(
        "pack",
        build,
        (in_hbm(keys), in_hbm(values)),
        [WHOLE] * 2,
        jax.ShapeDtypeStruct((2 * rows, width), jnp.bfloat16),
        WHOLE,
        2,
        8 * rows * width,
    )


def pack_rest(tile_lists, me, across_list, keys, values, first, after):
    rows = keys.shape[0]
    width = keys.shape[1] - first
    tile_count = rows // TILE

    def build(list_ref, me_ref, across_ref, k_ref, v_ref, *refs):
        packed, meta, sems = refs[-3:]
        copies = pack_copies(k_ref, v_ref, first, packed, sems)
        for copy in copies:
            copy.start()
        me = me_ref[0]
        for entry in range(8):
            meta[entry] = tile_at(list_ref, entry, tile_count)
        meta[8] = me
        meta[9] = tile_at(across_ref, jnp.where(me % 4 >= 2, 1, 5), tile_count)
        for copy in copies:
            copy.wait()

    return move(
        "pack_rest",
        build,
        (tile_lists, me, across_list, in_hbm(keys), in_hbm(values), *after),
        [SCALAR] * 3 + [WHOLE] * (2 + len(after)),
        [
            jax.ShapeDtypeStruct((2 * rows, width), jnp.bfloat16),
            jax.ShapeDtypeStruct((10,), jnp.int32),
        ],
        [WHOLE, SCALAR],
        2,
        8 * rows * width,
    )


def choose(meta, far_list, over, keys, values, first, low, high, after):
    rows, width = low.shape[0] // 2, low.shape[1]
    tile_count = rows // TILE

    def build(meta, far_ref, over_ref, k_ref, v_ref, low, high, *refs):
        to_two, to_one, to_far, note, sems = refs[-5:]
        spot, plane = meta[8] % 4, meta[8] // 4
        right = spot >= 2
        read = pltpu.make_async_copy(
            over_ref.at[pl.ds(2 * TILE, NOTE_ROWS), pl.ds(0, HD)], note, sems.at[6]
        )
        read.start()
        own = ((k_ref, 0, first), (v_ref, 0, first))
        below = ((low, 0, 0), (low, rows, 0))
        above = ((high, 0, 0), (high, rows, 0))

        def copies(source, tile, target, at):
            return tile_copies(source, tile, target, None, sems, at)

        tile = tile_at(far_ref, jnp.where(plane % 2 == 0, 3, 7), tile_count)
        start_if((plane == 0) | (plane == 3), copies(own, tile, to_far, 0))
        start_if(plane == 1, copies(above, tile, to_far, 0))
        start_if(plane == 2, copies(below, tile, to_far, 0))
        start_if(right, copies(below, meta[9], to_two, 2))
        start_if(jnp.logical_not(right), copies(above, meta[9], to_two, 2))
        read.wait()
        here = (lax.broadcasted_iota(jnp.int32, note.shape, 1) == jnp.where(spot % 2 == 0, 4, 0)) & (
            lax.broadcasted_iota(jnp.int32, note.shape, 0) == 0
        )
        tile = jnp.sum(jnp.where(here, note[...].astype(jnp.float32), 0.0))
        tile = jnp.clip(tile.astype(jnp.int32), 0, tile_count - 1)
        start_if(spot == 0, copies(above, tile, to_one, 4))
        start_if(spot == 3, copies(below, tile, to_one, 4))
        start_if((spot == 1) | (spot == 2), copies(own, tile, to_one, 4))
        for at, target in ((0, to_far), (2, to_two), (4, to_one)):
            for copy in copies(own, 0, target, at):
                copy.wait()

    return move(
        "choose",
        build,
        (meta, far_list, over, in_hbm(keys), in_hbm(values), low, high, *after),
        [SCALAR] * 2 + [WHOLE] * (5 + len(after)),
        [jax.ShapeDtypeStruct((2 * TILE, width), jnp.bfloat16)] * 3,
        [WHOLE] * 3,
        7,
        24 * TILE * width,
        [pltpu.VMEM((NOTE_ROWS, HD), jnp.bfloat16)],
    )


def send(array, route):
    return lax.ppermute(array, "frame", route)


def fixed(block):
    return lambda meta: block


def body_direct(queries, key_heads, value_heads, tile_lists):
    frames = lax.axis_size("frame")
    levels = frames.bit_length() - 1
    rows, width = key_heads.shape
    me = lax.axis_index("frame")
    lists = jnp.clip(lax.all_gather(tile_lists, "frame", tiled=True), 0, rows // TILE - 1)
    meta = me.astype(jnp.int32).reshape(1)
    sources = [([(key_heads, rows, fixed(0), 0)], [(value_heads, rows, fixed(0), 0)], None)]
    for level in range(levels):
        for entry, distance in ((level, 1 << level), (levels + level, -(1 << level))):
            route = [(i, i + distance) for i in range(frames) if 0 <= i + distance < frames]
            start = lists[jnp.clip(me + distance, 0, frames - 1), entry] * TILE
            both = [lax.dynamic_slice_in_dim(a, start, TILE, 0) for a in (key_heads, value_heads)]
            both = send(jnp.concatenate(both, axis=0), route)

            def usable(meta, distance=distance):
                return (meta[0] >= distance) & (meta[0] - distance < frames)

            sources.append(([(both, TILE, fixed(0), 0)], [(both, TILE, fixed(1), 0)], usable))
    return attend(queries, meta, sources, 0, width // (2 * HD), 2, final=True)


def body_planes(queries, key_heads, value_heads, tile_lists):
    frames = 16
    rows, width = key_heads.shape
    tile_count = rows // TILE
    half = width // 2
    heads = 3
    steps = half // (heads * HD)
    every = range(frames)
    up = [(i, i + 4) for i in every if i + 4 < frames]
    down = [(i, i - 4) for i in every if i - 4 >= 0]
    beside = [(i, i ^ 1) for i in every]
    across = [(i, i ^ 2) for i in every]
    corner = [(i, i ^ 3) for i in every]
    far = [(i, i + (8, -4, 4, -8)[i // 4]) for i in every]

    def right(meta):
        return meta[8] % 4 >= 2

    def two_there(meta):
        return jnp.where(right(meta), meta[8] + 2 < frames, meta[8] >= 2)

    def one_there(meta):
        return (meta[8] >= 1) & (meta[8] < frames - 1)

    def own_frame():
        return [(key_heads, rows, fixed(0), 0)], [(value_heads, rows, fixed(0), 0)], None

    def tile_of(array, tile, usable):
        return [(array, TILE, tile, 0)], [(array, TILE, lambda meta: tile(meta) + tile_count, 0)], usable

    def sent_tile(array, column=0, usable=None):
        return [(array, TILE, fixed(0), column)], [(array, TILE, fixed(1), column)], usable

    me = lax.axis_index("frame").astype(jnp.int32).reshape(1)
    far_list = send(tile_lists, [(j, i) for i, j in far])
    beside_list = send(tile_lists, beside)
    across_list = send(tile_lists, across)
    first = pack(key_heads, value_heads, half)
    low = [send(first, up)]
    high = [send(first, down)]
    to_beside, to_across = begin(me, beside_list, across_list, key_heads, value_heads)
    over = send(to_across, across)
    next_to = send(to_beside, beside)
    begun = attend(queries, me, [own_frame()], 0, 2 * steps, heads)
    second, meta = pack_rest(tile_lists, me, across_list, key_heads, value_heads, half, [begun[0]])
    low.append(send(second, up))
    high.append(send(second, down))

    after = []
    middles, finals = [], []
    for n in (0, 1):
        sent = choose(meta, far_list, over, key_heads, value_heads, n * half, low[n], high[n], after)
        two = send(sent[0], across)
        one = send(sent[1], corner)
        from_far = send(sent[2], far)
        middle = attend(
            queries,
            meta,
            [
                sent_tile(next_to, n * steps),
                sent_tile(over, n * steps),
                tile_of(low[n], lambda meta: meta[2], lambda meta: meta[8] >= 4),
                tile_of(high[n], lambda meta: meta[6], lambda meta: meta[8] + 4 < frames),
            ],
            n * steps,
            steps,
            heads,
            begun,
            held=n * steps,
        )
        after = [middle[0]]
        middles.append(middle)
        finals.append([sent_tile(two, 0, two_there), sent_tile(one, 0, one_there), sent_tile(from_far)])
    out = None
    for n in (0, 1):
        out = attend(queries, meta, finals[n], n * steps, steps, heads, middles[n], True, out)
    return out


def solution(mesh):
    body = body_planes if mesh.shape["frame"] == 16 else body_direct
    in_specs = (
        P(("groups", "frame"), None),
        P(("groups", "frame"), None),
        P(("groups", "frame"), None),
        P("frame", None),
    )
    out_specs = P(("groups", "frame"), None)
    return jax.shard_map(body, mesh=mesh, in_specs=in_specs, out_specs=out_specs, check_vma=False)
```

```python
import functools
import math

import jax
import jax.numpy as jnp
from jax import lax
from jax.experimental import pallas as pl
from jax.experimental.pallas import tpu as pltpu
from jax.sharding import PartitionSpec as P

HD = 128
TILE = 128
NOTE_ROWS = 16
LOG2_SCALE = math.log2(math.e) / math.sqrt(HD)
VMEM_LIMIT = 24 * 1024 * 1024


def attend_kernel(plan, heads, carry_in, final, meta, *refs):
    refs = list(refs)
    q_ref = refs.pop(0)
    sources = []
    for parts, usable in plan:
        k_refs = [refs.pop(0) for _ in range(parts)]
        v_refs = [refs.pop(0) for _ in range(parts)]
        bias = None
        if usable is not None:
            bias = jnp.where(usable(meta), 0.0, -jnp.inf).astype(jnp.float32)
        sources.append((k_refs, v_refs, bias))
    if carry_in:
        acc_in, sum_in, max_in = refs.pop(0), refs.pop(0), refs.pop(0)
    outs = refs[-1:] if final else refs[-3:]
    rows = q_ref.shape[0]

    def load(some, cols):
        total = some[0][:, cols]
        for other in some[1:]:
            total = total + other[:, cols]
        return total

    groups = [[s] for s in sources if s[0][0].shape[0] > TILE]
    narrow = [s for s in sources if s[0][0].shape[0] == TILE]
    groups += [narrow[at : at + 2] for at in range(0, len(narrow), 2)]

    def columns(head):
        return slice(head * HD, (head + 1) * HD)

    def scores_of(head):
        cols = columns(head)
        scores = []
        for group in groups:
            key = jnp.concatenate([load(k, cols) for k, _, _ in group], axis=0)
            part = lax.dot_general(
                q_ref[:, cols], key, (((1,), (1,)), ((), ())), preferred_element_type=jnp.float32
            )
            pieces = []
            at = 0
            for k, _, bias in group:
                for _ in range(k[0].shape[0] // TILE):
                    piece = part[:, at : at + TILE] * LOG2_SCALE
                    pieces.append(piece if bias is None else piece + bias)
                    at += TILE
            scores.append(pieces)
        return scores

    def weigh(head, scores):
        peak = functools.reduce(jnp.maximum, [piece for pieces in scores for piece in pieces])
        peak = jnp.broadcast_to(jnp.max(peak, axis=1, keepdims=True), (rows, HD))
        if carry_in:
            peak = jnp.maximum(max_in[:, columns(head)], peak)
        weights = [
            jnp.concatenate([jnp.exp2(piece - peak).astype(jnp.bfloat16) for piece in pieces], axis=1)
            for pieces in scores
        ]
        return peak, weights

    def add_up(head, peak, weights):
        cols = columns(head)
        acc = total = None
        if carry_in:
            shrink = jnp.exp2(max_in[:, cols] - peak)
            acc = acc_in[:, cols] * shrink
            total = sum_in[:, cols] * shrink
        for group, weight in zip(groups, weights):
            value = jnp.concatenate([load(v, cols) for _, v, _ in group], axis=0)
            both = jnp.concatenate([value, jnp.ones_like(value)], axis=1)
            added = jnp.dot(weight, both, preferred_element_type=jnp.float32)
            acc = added[:, :HD] if acc is None else acc + added[:, :HD]
            total = added[:, HD:] if total is None else total + added[:, HD:]
        if final:
            outs[0][:, cols] = (acc / total).astype(jnp.bfloat16)
        else:
            outs[0][:, cols] = acc
            outs[1][:, cols] = total
            outs[2][:, cols] = peak

    scores = scores_of(0)
    last = None
    for head in range(heads):
        following = scores_of(head + 1) if head + 1 < heads else None
        weighed = weigh(head, scores)
        if last is not None:
            add_up(*last)
        last = (head, *weighed)
        scores = following
    add_up(*last)


def attend(queries, meta, sources, first, steps, heads, carry=None, final=False, into=None, held=0):
    rows, width = queries.shape
    block = heads * HD

    def spec(count, row, column):
        return pl.BlockSpec((count, block), lambda step, meta: (row(meta), column + step))

    def zero(meta):
        return 0

    operands, specs = [queries], [spec(rows, zero, first)]
    plan, keys_seen = [], 0
    for keys, values, usable in sources:
        for array, count, row, column in list(keys) + list(values):
            operands.append(array)
            specs.append(spec(count, row, column))
        keys_seen += keys[0][1]
        plan.append((len(keys), usable))
    if carry is not None:
        operands += list(carry)
        specs += [spec(rows, zero, held)] * 3
    aliases = {}
    if final:
        out_shape = jax.ShapeDtypeStruct((rows, width), jnp.bfloat16)
        out_specs = spec(rows, zero, first)
        if into is not None:
            aliases = {len(operands) + 1: 0}
            operands.append(into)
            specs.append(pl.BlockSpec(memory_space=pl.ANY))
    else:
        out_shape = [jax.ShapeDtypeStruct((rows, steps * block), jnp.float32)] * 3
        out_specs = [spec(rows, zero, 0)] * 3
    done = steps * block
    return pl.pallas_call(
        functools.partial(attend_kernel, plan, heads, carry is not None, final),
        name="attend_last" if final else "attend_more" if carry is not None else "attend_own",
        out_shape=out_shape,
        grid_spec=pltpu.PrefetchScalarGridSpec(
            num_scalar_prefetch=1, grid=(steps,), in_specs=specs, out_specs=out_specs
        ),
        input_output_aliases=aliases,
        compiler_params=pltpu.CompilerParams(vmem_limit_bytes=VMEM_LIMIT),
        cost_estimate=pl.CostEstimate(
            flops=4 * rows * keys_seen * done,
            bytes_accessed=4 * keys_seen * done + 2 * rows * done,
            transcendentals=rows * keys_seen * (done // HD),
        ),
    )(meta, *operands)


SCALAR = pl.BlockSpec(memory_space=pltpu.SMEM)
WHOLE = pl.BlockSpec(memory_space=pl.ANY)


def move(name, build, operands, specs, out_shape, out_specs, copies, moved, scratch=()):
    return pl.pallas_call(
        build,
        name=name,
        out_shape=out_shape,
        in_specs=specs,
        out_specs=out_specs,
        scratch_shapes=[*scratch, pltpu.SemaphoreType.DMA((copies,))],
        compiler_params=pltpu.CompilerParams(vmem_limit_bytes=VMEM_LIMIT),
        cost_estimate=pl.CostEstimate(flops=0, bytes_accessed=moved, transcendentals=0),
    )(*operands)


def in_hbm(array):
    return pltpu.with_memory_space_constraint(array, pltpu.HBM)


def tile_copies(sources, tile, target, column, sems, at):
    width = target.shape[1] if column is None else column[1]
    to = 0 if column is None else column[0]
    return [
        pltpu.make_async_copy(
            ref.at[pl.ds(pl.multiple_of(row + tile * TILE, TILE), TILE), pl.ds(first, width)],
            target.at[pl.ds(n * TILE, TILE), pl.ds(to, width)],
            sems.at[at + n],
        )
        for n, (ref, row, first) in enumerate(sources)
    ]


def start_if(condition, copies):
    @pl.when(condition)
    def _():
        for copy in copies:
            copy.start()


def tile_at(ref, entry, tile_count):
    return jnp.clip(ref[0, entry], 0, tile_count - 1)


def begin(me, beside_list, across_list, keys, values):
    rows, width = keys.shape
    tile_count = rows // TILE

    def build(me_ref, beside_ref, across_ref, k_ref, v_ref, to_beside, to_across, note, sems):
        me = me_ref[0]
        own = ((k_ref, 0, 0), (v_ref, 0, 0))
        tile = tile_at(across_ref, jnp.where(me % 4 >= 2, 5, 1), tile_count)
        copies = tile_copies(own, tile, to_across, None, sems, 0)
        tile = tile_at(beside_ref, jnp.where(me % 2 == 0, 0, 4), tile_count)
        copies += tile_copies(own, tile, to_beside, None, sems, 2)
        for copy in copies:
            copy.start()
        lane = lax.broadcasted_iota(jnp.int32, note.shape, 1)
        row = jnp.zeros(note.shape, jnp.float32)
        for entry in range(8):
            row = jnp.where(lane == entry, tile_at(beside_ref, entry, tile_count).astype(jnp.float32), row)
        note[...] = row.astype(jnp.bfloat16)
        copies.append(
            pltpu.make_async_copy(note, to_across.at[pl.ds(2 * TILE, NOTE_ROWS)], sems.at[4])
        )
        copies[-1].start()
        for copy in copies:
            copy.wait()

    return move(
        "begin",
        build,
        (me, beside_list, across_list, in_hbm(keys), in_hbm(values)),
        [SCALAR] * 3 + [WHOLE] * 2,
        [
            jax.ShapeDtypeStruct((2 * TILE, width), jnp.bfloat16),
            jax.ShapeDtypeStruct((2 * TILE + NOTE_ROWS, width), jnp.bfloat16),
        ],
        [WHOLE, WHOLE],
        5,
        16 * TILE * width,
        [pltpu.VMEM((NOTE_ROWS, width), jnp.bfloat16)],
    )


def pack_copies(k_ref, v_ref, first, packed, sems):
    rows, width = k_ref.shape[0], packed.shape[1]
    return [
        pltpu.make_async_copy(
            ref.at[:, pl.ds(first, width)], packed.at[pl.ds(n * rows, rows)], sems.at[n]
        )
        for n, ref in enumerate((k_ref, v_ref))
    ]


def pack(keys, values, width, after):
    rows = keys.shape[0]

    def build(k_ref, v_ref, *refs):
        copies = pack_copies(k_ref, v_ref, 0, *refs[-2:])
        for copy in copies:
            copy.start()
        for copy in copies:
            copy.wait()

    return move(
        "pack",
        build,
        (in_hbm(keys), in_hbm(values), *after),
        [WHOLE] * (2 + len(after)),
        jax.ShapeDtypeStruct((2 * rows, width), jnp.bfloat16),
        WHOLE,
        2,
        8 * rows * width,
    )


def pack_rest(tile_lists, me, across_list, keys, values, first, after):
    rows = keys.shape[0]
    width = keys.shape[1] - first
    tile_count = rows // TILE

    def build(list_ref, me_ref, across_ref, k_ref, v_ref, *refs):
        packed, meta, sems = refs[-3:]
        copies = pack_copies(k_ref, v_ref, first, packed, sems)
        for copy in copies:
            copy.start()
        me = me_ref[0]
        for entry in range(8):
            meta[entry] = tile_at(list_ref, entry, tile_count)
        meta[8] = me
        meta[9] = tile_at(across_ref, jnp.where(me % 4 >= 2, 1, 5), tile_count)
        for copy in copies:
            copy.wait()

    return move(
        "pack_rest",
        build,
        (tile_lists, me, across_list, in_hbm(keys), in_hbm(values), *after),
        [SCALAR] * 3 + [WHOLE] * (2 + len(after)),
        [
            jax.ShapeDtypeStruct((2 * rows, width), jnp.bfloat16),
            jax.ShapeDtypeStruct((10,), jnp.int32),
        ],
        [WHOLE, SCALAR],
        2,
        8 * rows * width,
    )


def choose(meta, far_list, over, keys, values, first, low, high, after):
    rows, width = low.shape[0] // 2, low.shape[1]
    tile_count = rows // TILE

    def build(meta, far_ref, over_ref, k_ref, v_ref, low, high, *refs):
        to_two, to_one, to_far, note, sems = refs[-5:]
        spot, plane = meta[8] % 4, meta[8] // 4
        right = spot >= 2
        read = pltpu.make_async_copy(
            over_ref.at[pl.ds(2 * TILE, NOTE_ROWS), pl.ds(0, HD)], note, sems.at[6]
        )
        read.start()
        own = ((k_ref, 0, first), (v_ref, 0, first))
        below = ((low, 0, 0), (low, rows, 0))
        above = ((high, 0, 0), (high, rows, 0))

        def copies(source, tile, target, at):
            return tile_copies(source, tile, target, None, sems, at)

        tile = tile_at(far_ref, jnp.where(plane % 2 == 0, 3, 7), tile_count)
        start_if((plane == 0) | (plane == 3), copies(own, tile, to_far, 0))
        start_if(plane == 1, copies(above, tile, to_far, 0))
        start_if(plane == 2, copies(below, tile, to_far, 0))
        start_if(right, copies(below, meta[9], to_two, 2))
        start_if(jnp.logical_not(right), copies(above, meta[9], to_two, 2))
        read.wait()
        here = (lax.broadcasted_iota(jnp.int32, note.shape, 1) == jnp.where(spot % 2 == 0, 4, 0)) & (
            lax.broadcasted_iota(jnp.int32, note.shape, 0) == 0
        )
        tile = jnp.sum(jnp.where(here, note[...].astype(jnp.float32), 0.0))
        tile = jnp.clip(tile.astype(jnp.int32), 0, tile_count - 1)
        start_if(spot == 0, copies(above, tile, to_one, 4))
        start_if(spot == 3, copies(below, tile, to_one, 4))
        start_if((spot == 1) | (spot == 2), copies(own, tile, to_one, 4))
        for at, target in ((0, to_far), (2, to_two), (4, to_one)):
            for copy in copies(own, 0, target, at):
                copy.wait()

    return move(
        "choose",
        build,
        (meta, far_list, over, in_hbm(keys), in_hbm(values), low, high, *after),
        [SCALAR] * 2 + [WHOLE] * (5 + len(after)),
        [jax.ShapeDtypeStruct((2 * TILE, width), jnp.bfloat16)] * 3,
        [WHOLE] * 3,
        7,
        24 * TILE * width,
        [pltpu.VMEM((NOTE_ROWS, HD), jnp.bfloat16)],
    )


def send(array, route):
    return lax.ppermute(array, "frame", route)


def fixed(block):
    return lambda meta: block


def body_direct(queries, key_heads, value_heads, tile_lists):
    frames = lax.axis_size("frame")
    levels = frames.bit_length() - 1
    rows, width = key_heads.shape
    me = lax.axis_index("frame")
    lists = jnp.clip(lax.all_gather(tile_lists, "frame", tiled=True), 0, rows // TILE - 1)
    meta = me.astype(jnp.int32).reshape(1)
    sources = [([(key_heads, rows, fixed(0), 0)], [(value_heads, rows, fixed(0), 0)], None)]
    for level in range(levels):
        for entry, distance in ((level, 1 << level), (levels + level, -(1 << level))):
            route = [(i, i + distance) for i in range(frames) if 0 <= i + distance < frames]
            start = lists[jnp.clip(me + distance, 0, frames - 1), entry] * TILE
            both = [lax.dynamic_slice_in_dim(a, start, TILE, 0) for a in (key_heads, value_heads)]
            both = send(jnp.concatenate(both, axis=0), route)

            def usable(meta, distance=distance):
                return (meta[0] >= distance) & (meta[0] - distance < frames)

            sources.append(([(both, TILE, fixed(0), 0)], [(both, TILE, fixed(1), 0)], usable))
    return attend(queries, meta, sources, 0, width // (2 * HD), 2, final=True)


def body_planes(queries, key_heads, value_heads, tile_lists):
    frames = 16
    rows, width = key_heads.shape
    tile_count = rows // TILE
    half = width // 2
    heads = 3
    steps = half // (heads * HD)
    every = range(frames)
    up = [(i, i + 4) for i in every if i + 4 < frames]
    down = [(i, i - 4) for i in every if i - 4 >= 0]
    beside = [(i, i ^ 1) for i in every]
    across = [(i, i ^ 2) for i in every]
    corner = [(i, i ^ 3) for i in every]
    far = [(i, i + (8, -4, 4, -8)[i // 4]) for i in every]

    def right(meta):
        return meta[8] % 4 >= 2

    def two_there(meta):
        return jnp.where(right(meta), meta[8] + 2 < frames, meta[8] >= 2)

    def one_there(meta):
        return (meta[8] >= 1) & (meta[8] < frames - 1)

    def own_frame():
        return [(key_heads, rows, fixed(0), 0)], [(value_heads, rows, fixed(0), 0)], None

    def tile_of(array, tile, usable):
        return [(array, TILE, tile, 0)], [(array, TILE, lambda meta: tile(meta) + tile_count, 0)], usable

    def sent_tile(array, column=0, usable=None):
        return [(array, TILE, fixed(0), column)], [(array, TILE, fixed(1), column)], usable

    me = lax.axis_index("frame").astype(jnp.int32).reshape(1)
    far_list = send(tile_lists, [(j, i) for i, j in far])
    beside_list = send(tile_lists, beside)
    across_list = send(tile_lists, across)
    first = pack(key_heads, value_heads, half, [across_list, far_list])
    low = [send(first, up)]
    high = [send(first, down)]
    to_beside, to_across = begin(me, beside_list, across_list, key_heads, value_heads)
    over = send(to_across, across)
    next_to = send(to_beside, beside)
    begun = attend(queries, me, [own_frame()], 0, 2 * steps, heads)
    second, meta = pack_rest(tile_lists, me, across_list, key_heads, value_heads, half, [begun[0]])
    low.append(send(second, up))
    high.append(send(second, down))

    after = []
    middles, finals = [], []
    for n in (0, 1):
        sent = choose(meta, far_list, over, key_heads, value_heads, n * half, low[n], high[n], after)
        two = send(sent[0], across)
        one = send(sent[1], corner)
        from_far = send(sent[2], far)
        middle = attend(
            queries,
            meta,
            [
                sent_tile(next_to, n * steps),
                sent_tile(over, n * steps),
                tile_of(low[n], lambda meta: meta[2], lambda meta: meta[8] >= 4),
                tile_of(high[n], lambda meta: meta[6], lambda meta: meta[8] + 4 < frames),
            ],
            n * steps,
            steps,
            heads,
            begun,
            held=n * steps,
        )
        after = [middle[0]]
        middles.append(middle)
        finals.append([sent_tile(two, 0, two_there), sent_tile(one, 0, one_there), sent_tile(from_far)])
    out = None
    for n in (0, 1):
        out = attend(queries, meta, finals[n], n * steps, steps, heads, middles[n], True, out)
    return out


def solution(mesh):
    body = body_planes if mesh.shape["frame"] == 16 else body_direct
    in_specs = (
        P(("groups", "frame"), None),
        P(("groups", "frame"), None),
        P(("groups", "frame"), None),
        P("frame", None),
    )
    out_specs = P(("groups", "frame"), None)
    return jax.shard_map(body, mesh=mesh, in_specs=in_specs, out_specs=out_specs, check_vma=False)
```

```python
import functools
import math

import jax
import jax.numpy as jnp
from jax import lax
from jax.experimental import pallas as pl
from jax.experimental.pallas import tpu as pltpu
from jax.sharding import PartitionSpec as P

HD = 128
TILE = 128
NOTE_ROWS = 16
LOG2_SCALE = math.log2(math.e) / math.sqrt(HD)
VMEM_LIMIT = 24 * 1024 * 1024


def attend_kernel(plan, heads, carry_in, final, meta, *refs):
    refs = list(refs)
    q_ref = refs.pop(0)
    sources = []
    for parts, usable in plan:
        k_refs = [refs.pop(0) for _ in range(parts)]
        v_refs = [refs.pop(0) for _ in range(parts)]
        bias = None
        if usable is not None:
            bias = jnp.where(usable(meta), 0.0, -jnp.inf).astype(jnp.float32)
        sources.append((k_refs, v_refs, bias))
    if carry_in:
        acc_in, sum_in, max_in = refs.pop(0), refs.pop(0), refs.pop(0)
    outs = refs[-1:] if final else refs[-3:]
    rows = q_ref.shape[0]

    def load(some, cols):
        total = some[0][:, cols]
        for other in some[1:]:
            total = total + other[:, cols]
        return total

    groups = [[s] for s in sources if s[0][0].shape[0] > TILE]
    narrow = [s for s in sources if s[0][0].shape[0] == TILE]
    groups += [narrow[at : at + 2] for at in range(0, len(narrow), 2)]

    def columns(head):
        return slice(head * HD, (head + 1) * HD)

    def scores_of(head):
        cols = columns(head)
        scores = []
        for group in groups:
            key = jnp.concatenate([load(k, cols) for k, _, _ in group], axis=0)
            part = lax.dot_general(
                q_ref[:, cols], key, (((1,), (1,)), ((), ())), preferred_element_type=jnp.float32
            )
            pieces = []
            at = 0
            for k, _, bias in group:
                for _ in range(k[0].shape[0] // TILE):
                    piece = part[:, at : at + TILE] * LOG2_SCALE
                    pieces.append(piece if bias is None else piece + bias)
                    at += TILE
            scores.append(pieces)
        return scores

    def weigh(head, scores):
        peak = functools.reduce(jnp.maximum, [piece for pieces in scores for piece in pieces])
        peak = jnp.broadcast_to(jnp.max(peak, axis=1, keepdims=True), (rows, HD))
        if carry_in:
            peak = jnp.maximum(max_in[:, columns(head)], peak)
        weights = [
            jnp.concatenate([jnp.exp2(piece - peak).astype(jnp.bfloat16) for piece in pieces], axis=1)
            for pieces in scores
        ]
        return peak, weights

    def add_up(head, peak, weights):
        cols = columns(head)
        acc = total = None
        if carry_in:
            shrink = jnp.exp2(max_in[:, cols] - peak)
            acc = acc_in[:, cols] * shrink
            total = sum_in[:, cols] * shrink
        for group, weight in zip(groups, weights):
            value = jnp.concatenate([load(v, cols) for _, v, _ in group], axis=0)
            both = jnp.concatenate([value, jnp.ones_like(value)], axis=1)
            added = jnp.dot(weight, both, preferred_element_type=jnp.float32)
            acc = added[:, :HD] if acc is None else acc + added[:, :HD]
            total = added[:, HD:] if total is None else total + added[:, HD:]
        if final:
            outs[0][:, cols] = (acc / total).astype(jnp.bfloat16)
        else:
            outs[0][:, cols] = acc
            outs[1][:, cols] = total
            outs[2][:, cols] = peak

    scores = scores_of(0)
    last = None
    for head in range(heads):
        following = scores_of(head + 1) if head + 1 < heads else None
        weighed = weigh(head, scores)
        if last is not None:
            add_up(*last)
        last = (head, *weighed)
        scores = following
    add_up(*last)


def attend(queries, meta, sources, first, steps, heads, carry=None, final=False, into=None, held=0):
    rows, width = queries.shape
    block = heads * HD

    def spec(count, row, column):
        return pl.BlockSpec((count, block), lambda step, meta: (row(meta), column + step))

    def zero(meta):
        return 0

    operands, specs = [queries], [spec(rows, zero, first)]
    plan, keys_seen = [], 0
    for keys, values, usable in sources:
        for array, count, row, column in list(keys) + list(values):
            operands.append(array)
            specs.append(spec(count, row, column))
        keys_seen += keys[0][1]
        plan.append((len(keys), usable))
    if carry is not None:
        operands += list(carry)
        specs += [spec(rows, zero, held)] * 3
    aliases = {}
    if final:
        out_shape = jax.ShapeDtypeStruct((rows, width), jnp.bfloat16)
        out_specs = spec(rows, zero, first)
        if into is not None:
            aliases = {len(operands) + 1: 0}
            operands.append(into)
            specs.append(pl.BlockSpec(memory_space=pl.ANY))
    else:
        out_shape = [jax.ShapeDtypeStruct((rows, steps * block), jnp.float32)] * 3
        out_specs = [spec(rows, zero, 0)] * 3
    done = steps * block
    return pl.pallas_call(
        functools.partial(attend_kernel, plan, heads, carry is not None, final),
        name="attend_last" if final else "attend_more" if carry is not None else "attend_own",
        out_shape=out_shape,
        grid_spec=pltpu.PrefetchScalarGridSpec(
            num_scalar_prefetch=1, grid=(steps,), in_specs=specs, out_specs=out_specs
        ),
        input_output_aliases=aliases,
        compiler_params=pltpu.CompilerParams(vmem_limit_bytes=VMEM_LIMIT),
        cost_estimate=pl.CostEstimate(
            flops=4 * rows * keys_seen * done,
            bytes_accessed=4 * keys_seen * done + 2 * rows * done,
            transcendentals=rows * keys_seen * (done // HD),
        ),
    )(meta, *operands)


SCALAR = pl.BlockSpec(memory_space=pltpu.SMEM)
WHOLE = pl.BlockSpec(memory_space=pl.ANY)


def move(name, build, operands, specs, out_shape, out_specs, copies, moved, scratch=()):
    return pl.pallas_call(
        build,
        name=name,
        out_shape=out_shape,
        in_specs=specs,
        out_specs=out_specs,
        scratch_shapes=[*scratch, pltpu.SemaphoreType.DMA((copies,))],
        compiler_params=pltpu.CompilerParams(vmem_limit_bytes=VMEM_LIMIT),
        cost_estimate=pl.CostEstimate(flops=0, bytes_accessed=moved, transcendentals=0),
    )(*operands)


def in_hbm(array):
    return pltpu.with_memory_space_constraint(array, pltpu.HBM)


def tile_copies(sources, tile, target, column, sems, at):
    width = target.shape[1] if column is None else column[1]
    to = 0 if column is None else column[0]
    return [
        pltpu.make_async_copy(
            ref.at[pl.ds(pl.multiple_of(row + tile * TILE, TILE), TILE), pl.ds(first, width)],
            target.at[pl.ds(n * TILE, TILE), pl.ds(to, width)],
            sems.at[at + n],
        )
        for n, (ref, row, first) in enumerate(sources)
    ]


def start_if(condition, copies):
    @pl.when(condition)
    def _():
        for copy in copies:
            copy.start()


def tile_at(ref, entry, tile_count):
    return jnp.clip(ref[0, entry], 0, tile_count - 1)


def begin(me, beside_list, across_list, keys, values):
    rows, width = keys.shape
    tile_count = rows // TILE

    def build(me_ref, beside_ref, across_ref, k_ref, v_ref, to_beside, to_across, note, sems):
        me = me_ref[0]
        own = ((k_ref, 0, 0), (v_ref, 0, 0))
        tile = tile_at(across_ref, jnp.where(me % 4 >= 2, 5, 1), tile_count)
        copies = tile_copies(own, tile, to_across, None, sems, 0)
        tile = tile_at(beside_ref, jnp.where(me % 2 == 0, 0, 4), tile_count)
        copies += tile_copies(own, tile, to_beside, None, sems, 2)
        for copy in copies:
            copy.start()
        lane = lax.broadcasted_iota(jnp.int32, note.shape, 1)
        row = jnp.zeros(note.shape, jnp.float32)
        for entry in range(8):
            row = jnp.where(lane == entry, tile_at(beside_ref, entry, tile_count).astype(jnp.float32), row)
        note[...] = row.astype(jnp.bfloat16)
        copies.append(
            pltpu.make_async_copy(note, to_across.at[pl.ds(2 * TILE, NOTE_ROWS)], sems.at[4])
        )
        copies[-1].start()
        for copy in copies:
            copy.wait()

    return move(
        "begin",
        build,
        (me, beside_list, across_list, in_hbm(keys), in_hbm(values)),
        [SCALAR] * 3 + [WHOLE] * 2,
        [
            pltpu.VMEM((2 * TILE, width), jnp.bfloat16),
            pltpu.VMEM((2 * TILE + NOTE_ROWS, width), jnp.bfloat16),
        ],
        [WHOLE, WHOLE],
        5,
        16 * TILE * width,
        [pltpu.VMEM((NOTE_ROWS, width), jnp.bfloat16)],
    )


def pack_copies(k_ref, v_ref, first, packed, sems):
    rows, width = k_ref.shape[0], packed.shape[1]
    return [
        pltpu.make_async_copy(
            ref.at[:, pl.ds(first, width)], packed.at[pl.ds(n * rows, rows)], sems.at[n]
        )
        for n, ref in enumerate((k_ref, v_ref))
    ]


def pack(keys, values, width, after):
    rows = keys.shape[0]

    def build(k_ref, v_ref, *refs):
        copies = pack_copies(k_ref, v_ref, 0, *refs[-2:])
        for copy in copies:
            copy.start()
        for copy in copies:
            copy.wait()

    return move(
        "pack",
        build,
        (in_hbm(keys), in_hbm(values), *after),
        [WHOLE] * (2 + len(after)),
        pltpu.VMEM((2 * rows, width), jnp.bfloat16),
        WHOLE,
        2,
        8 * rows * width,
    )


def pack_rest(tile_lists, me, across_list, keys, values, first, after):
    rows = keys.shape[0]
    width = keys.shape[1] - first
    tile_count = rows // TILE

    def build(list_ref, me_ref, across_ref, k_ref, v_ref, *refs):
        packed, meta, sems = refs[-3:]
        copies = pack_copies(k_ref, v_ref, first, packed, sems)
        for copy in copies:
            copy.start()
        me = me_ref[0]
        for entry in range(8):
            meta[entry] = tile_at(list_ref, entry, tile_count)
        meta[8] = me
        meta[9] = tile_at(across_ref, jnp.where(me % 4 >= 2, 1, 5), tile_count)
        for copy in copies:
            copy.wait()

    return move(
        "pack_rest",
        build,
        (tile_lists, me, across_list, in_hbm(keys), in_hbm(values), *after),
        [SCALAR] * 3 + [WHOLE] * (2 + len(after)),
        [
            pltpu.VMEM((2 * rows, width), jnp.bfloat16),
            jax.ShapeDtypeStruct((10,), jnp.int32),
        ],
        [WHOLE, SCALAR],
        2,
        8 * rows * width,
    )


def choose(meta, far_list, over, keys, values, first, low, high, after):
    rows, width = low.shape[0] // 2, low.shape[1]
    tile_count = rows // TILE

    def build(meta, far_ref, over_ref, k_ref, v_ref, low, high, *refs):
        to_two, to_one, to_far, note, sems = refs[-5:]
        spot, plane = meta[8] % 4, meta[8] // 4
        right = spot >= 2
        read = pltpu.make_async_copy(
            over_ref.at[pl.ds(2 * TILE, NOTE_ROWS), pl.ds(0, HD)], note, sems.at[6]
        )
        read.start()
        own = ((k_ref, 0, first), (v_ref, 0, first))
        below = ((low, 0, 0), (low, rows, 0))
        above = ((high, 0, 0), (high, rows, 0))

        def copies(source, tile, target, at):
            return tile_copies(source, tile, target, None, sems, at)

        tile = tile_at(far_ref, jnp.where(plane % 2 == 0, 3, 7), tile_count)
        start_if((plane == 0) | (plane == 3), copies(own, tile, to_far, 0))
        start_if(plane == 1, copies(above, tile, to_far, 0))
        start_if(plane == 2, copies(below, tile, to_far, 0))
        start_if(right, copies(below, meta[9], to_two, 2))
        start_if(jnp.logical_not(right), copies(above, meta[9], to_two, 2))
        read.wait()
        here = (lax.broadcasted_iota(jnp.int32, note.shape, 1) == jnp.where(spot % 2 == 0, 4, 0)) & (
            lax.broadcasted_iota(jnp.int32, note.shape, 0) == 0
        )
        tile = jnp.sum(jnp.where(here, note[...].astype(jnp.float32), 0.0))
        tile = jnp.clip(tile.astype(jnp.int32), 0, tile_count - 1)
        start_if(spot == 0, copies(above, tile, to_one, 4))
        start_if(spot == 3, copies(below, tile, to_one, 4))
        start_if((spot == 1) | (spot == 2), copies(own, tile, to_one, 4))
        for at, target in ((0, to_far), (2, to_two), (4, to_one)):
            for copy in copies(own, 0, target, at):
                copy.wait()

    return move(
        "choose",
        build,
        (meta, far_list, over, in_hbm(keys), in_hbm(values), low, high, *after),
        [SCALAR] * 2 + [WHOLE] * (5 + len(after)),
        [pltpu.VMEM((2 * TILE, width), jnp.bfloat16)] * 3,
        [WHOLE] * 3,
        7,
        24 * TILE * width,
        [pltpu.VMEM((NOTE_ROWS, HD), jnp.bfloat16)],
    )


def send(array, route):
    return lax.ppermute(array, "frame", route)


def fixed(block):
    return lambda meta: block


def body_direct(queries, key_heads, value_heads, tile_lists):
    frames = lax.axis_size("frame")
    levels = frames.bit_length() - 1
    rows, width = key_heads.shape
    me = lax.axis_index("frame")
    lists = jnp.clip(lax.all_gather(tile_lists, "frame", tiled=True), 0, rows // TILE - 1)
    meta = me.astype(jnp.int32).reshape(1)
    sources = [([(key_heads, rows, fixed(0), 0)], [(value_heads, rows, fixed(0), 0)], None)]
    for level in range(levels):
        for entry, distance in ((level, 1 << level), (levels + level, -(1 << level))):
            route = [(i, i + distance) for i in range(frames) if 0 <= i + distance < frames]
            start = lists[jnp.clip(me + distance, 0, frames - 1), entry] * TILE
            both = [lax.dynamic_slice_in_dim(a, start, TILE, 0) for a in (key_heads, value_heads)]
            both = send(jnp.concatenate(both, axis=0), route)

            def usable(meta, distance=distance):
                return (meta[0] >= distance) & (meta[0] - distance < frames)

            sources.append(([(both, TILE, fixed(0), 0)], [(both, TILE, fixed(1), 0)], usable))
    return attend(queries, meta, sources, 0, width // (2 * HD), 2, final=True)


def body_planes(queries, key_heads, value_heads, tile_lists):
    frames = 16
    rows, width = key_heads.shape
    tile_count = rows // TILE
    half = width // 2
    heads = 3
    steps = half // (heads * HD)
    every = range(frames)
    up = [(i, i + 4) for i in every if i + 4 < frames]
    down = [(i, i - 4) for i in every if i - 4 >= 0]
    beside = [(i, i ^ 1) for i in every]
    across = [(i, i ^ 2) for i in every]
    corner = [(i, i ^ 3) for i in every]
    far = [(i, i + (8, -4, 4, -8)[i // 4]) for i in every]

    def right(meta):
        return meta[8] % 4 >= 2

    def two_there(meta):
        return jnp.where(right(meta), meta[8] + 2 < frames, meta[8] >= 2)

    def one_there(meta):
        return (meta[8] >= 1) & (meta[8] < frames - 1)

    def own_frame():
        return [(key_heads, rows, fixed(0), 0)], [(value_heads, rows, fixed(0), 0)], None

    def tile_of(array, tile, usable):
        return [(array, TILE, tile, 0)], [(array, TILE, lambda meta: tile(meta) + tile_count, 0)], usable

    def sent_tile(array, column=0, usable=None):
        return [(array, TILE, fixed(0), column)], [(array, TILE, fixed(1), column)], usable

    me = lax.axis_index("frame").astype(jnp.int32).reshape(1)
    far_list = send(tile_lists, [(j, i) for i, j in far])
    beside_list = send(tile_lists, beside)
    across_list = send(tile_lists, across)
    first = pack(key_heads, value_heads, half, [across_list, far_list])
    low = [send(first, up)]
    high = [send(first, down)]
    to_beside, to_across = begin(me, beside_list, across_list, key_heads, value_heads)
    over = send(to_across, across)
    next_to = send(to_beside, beside)
    begun = attend(queries, me, [own_frame()], 0, 2 * steps, heads)
    second, meta = pack_rest(tile_lists, me, across_list, key_heads, value_heads, half, [begun[0]])
    low.append(send(second, up))
    high.append(send(second, down))

    after = []
    middles, finals = [], []
    for n in (0, 1):
        sent = choose(meta, far_list, over, key_heads, value_heads, n * half, low[n], high[n], after)
        two = send(sent[0], across)
        one = send(sent[1], corner)
        from_far = send(sent[2], far)
        middle = attend(
            queries,
            meta,
            [
                sent_tile(next_to, n * steps),
                sent_tile(over, n * steps),
                tile_of(low[n], lambda meta: meta[2], lambda meta: meta[8] >= 4),
                tile_of(high[n], lambda meta: meta[6], lambda meta: meta[8] + 4 < frames),
            ],
            n * steps,
            steps,
            heads,
            begun,
            held=n * steps,
        )
        after = [middle[0]]
        middles.append(middle)
        finals.append([sent_tile(two, 0, two_there), sent_tile(one, 0, one_there), sent_tile(from_far)])
    out = None
    for n in (0, 1):
        out = attend(queries, meta, finals[n], n * steps, steps, heads, middles[n], True, out)
    return out


def solution(mesh):
    body = body_planes if mesh.shape["frame"] == 16 else body_direct
    in_specs = (
        P(("groups", "frame"), None),
        P(("groups", "frame"), None),
        P(("groups", "frame"), None),
        P("frame", None),
    )
    out_specs = P(("groups", "frame"), None)
    return jax.shard_map(body, mesh=mesh, in_specs=in_specs, out_specs=out_specs, check_vma=False)
```

```python
import functools
import math

import jax
import jax.numpy as jnp
from jax import lax
from jax.experimental import pallas as pl
from jax.experimental.pallas import tpu as pltpu
from jax.sharding import PartitionSpec as P

HD = 128
TILE = 128
NOTE_ROWS = 16
LOG2_SCALE = math.log2(math.e) / math.sqrt(HD)
VMEM_LIMIT = 24 * 1024 * 1024


def attend_kernel(plan, heads, carry_in, final, meta, *refs):
    refs = list(refs)
    q_ref = refs.pop(0)
    sources = []
    for parts, usable in plan:
        k_refs = [refs.pop(0) for _ in range(parts)]
        v_refs = [refs.pop(0) for _ in range(parts)]
        bias = None
        if usable is not None:
            bias = jnp.where(usable(meta), 0.0, -jnp.inf).astype(jnp.float32)
        sources.append((k_refs, v_refs, bias))
    if carry_in:
        acc_in, sum_in, max_in = refs.pop(0), refs.pop(0), refs.pop(0)
    outs = refs[-1:] if final else refs[-3:]
    rows = q_ref.shape[0]

    def load(some, cols):
        total = some[0][:, cols]
        for other in some[1:]:
            total = total + other[:, cols]
        return total

    groups = [[s] for s in sources if s[0][0].shape[0] > TILE]
    narrow = [s for s in sources if s[0][0].shape[0] == TILE]
    groups += [narrow[at : at + 2] for at in range(0, len(narrow), 2)]

    def columns(head):
        return slice(head * HD, (head + 1) * HD)

    def scores_of(head):
        cols = columns(head)
        scores = []
        for group in groups:
            key = jnp.concatenate([load(k, cols) for k, _, _ in group], axis=0)
            part = lax.dot_general(
                q_ref[:, cols], key, (((1,), (1,)), ((), ())), preferred_element_type=jnp.float32
            )
            pieces = []
            at = 0
            for k, _, bias in group:
                for _ in range(k[0].shape[0] // TILE):
                    piece = part[:, at : at + TILE] * LOG2_SCALE
                    pieces.append(piece if bias is None else piece + bias)
                    at += TILE
            scores.append(pieces)
        return scores

    def weigh(head, scores):
        peak = functools.reduce(jnp.maximum, [piece for pieces in scores for piece in pieces])
        peak = jnp.broadcast_to(jnp.max(peak, axis=1, keepdims=True), (rows, HD))
        if carry_in:
            peak = jnp.maximum(max_in[:, columns(head)], peak)
        weights = [
            jnp.concatenate([jnp.exp2(piece - peak).astype(jnp.bfloat16) for piece in pieces], axis=1)
            for pieces in scores
        ]
        return peak, weights

    def add_up(head, peak, weights):
        cols = columns(head)
        acc = total = None
        if carry_in:
            shrink = jnp.exp2(max_in[:, cols] - peak)
            acc = acc_in[:, cols] * shrink
            total = sum_in[:, cols] * shrink
        for group, weight in zip(groups, weights):
            value = jnp.concatenate([load(v, cols) for _, v, _ in group], axis=0)
            both = jnp.concatenate([value, jnp.ones_like(value)], axis=1)
            added = jnp.dot(weight, both, preferred_element_type=jnp.float32)
            acc = added[:, :HD] if acc is None else acc + added[:, :HD]
            total = added[:, HD:] if total is None else total + added[:, HD:]
        if final:
            outs[0][:, cols] = (acc / total).astype(jnp.bfloat16)
        else:
            outs[0][:, cols] = acc
            outs[1][:, cols] = total
            outs[2][:, cols] = peak

    scores = scores_of(0)
    last = None
    for head in range(heads):
        following = scores_of(head + 1) if head + 1 < heads else None
        weighed = weigh(head, scores)
        if last is not None:
            add_up(*last)
        last = (head, *weighed)
        scores = following
    add_up(*last)


def attend(queries, meta, sources, first, steps, heads, carry=None, final=False, into=None, held=0):
    rows, width = queries.shape
    block = heads * HD

    def spec(count, row, column):
        return pl.BlockSpec((count, block), lambda step, meta: (row(meta), column + step))

    def zero(meta):
        return 0

    operands, specs = [queries], [spec(rows, zero, first)]
    plan, keys_seen = [], 0
    for keys, values, usable in sources:
        for array, count, row, column in list(keys) + list(values):
            operands.append(array)
            specs.append(spec(count, row, column))
        keys_seen += keys[0][1]
        plan.append((len(keys), usable))
    if carry is not None:
        operands += list(carry)
        specs += [spec(rows, zero, held)] * 3
    aliases = {}
    if final:
        out_shape = jax.ShapeDtypeStruct((rows, width), jnp.bfloat16)
        out_specs = spec(rows, zero, first)
        if into is not None:
            aliases = {len(operands) + 1: 0}
            operands.append(into)
            specs.append(pl.BlockSpec(memory_space=pl.ANY))
    else:
        out_shape = [jax.ShapeDtypeStruct((rows, steps * block), jnp.float32)] * 3
        out_specs = [spec(rows, zero, 0)] * 3
    done = steps * block
    return pl.pallas_call(
        functools.partial(attend_kernel, plan, heads, carry is not None, final),
        name="attend_last" if final else "attend_more" if carry is not None else "attend_own",
        out_shape=out_shape,
        grid_spec=pltpu.PrefetchScalarGridSpec(
            num_scalar_prefetch=1, grid=(steps,), in_specs=specs, out_specs=out_specs
        ),
        input_output_aliases=aliases,
        compiler_params=pltpu.CompilerParams(vmem_limit_bytes=VMEM_LIMIT),
        cost_estimate=pl.CostEstimate(
            flops=4 * rows * keys_seen * done,
            bytes_accessed=4 * keys_seen * done + 2 * rows * done,
            transcendentals=rows * keys_seen * (done // HD),
        ),
    )(meta, *operands)


SCALAR = pl.BlockSpec(memory_space=pltpu.SMEM)
WHOLE = pl.BlockSpec(memory_space=pl.ANY)


def move(name, build, operands, specs, out_shape, out_specs, copies, moved, scratch=()):
    return pl.pallas_call(
        build,
        name=name,
        out_shape=out_shape,
        in_specs=specs,
        out_specs=out_specs,
        scratch_shapes=[*scratch, pltpu.SemaphoreType.DMA((copies,))],
        compiler_params=pltpu.CompilerParams(vmem_limit_bytes=VMEM_LIMIT),
        cost_estimate=pl.CostEstimate(flops=0, bytes_accessed=moved, transcendentals=0),
    )(*operands)


def in_hbm(array):
    return pltpu.with_memory_space_constraint(array, pltpu.HBM)


def tile_copies(sources, tile, target, sems, at):
    return [
        pltpu.make_async_copy(
            ref.at[pl.ds(pl.multiple_of(row + tile * TILE, TILE), TILE), pl.ds(first, target.shape[1])],
            target.at[pl.ds(n * TILE, TILE)],
            sems.at[at + n],
        )
        for n, (ref, row, first) in enumerate(sources)
    ]


def start_if(condition, copies):
    @pl.when(condition)
    def _():
        for copy in copies:
            copy.start()


def tile_at(ref, entry, tile_count):
    return jnp.clip(ref[0, entry], 0, tile_count - 1)


def write_note(note, ref, tile_count):
    lane = lax.broadcasted_iota(jnp.int32, note.shape, 1)
    row = jnp.zeros(note.shape, jnp.float32)
    for entry in range(8):
        row = jnp.where(lane == entry, tile_at(ref, entry, tile_count).astype(jnp.float32), row)
    note[...] = row.astype(jnp.bfloat16)


def read_note(note, entry, tile_count):
    here = (lax.broadcasted_iota(jnp.int32, note.shape, 1) == entry) & (
        lax.broadcasted_iota(jnp.int32, note.shape, 0) == 0
    )
    value = jnp.sum(jnp.where(here, note.astype(jnp.float32), 0.0))
    return jnp.clip(value.astype(jnp.int32), 0, tile_count - 1)


def begin(tile_lists, me, beside_list, across_list, keys, values, width):
    rows, all_width = keys.shape
    tile_count = rows // TILE

    def build(list_ref, me_ref, beside_ref, across_ref, k_ref, v_ref, *refs):
        meta, packed, to_beside, to_across, own_note, beside_note, sems = refs
        me = me_ref[0]
        right = me % 4 >= 2
        own = ((k_ref, 0, 0), (v_ref, 0, 0))
        copies = [
            pltpu.make_async_copy(
                ref.at[:, pl.ds(0, width)], packed.at[pl.ds(n * rows, rows)], sems.at[n]
            )
            for n, ref in enumerate((k_ref, v_ref))
        ]
        tile = tile_at(across_ref, jnp.where(right, 5, 1), tile_count)
        copies += tile_copies(own, tile, to_across, sems, 2)
        tile = tile_at(beside_ref, jnp.where(me % 2 == 0, 0, 4), tile_count)
        copies += tile_copies(own, tile, to_beside, sems, 4)
        for copy in copies:
            copy.start()
        write_note(own_note, list_ref, tile_count)
        write_note(beside_note, beside_ref, tile_count)
        notes = [
            pltpu.make_async_copy(
                own_note, packed.at[pl.ds(2 * rows, NOTE_ROWS), pl.ds(0, HD)], sems.at[6]
            ),
            pltpu.make_async_copy(
                beside_note, to_across.at[pl.ds(2 * TILE, NOTE_ROWS), pl.ds(0, HD)], sems.at[7]
            ),
        ]
        for copy in notes:
            copy.start()
        for entry in range(8):
            meta[entry] = tile_at(list_ref, entry, tile_count)
        meta[8] = me
        meta[9] = tile_at(across_ref, jnp.where(right, 1, 5), tile_count)
        for copy in copies + notes:
            copy.wait()

    return move(
        "begin",
        build,
        (tile_lists, me, beside_list, across_list, in_hbm(keys), in_hbm(values)),
        [SCALAR] * 4 + [WHOLE] * 2,
        [
            jax.ShapeDtypeStruct((10,), jnp.int32),
            jax.ShapeDtypeStruct((2 * rows + NOTE_ROWS, width), jnp.bfloat16),
            jax.ShapeDtypeStruct((2 * TILE, all_width), jnp.bfloat16),
            jax.ShapeDtypeStruct((2 * TILE + NOTE_ROWS, all_width), jnp.bfloat16),
        ],
        [SCALAR, WHOLE, WHOLE, WHOLE],
        8,
        24 * TILE * all_width,
        [pltpu.VMEM((NOTE_ROWS, HD), jnp.bfloat16)] * 2,
    )


def pack(keys, values, first, width, after):
    rows = keys.shape[0]

    def build(k_ref, v_ref, *refs):
        out_ref, sems = refs[-2:]
        copies = [
            pltpu.make_async_copy(
                ref.at[:, pl.ds(first, width)], out_ref.at[pl.ds(n * rows, rows)], sems.at[n]
            )
            for n, ref in enumerate((k_ref, v_ref))
        ]
        for copy in copies:
            copy.start()
        for copy in copies:
            copy.wait()

    return move(
        "pack",
        build,
        (in_hbm(keys), in_hbm(values), *after),
        [WHOLE] * (2 + len(after)),
        jax.ShapeDtypeStruct((2 * rows, width), jnp.bfloat16),
        WHOLE,
        2,
        8 * rows * width,
    )


def choose(meta, wants, over, keys, values, first, outer, inner, after):
    rows, width = keys.shape[0], outer.shape[1]
    tile_count = rows // TILE
    again = wants is not None

    def build(meta, *refs):
        if again:
            wants, k_ref, v_ref, outer, inner = refs[:5]
        else:
            over_ref, k_ref, v_ref, outer, inner = refs[:5]
            wants, notes = refs[-7], refs[-2]
        to_two, to_one, to_outer, to_inner = refs[-5:-1] if again else refs[-6:-2]
        sems = refs[-1]
        spot, plane = meta[8] % 4, meta[8] // 4
        right, odd = spot >= 2, plane % 2 == 1
        own = ((k_ref, 0, first), (v_ref, 0, first))
        from_outer = ((outer, 0, 0), (outer, rows, 0))
        from_inner = ((inner, 0, 0), (inner, rows, 0))
        if not again:
            reads = [
                pltpu.make_async_copy(
                    ref.at[pl.ds(at, NOTE_ROWS), pl.ds(0, HD)], notes.at[n], sems.at[8 + n]
                )
                for n, (ref, at) in enumerate(((over_ref, 2 * TILE), (outer, 2 * rows), (inner, 2 * rows)))
            ]
            for read in reads:
                read.start()
        start_if(right == odd, tile_copies(from_outer, meta[9], to_two, sems, 0))
        start_if(right != odd, tile_copies(from_inner, meta[9], to_two, sems, 0))
        if not again:
            for read in reads:
                read.wait()
            wants[0] = read_note(notes[0], jnp.where(spot % 2 == 0, 4, 0), tile_count)
            wants[1] = read_note(notes[1], jnp.where(plane == 1, 7, 3), tile_count)
            wants[2] = read_note(notes[2], jnp.where(plane == 1, 3, 7), tile_count)
        near_outer = ((spot == 0) & jnp.logical_not(odd)) | ((spot == 3) & odd)
        near_inner = ((spot == 0) & odd) | ((spot == 3) & jnp.logical_not(odd))
        start_if(near_outer, tile_copies(from_outer, wants[0], to_one, sems, 2))
        start_if(near_inner, tile_copies(from_inner, wants[0], to_one, sems, 2))
        start_if((spot == 1) | (spot == 2), tile_copies(own, wants[0], to_one, sems, 2))
        for copy in tile_copies(from_inner, wants[1], to_outer, sems, 4):
            copy.start()
        for copy in tile_copies(from_outer, wants[2], to_inner, sems, 6):
            copy.start()
        for n, target in enumerate((to_two, to_one, to_outer, to_inner)):
            for copy in tile_copies(from_outer, 0, target, sems, 2 * n):
                copy.wait()

    sent = [jax.ShapeDtypeStruct((2 * TILE, width), jnp.bfloat16)] * 4
    if again:
        operands, specs = (meta, wants), [SCALAR, SCALAR]
    else:
        operands, specs = (meta, over), [SCALAR, WHOLE]
        sent = [jax.ShapeDtypeStruct((3,), jnp.int32)] + sent
    return move(
        "choose_again" if again else "choose",
        build,
        (*operands, in_hbm(keys), in_hbm(values), outer, inner, *after),
        specs + [WHOLE] * (4 + len(after)),
        sent,
        [SCALAR] * (not again) + [WHOLE] * 4,
        11,
        32 * TILE * width,
        [] if again else [pltpu.VMEM((3, NOTE_ROWS, HD), jnp.bfloat16)],
    )


def send(array, route):
    return lax.ppermute(array, "frame", route)


def fixed(block):
    return lambda meta: block


def body_direct(queries, key_heads, value_heads, tile_lists):
    frames = lax.axis_size("frame")
    levels = frames.bit_length() - 1
    rows, width = key_heads.shape
    me = lax.axis_index("frame")
    lists = jnp.clip(lax.all_gather(tile_lists, "frame", tiled=True), 0, rows // TILE - 1)
    meta = me.astype(jnp.int32).reshape(1)
    sources = [([(key_heads, rows, fixed(0), 0)], [(value_heads, rows, fixed(0), 0)], None)]
    for level in range(levels):
        for entry, distance in ((level, 1 << level), (levels + level, -(1 << level))):
            route = [(i, i + distance) for i in range(frames) if 0 <= i + distance < frames]
            start = lists[jnp.clip(me + distance, 0, frames - 1), entry] * TILE
            both = [lax.dynamic_slice_in_dim(a, start, TILE, 0) for a in (key_heads, value_heads)]
            both = send(jnp.concatenate(both, axis=0), route)

            def usable(meta, distance=distance):
                return (meta[0] >= distance) & (meta[0] - distance < frames)

            sources.append(([(both, TILE, fixed(0), 0)], [(both, TILE, fixed(1), 0)], usable))
    return attend(queries, meta, sources, 0, width // (2 * HD), 2, final=True)


def body_planes(queries, key_heads, value_heads, tile_lists):
    frames = 16
    rows, width = key_heads.shape
    tile_count = rows // TILE
    half = width // 2
    heads = 3
    steps = half // (heads * HD)
    every = range(frames)
    beside = [(i, i ^ 1) for i in every]
    across = [(i, i ^ 2) for i in every]
    corner = [(i, i ^ 3) for i in every]
    outer = [(i, i ^ 4) for i in every]
    inner = [(i, i ^ 12) for i in every if i // 4 in (1, 2)]
    outward = [(i, i ^ 4) for i in every if i // 4 in (1, 2)]

    def right(meta):
        return meta[8] % 4 >= 2

    def two_there(meta):
        return jnp.where(right(meta), meta[8] + 2 < frames, meta[8] >= 2)

    def one_there(meta):
        return (meta[8] >= 1) & (meta[8] < frames - 1)

    def outer_tile(meta):
        return jnp.where(meta[8] // 4 % 2 == 1, meta[2], meta[6])

    def inner_tile(meta):
        return jnp.where(meta[8] // 4 % 2 == 1, meta[6], meta[2])

    def inner_there(meta):
        return (meta[8] >= 4) & (meta[8] < frames - 4)

    def own_frame():
        return [(key_heads, rows, fixed(0), 0)], [(value_heads, rows, fixed(0), 0)], None

    def tile_of(array, tile, usable=None):
        return [(array, TILE, tile, 0)], [(array, TILE, lambda meta: tile(meta) + tile_count, 0)], usable

    def sent_tile(arrays, column=0, usable=None):
        return [(a, TILE, fixed(0), column) for a in arrays], [(a, TILE, fixed(1), column) for a in arrays], usable

    me = lax.axis_index("frame").astype(jnp.int32).reshape(1)
    beside_list = send(tile_lists, beside)
    across_list = send(tile_lists, across)
    meta, first, to_beside, to_across = begin(
        tile_lists, me, beside_list, across_list, key_heads, value_heads, half
    )
    over = send(to_across, across)
    next_to = send(to_beside, beside)
    begun = attend(queries, meta, [own_frame()], 0, 2 * steps, heads)
    second = pack(key_heads, value_heads, half, half, [begun[0]])

    after, wants = [], None
    middles, finals = [], []
    for n, packed in enumerate((first, second)):
        from_outer = send(packed, outer)
        from_inner = send(packed, inner)
        sent = choose(meta, wants, over, key_heads, value_heads, n * half, from_outer, from_inner, after)
        if wants is None:
            wants, *sent = sent
        two = send(sent[0], across)
        one = send(sent[1], corner)
        far = [send(sent[2], outward), send(sent[3], inner)]
        middle = attend(
            queries,
            meta,
            [
                sent_tile([next_to], n * steps),
                sent_tile([over], n * steps),
                tile_of(from_outer, outer_tile),
                tile_of(from_inner, inner_tile, inner_there),
            ],
            n * steps,
            steps,
            heads,
            begun,
            held=n * steps,
        )
        after = [middle[0]]
        middles.append(middle)
        finals.append([sent_tile([two], 0, two_there), sent_tile([one], 0, one_there), sent_tile(far)])
    out = None
    for n in (0, 1):
        out = attend(queries, meta, finals[n], n * steps, steps, heads, middles[n], True, out)
    return out


def solution(mesh):
    body = body_planes if mesh.shape["frame"] == 16 else body_direct
    in_specs = (
        P(("groups", "frame"), None),
        P(("groups", "frame"), None),
        P(("groups", "frame"), None),
        P("frame", None),
    )
    out_specs = P(("groups", "frame"), None)
    return jax.shard_map(body, mesh=mesh, in_specs=in_specs, out_specs=out_specs, check_vma=False)
```

```python
import functools
import math

import jax
import jax.numpy as jnp
from jax import lax
from jax.experimental import pallas as pl
from jax.experimental.pallas import tpu as pltpu
from jax.sharding import PartitionSpec as P

HD = 128
TILE = 128
NOTE_ROWS = 16
LOG2_SCALE = math.log2(math.e) / math.sqrt(HD)
VMEM_LIMIT = 24 * 1024 * 1024


def attend_kernel(plan, heads, carry_in, final, meta, *refs):
    refs = list(refs)
    q_ref = refs.pop(0)
    sources = []
    for parts, usable in plan:
        k_refs = [refs.pop(0) for _ in range(parts)]
        v_refs = [refs.pop(0) for _ in range(parts)]
        bias = None
        if usable is not None:
            bias = jnp.where(usable(meta), 0.0, -jnp.inf).astype(jnp.float32)
        sources.append((k_refs, v_refs, bias))
    if carry_in:
        acc_in, sum_in, max_in = refs.pop(0), refs.pop(0), refs.pop(0)
    outs = refs[-1:] if final else refs[-3:]
    rows = q_ref.shape[0]

    def load(some, cols):
        total = some[0][:, cols]
        for other in some[1:]:
            total = total + other[:, cols]
        return total

    groups = [[s] for s in sources if s[0][0].shape[0] > TILE]
    narrow = [s for s in sources if s[0][0].shape[0] == TILE]
    groups += [narrow[at : at + 2] for at in range(0, len(narrow), 2)]

    def columns(head):
        return slice(head * HD, (head + 1) * HD)

    def scores_of(head):
        cols = columns(head)
        scores = []
        for group in groups:
            key = jnp.concatenate([load(k, cols) for k, _, _ in group], axis=0)
            part = lax.dot_general(
                q_ref[:, cols], key, (((1,), (1,)), ((), ())), preferred_element_type=jnp.float32
            )
            pieces = []
            at = 0
            for k, _, bias in group:
                for _ in range(k[0].shape[0] // TILE):
                    piece = part[:, at : at + TILE] * LOG2_SCALE
                    pieces.append(piece if bias is None else piece + bias)
                    at += TILE
            scores.append(pieces)
        return scores

    def weigh(head, scores):
        peak = functools.reduce(jnp.maximum, [piece for pieces in scores for piece in pieces])
        peak = jnp.broadcast_to(jnp.max(peak, axis=1, keepdims=True), (rows, HD))
        if carry_in:
            peak = jnp.maximum(max_in[:, columns(head)], peak)
        weights = [
            jnp.concatenate([jnp.exp2(piece - peak).astype(jnp.bfloat16) for piece in pieces], axis=1)
            for pieces in scores
        ]
        return peak, weights

    def add_up(head, peak, weights):
        cols = columns(head)
        acc = total = None
        if carry_in:
            shrink = jnp.exp2(max_in[:, cols] - peak)
            acc = acc_in[:, cols] * shrink
            total = sum_in[:, cols] * shrink
        for group, weight in zip(groups, weights):
            value = jnp.concatenate([load(v, cols) for _, v, _ in group], axis=0)
            both = jnp.concatenate([value, jnp.ones_like(value)], axis=1)
            added = jnp.dot(weight, both, preferred_element_type=jnp.float32)
            acc = added[:, :HD] if acc is None else acc + added[:, :HD]
            total = added[:, HD:] if total is None else total + added[:, HD:]
        if final:
            outs[0][:, cols] = (acc / total).astype(jnp.bfloat16)
        else:
            outs[0][:, cols] = acc
            outs[1][:, cols] = total
            outs[2][:, cols] = peak

    scores = scores_of(0)
    last = None
    for head in range(heads):
        following = scores_of(head + 1) if head + 1 < heads else None
        weighed = weigh(head, scores)
        if last is not None:
            add_up(*last)
        last = (head, *weighed)
        scores = following
    add_up(*last)


def attend(queries, meta, sources, first, steps, heads, carry=None, final=False, into=None, held=0):
    rows, width = queries.shape
    block = heads * HD

    def spec(count, row, column):
        return pl.BlockSpec((count, block), lambda step, meta: (row(meta), column + step))

    def zero(meta):
        return 0

    operands, specs = [queries], [spec(rows, zero, first)]
    plan, keys_seen = [], 0
    for keys, values, usable in sources:
        for array, count, row, column in list(keys) + list(values):
            operands.append(array)
            specs.append(spec(count, row, column))
        keys_seen += keys[0][1]
        plan.append((len(keys), usable))
    if carry is not None:
        operands += list(carry)
        specs += [spec(rows, zero, held)] * 3
    aliases = {}
    if final:
        out_shape = jax.ShapeDtypeStruct((rows, width), jnp.bfloat16)
        out_specs = spec(rows, zero, first)
        if into is not None:
            aliases = {len(operands) + 1: 0}
            operands.append(into)
            specs.append(pl.BlockSpec(memory_space=pl.ANY))
    else:
        out_shape = [jax.ShapeDtypeStruct((rows, steps * block), jnp.float32)] * 3
        out_specs = [spec(rows, zero, 0)] * 3
    done = steps * block
    return pl.pallas_call(
        functools.partial(attend_kernel, plan, heads, carry is not None, final),
        name="attend_last" if final else "attend_more" if carry is not None else "attend_own",
        out_shape=out_shape,
        grid_spec=pltpu.PrefetchScalarGridSpec(
            num_scalar_prefetch=1, grid=(steps,), in_specs=specs, out_specs=out_specs
        ),
        input_output_aliases=aliases,
        compiler_params=pltpu.CompilerParams(vmem_limit_bytes=VMEM_LIMIT),
        cost_estimate=pl.CostEstimate(
            flops=4 * rows * keys_seen * done,
            bytes_accessed=4 * keys_seen * done + 2 * rows * done,
            transcendentals=rows * keys_seen * (done // HD),
        ),
    )(meta, *operands)


SCALAR = pl.BlockSpec(memory_space=pltpu.SMEM)
WHOLE = pl.BlockSpec(memory_space=pl.ANY)


def move(name, build, operands, specs, out_shape, out_specs, copies, moved, scratch=()):
    return pl.pallas_call(
        build,
        name=name,
        out_shape=out_shape,
        in_specs=specs,
        out_specs=out_specs,
        scratch_shapes=[*scratch, pltpu.SemaphoreType.DMA((copies,))],
        compiler_params=pltpu.CompilerParams(vmem_limit_bytes=VMEM_LIMIT),
        cost_estimate=pl.CostEstimate(flops=0, bytes_accessed=moved, transcendentals=0),
    )(*operands)


def in_hbm(array):
    return pltpu.with_memory_space_constraint(array, pltpu.HBM)


def tile_copies(sources, tile, target, sems, at):
    return [
        pltpu.make_async_copy(
            ref.at[pl.ds(pl.multiple_of(row + tile * TILE, TILE), TILE), pl.ds(first, target.shape[1])],
            target.at[pl.ds(n * TILE, TILE)],
            sems.at[at + n],
        )
        for n, (ref, row, first) in enumerate(sources)
    ]


def start_if(condition, copies):
    @pl.when(condition)
    def _():
        for copy in copies:
            copy.start()


def tile_at(ref, entry, tile_count):
    return jnp.clip(ref[0, entry], 0, tile_count - 1)


def write_note(note, ref, tile_count):
    lane = lax.broadcasted_iota(jnp.int32, note.shape, 1)
    row = jnp.zeros(note.shape, jnp.float32)
    for entry in range(8):
        row = jnp.where(lane == entry, tile_at(ref, entry, tile_count).astype(jnp.float32), row)
    note[...] = row.astype(jnp.bfloat16)


def read_note(note, entry, tile_count):
    here = (lax.broadcasted_iota(jnp.int32, note.shape, 1) == entry) & (
        lax.broadcasted_iota(jnp.int32, note.shape, 0) == 0
    )
    value = jnp.sum(jnp.where(here, note.astype(jnp.float32), 0.0))
    return jnp.clip(value.astype(jnp.int32), 0, tile_count - 1)


def part_copies(k_ref, v_ref, first, width, target, sems, at):
    rows = k_ref.shape[0]
    return [
        pltpu.make_async_copy(
            ref.at[:, pl.ds(first, width)], target.at[pl.ds(n * rows, rows)], sems.at[at + n]
        )
        for n, ref in enumerate((k_ref, v_ref))
    ]


def begin(tile_lists, me, across_list, keys, values, width):
    rows, all_width = keys.shape
    tile_count = rows // TILE

    def build(me_ref, across_ref, list_hbm, k_ref, v_ref, meta, packed, to_across, list_ref, note, sems):
        read = pltpu.make_async_copy(list_hbm, list_ref, sems.at[5])
        read.start()
        me = me_ref[0]
        right = me % 4 >= 2
        copies = part_copies(k_ref, v_ref, 0, width, packed, sems, 0)
        tile = tile_at(across_ref, jnp.where(right, 5, 1), tile_count)
        copies += tile_copies(((k_ref, 0, 0), (v_ref, 0, 0)), tile, to_across, sems, 2)
        for copy in copies:
            copy.start()
        read.wait()
        write_note(note, list_ref, tile_count)
        last = pltpu.make_async_copy(
            note, packed.at[pl.ds(2 * rows, NOTE_ROWS), pl.ds(0, HD)], sems.at[4]
        )
        last.start()
        for entry in range(8):
            meta[entry] = tile_at(list_ref, entry, tile_count)
        meta[8] = me
        meta[9] = tile_at(across_ref, jnp.where(right, 1, 5), tile_count)
        for copy in copies + [last]:
            copy.wait()

    return move(
        "begin",
        build,
        (me, across_list, in_hbm(tile_lists), in_hbm(keys), in_hbm(values)),
        [SCALAR] * 2 + [WHOLE] * 3,
        [
            jax.ShapeDtypeStruct((10,), jnp.int32),
            jax.ShapeDtypeStruct((2 * rows + NOTE_ROWS, width), jnp.bfloat16),
            jax.ShapeDtypeStruct((2 * TILE, all_width), jnp.bfloat16),
        ],
        [SCALAR, WHOLE, WHOLE],
        6,
        8 * rows * width + 8 * TILE * all_width,
        [pltpu.SMEM(tile_lists.shape, jnp.int32), pltpu.VMEM((NOTE_ROWS, HD), jnp.bfloat16)],
    )


def choose_near(meta, beside_list, corner_list, keys, values):
    rows, width = keys.shape
    tile_count = rows // TILE

    def build(meta, beside_ref, corner_ref, k_ref, v_ref, wanted, to_beside, to_corner, sems):
        even = meta[8] % 2 == 0
        own = ((k_ref, 0, 0), (v_ref, 0, 0))
        copies = tile_copies(own, tile_at(beside_ref, jnp.where(even, 0, 4), tile_count), to_beside, sems, 0)
        wanted[0] = tile_at(corner_ref, jnp.where(even, 4, 0), tile_count)
        copies += tile_copies(own, wanted[0], to_corner, sems, 2)
        for copy in copies:
            copy.start()
        for copy in copies:
            copy.wait()

    tile = jax.ShapeDtypeStruct((2 * TILE, width), jnp.bfloat16)
    return move(
        "choose_near",
        build,
        (meta, beside_list, corner_list, in_hbm(keys), in_hbm(values)),
        [SCALAR] * 3 + [WHOLE] * 2,
        [jax.ShapeDtypeStruct((1,), jnp.int32), tile, tile],
        [SCALAR, WHOLE, WHOLE],
        4,
        16 * TILE * width,
    )


def pack(keys, values, first, width, after):
    rows = keys.shape[0]

    def build(k_ref, v_ref, *refs):
        out_ref, stage, sems = refs[-3:]
        reads = part_copies(k_ref, v_ref, first, width, stage, sems, 0)
        writes = [
            pltpu.make_async_copy(
                stage.at[pl.ds(n * rows, rows)], out_ref.at[pl.ds(n * rows, rows)], sems.at[2 + n]
            )
            for n in (0, 1)
        ]
        for read in reads:
            read.start()
        for read, write in zip(reads, writes):
            read.wait()
            write.start()
        for write in writes:
            write.wait()

    return move(
        "pack",
        build,
        (in_hbm(keys), in_hbm(values), *after),
        [WHOLE] * (2 + len(after)),
        jax.ShapeDtypeStruct((2 * rows, width), jnp.bfloat16),
        WHOLE,
        4,
        8 * rows * width,
        [pltpu.VMEM((2 * rows, width), jnp.bfloat16)],
    )


def choose(meta, corner_tile, wants, outer, inner, after):
    rows, width = outer.shape[0] // 2 // TILE * TILE, outer.shape[1]
    tile_count = rows // TILE
    again = wants is not None

    def build(meta, corner_ref, *refs):
        if again:
            wants, outer, inner = refs[:3]
            to_two, to_one, to_outer, to_inner = refs[-5:-1]
        else:
            outer, inner, wants = refs[:2] + refs[-7:-6]
            to_two, to_one, to_outer, to_inner, notes = refs[-6:-1]
        sems = refs[-1]
        spot, plane = meta[8] % 4, meta[8] // 4
        right, odd = spot >= 2, plane % 2 == 1
        from_outer = ((outer, 0, 0), (outer, rows, 0))
        from_inner = ((inner, 0, 0), (inner, rows, 0))
        if not again:
            reads = [
                pltpu.make_async_copy(
                    ref.at[pl.ds(2 * rows, NOTE_ROWS), pl.ds(0, HD)], notes.at[n], sems.at[8 + n]
                )
                for n, ref in enumerate((outer, inner))
            ]
            for read in reads:
                read.start()
        for source, here in ((from_outer, right == odd), (from_inner, right != odd)):
            start_if(
                here,
                tile_copies(source, meta[9], to_two, sems, 0)
                + tile_copies(source, corner_ref[0], to_one, sems, 2),
            )
        if not again:
            for read in reads:
                read.wait()
            wants[0] = read_note(notes[0], jnp.where(plane == 1, 7, 3), tile_count)
            wants[1] = read_note(notes[1], jnp.where(plane == 1, 3, 7), tile_count)
        copies = tile_copies(from_inner, wants[0], to_outer, sems, 4)
        copies += tile_copies(from_outer, wants[1], to_inner, sems, 6)
        for copy in copies:
            copy.start()
        for n, target in enumerate((to_two, to_one, to_outer, to_inner)):
            for copy in tile_copies(from_outer, 0, target, sems, 2 * n):
                copy.wait()

    sent = [jax.ShapeDtypeStruct((2 * TILE, width), jnp.bfloat16)] * 4
    return move(
        "choose_again" if again else "choose",
        build,
        (meta, corner_tile, *([wants] if again else []), outer, inner, *after),
        [SCALAR] * (2 + again) + [WHOLE] * (2 + len(after)),
        ([] if again else [jax.ShapeDtypeStruct((2,), jnp.int32)]) + sent,
        [SCALAR] * (not again) + [WHOLE] * 4,
        10,
        32 * TILE * width,
        [] if again else [pltpu.VMEM((2, NOTE_ROWS, HD), jnp.bfloat16)],
    )


def send(array, route):
    return lax.ppermute(array, "frame", route)


def fixed(block):
    return lambda meta: block


def body_direct(queries, key_heads, value_heads, tile_lists):
    frames = lax.axis_size("frame")
    levels = frames.bit_length() - 1
    rows, width = key_heads.shape
    me = lax.axis_index("frame")
    lists = jnp.clip(lax.all_gather(tile_lists, "frame", tiled=True), 0, rows // TILE - 1)
    meta = me.astype(jnp.int32).reshape(1)
    sources = [([(key_heads, rows, fixed(0), 0)], [(value_heads, rows, fixed(0), 0)], None)]
    for level in range(levels):
        for entry, distance in ((level, 1 << level), (levels + level, -(1 << level))):
            route = [(i, i + distance) for i in range(frames) if 0 <= i + distance < frames]
            start = lists[jnp.clip(me + distance, 0, frames - 1), entry] * TILE
            both = [lax.dynamic_slice_in_dim(a, start, TILE, 0) for a in (key_heads, value_heads)]
            both = send(jnp.concatenate(both, axis=0), route)

            def usable(meta, distance=distance):
                return (meta[0] >= distance) & (meta[0] - distance < frames)

            sources.append(([(both, TILE, fixed(0), 0)], [(both, TILE, fixed(1), 0)], usable))
    return attend(queries, meta, sources, 0, width // (2 * HD), 2, final=True)


def body_planes(queries, key_heads, value_heads, tile_lists):
    frames = 16
    rows, width = key_heads.shape
    tile_count = rows // TILE
    heads = 4
    block = heads * HD
    parts = ((0, 2), (2, 1))
    every = range(frames)
    beside = [(i, i ^ 1) for i in every]
    across = [(i, i ^ 2) for i in every]
    corner_in = [(i, i ^ 3) for i in every if i % 4 in (1, 2)]
    corner_out = [(i, i ^ 3) for i in every if i % 4 in (0, 3)]
    outer = [(i, i ^ 4) for i in every]
    inner = [(i, i ^ 12) for i in every if i // 4 in (1, 2)]
    outward = [(i, i ^ 4) for i in every if i // 4 in (1, 2)]

    def right(meta):
        return meta[8] % 4 >= 2

    def two_there(meta):
        return jnp.where(right(meta), meta[8] + 2 < frames, meta[8] >= 2)

    def one_there(meta):
        return (meta[8] >= 1) & (meta[8] < frames - 1)

    def outer_tile(meta):
        return jnp.where(meta[8] // 4 % 2 == 1, meta[2], meta[6])

    def inner_tile(meta):
        return jnp.where(meta[8] // 4 % 2 == 1, meta[6], meta[2])

    def inner_there(meta):
        return (meta[8] >= 4) & (meta[8] < frames - 4)

    def own_frame():
        return [(key_heads, rows, fixed(0), 0)], [(value_heads, rows, fixed(0), 0)], None

    def tile_of(array, tile, usable=None):
        return [(array, TILE, tile, 0)], [(array, TILE, lambda meta: tile(meta) + tile_count, 0)], usable

    def sent_tile(arrays, usable=None):
        return (
            [(a, TILE, fixed(0), column) for a, column in arrays],
            [(a, TILE, fixed(1), column) for a, column in arrays],
            usable,
        )

    me = lax.axis_index("frame").astype(jnp.int32).reshape(1)
    across_list = send(tile_lists, across)
    beside_list = send(tile_lists, beside)
    corner_list = send(across_list, beside)
    first_width = parts[0][1] * block
    meta, first, to_across = begin(tile_lists, me, across_list, key_heads, value_heads, first_width)
    over = send(to_across, across)
    corner_tile, to_beside, to_corner = choose_near(meta, beside_list, corner_list, key_heads, value_heads)
    next_to = send(to_beside, beside)
    one_in = send(to_corner, corner_in)
    begun = attend(queries, corner_tile, [own_frame()], 0, width // block, heads)
    second = pack(key_heads, value_heads, first_width, width - first_width, [begun[0]])

    after, wants = [over, next_to, one_in], None
    middles, finals = [], []
    for (at, steps), packed in zip(parts, (first, second)):
        from_outer = send(packed, outer)
        from_inner = send(packed, inner)
        sent = choose(meta, corner_tile, wants, from_outer, from_inner, after)
        if wants is None:
            wants, *sent = sent
        two = send(sent[0], across)
        one = send(sent[1], corner_out)
        far = [send(sent[2], outward), send(sent[3], inner)]
        middle = attend(
            queries,
            meta,
            [
                sent_tile([(next_to, at)]),
                sent_tile([(over, at)]),
                tile_of(from_outer, outer_tile),
                tile_of(from_inner, inner_tile, inner_there),
            ],
            at,
            steps,
            heads,
            begun,
            held=at,
        )
        after = [middle[0]]
        middles.append(middle)
        finals.append(
            [
                sent_tile([(two, 0)], two_there),
                sent_tile([(one_in, at), (one, 0)], one_there),
                sent_tile([(a, 0) for a in far]),
            ]
        )
    out = None
    for (at, steps), sources, middle in zip(parts, finals, middles):
        out = attend(queries, meta, sources, at, steps, heads, middle, True, out)
    return out


def solution(mesh):
    body = body_planes if mesh.shape["frame"] == 16 else body_direct
    in_specs = (
        P(("groups", "frame"), None),
        P(("groups", "frame"), None),
        P(("groups", "frame"), None),
        P("frame", None),
    )
    out_specs = P(("groups", "frame"), None)
    return jax.shard_map(body, mesh=mesh, in_specs=in_specs, out_specs=out_specs, check_vma=False)
```

```python
import functools
import math

import jax
import jax.numpy as jnp
from jax import lax
from jax.experimental import pallas as pl
from jax.experimental.pallas import tpu as pltpu
from jax.sharding import PartitionSpec as P

HD = 128
TILE = 128
NOTE_ROWS = 16
LOG2_SCALE = math.log2(math.e) / math.sqrt(HD)
VMEM_LIMIT = 24 * 1024 * 1024


def attend_kernel(plan, heads, carry_in, final, meta, *refs):
    refs = list(refs)
    q_ref = refs.pop(0)
    sources = []
    for parts, usable in plan:
        k_refs = [refs.pop(0) for _ in range(parts)]
        v_refs = [refs.pop(0) for _ in range(parts)]
        bias = None
        if usable is not None:
            bias = jnp.where(usable(meta), 0.0, -jnp.inf).astype(jnp.float32)
        sources.append((k_refs, v_refs, bias))
    if carry_in:
        acc_in, sum_in, max_in = refs.pop(0), refs.pop(0), refs.pop(0)
    outs = refs[-1:] if final else refs[-3:]
    rows = q_ref.shape[0]

    def load(some, cols):
        total = some[0][:, cols]
        for other in some[1:]:
            total = total + other[:, cols]
        return total

    groups = [[s] for s in sources if s[0][0].shape[0] > TILE]
    narrow = [s for s in sources if s[0][0].shape[0] == TILE]
    groups += [narrow[at : at + 2] for at in range(0, len(narrow), 2)]

    def columns(head):
        return slice(head * HD, (head + 1) * HD)

    def scores_of(head):
        cols = columns(head)
        scores = []
        for group in groups:
            key = jnp.concatenate([load(k, cols) for k, _, _ in group], axis=0)
            part = lax.dot_general(
                q_ref[:, cols], key, (((1,), (1,)), ((), ())), preferred_element_type=jnp.float32
            )
            pieces = []
            at = 0
            for k, _, bias in group:
                for _ in range(k[0].shape[0] // TILE):
                    piece = part[:, at : at + TILE] * LOG2_SCALE
                    pieces.append(piece if bias is None else piece + bias)
                    at += TILE
            scores.append(pieces)
        return scores

    def weigh(head, scores):
        peak = functools.reduce(jnp.maximum, [piece for pieces in scores for piece in pieces])
        peak = jnp.broadcast_to(jnp.max(peak, axis=1, keepdims=True), (rows, HD))
        if carry_in:
            peak = jnp.maximum(max_in[:, columns(head)], peak)
        weights = [
            jnp.concatenate([jnp.exp2(piece - peak).astype(jnp.bfloat16) for piece in pieces], axis=1)
            for pieces in scores
        ]
        return peak, weights

    def add_up(head, peak, weights):
        cols = columns(head)
        acc = total = None
        if carry_in:
            shrink = jnp.exp2(max_in[:, cols] - peak)
            acc = acc_in[:, cols] * shrink
            total = sum_in[:, cols] * shrink
        for group, weight in zip(groups, weights):
            value = jnp.concatenate([load(v, cols) for _, v, _ in group], axis=0)
            both = jnp.concatenate([value, jnp.ones_like(value)], axis=1)
            added = jnp.dot(weight, both, preferred_element_type=jnp.float32)
            acc = added[:, :HD] if acc is None else acc + added[:, :HD]
            total = added[:, HD:] if total is None else total + added[:, HD:]
        if final:
            outs[0][:, cols] = (acc / total).astype(jnp.bfloat16)
        else:
            outs[0][:, cols] = acc
            outs[1][:, cols] = total
            outs[2][:, cols] = peak

    scores = scores_of(0)
    last = None
    for head in range(heads):
        following = scores_of(head + 1) if head + 1 < heads else None
        weighed = weigh(head, scores)
        if last is not None:
            add_up(*last)
        last = (head, *weighed)
        scores = following
    add_up(*last)


def attend(queries, meta, sources, first, steps, heads, carry=None, final=False, into=None, held=0):
    rows, width = queries.shape
    block = heads * HD

    def spec(count, row, column):
        return pl.BlockSpec((count, block), lambda step, meta: (row(meta), column + step))

    def zero(meta):
        return 0

    operands, specs = [queries], [spec(rows, zero, first)]
    plan, keys_seen = [], 0
    for keys, values, usable in sources:
        for array, count, row, column in list(keys) + list(values):
            operands.append(array)
            specs.append(spec(count, row, column))
        keys_seen += keys[0][1]
        plan.append((len(keys), usable))
    if carry is not None:
        operands += list(carry)
        specs += [spec(rows, zero, held)] * 3
    aliases = {}
    if final:
        out_shape = jax.ShapeDtypeStruct((rows, width), jnp.bfloat16)
        out_specs = spec(rows, zero, first)
        if into is not None:
            aliases = {len(operands) + 1: 0}
            operands.append(into)
            specs.append(pl.BlockSpec(memory_space=pl.ANY))
    else:
        out_shape = [jax.ShapeDtypeStruct((rows, steps * block), jnp.float32)] * 3
        out_specs = [spec(rows, zero, 0)] * 3
    done = steps * block
    return pl.pallas_call(
        functools.partial(attend_kernel, plan, heads, carry is not None, final),
        name="attend_last" if final else "attend_more" if carry is not None else "attend_own",
        out_shape=out_shape,
        grid_spec=pltpu.PrefetchScalarGridSpec(
            num_scalar_prefetch=1, grid=(steps,), in_specs=specs, out_specs=out_specs
        ),
        input_output_aliases=aliases,
        compiler_params=pltpu.CompilerParams(vmem_limit_bytes=VMEM_LIMIT),
        cost_estimate=pl.CostEstimate(
            flops=4 * rows * keys_seen * done,
            bytes_accessed=4 * keys_seen * done + 2 * rows * done,
            transcendentals=rows * keys_seen * (done // HD),
        ),
    )(meta, *operands)


SCALAR = pl.BlockSpec(memory_space=pltpu.SMEM)
WHOLE = pl.BlockSpec(memory_space=pl.ANY)


def move(name, build, operands, specs, out_shape, out_specs, copies, moved, scratch=()):
    return pl.pallas_call(
        build,
        name=name,
        out_shape=out_shape,
        in_specs=specs,
        out_specs=out_specs,
        scratch_shapes=[*scratch, pltpu.SemaphoreType.DMA((copies,))],
        compiler_params=pltpu.CompilerParams(vmem_limit_bytes=VMEM_LIMIT),
        cost_estimate=pl.CostEstimate(flops=0, bytes_accessed=moved, transcendentals=0),
    )(*operands)


def in_hbm(array):
    return pltpu.with_memory_space_constraint(array, pltpu.HBM)


def tile_copies(sources, tile, target, sems, at):
    return [
        pltpu.make_async_copy(
            ref.at[pl.ds(pl.multiple_of(row + tile * TILE, TILE), TILE), pl.ds(first, target.shape[1])],
            target.at[pl.ds(n * TILE, TILE)],
            sems.at[at + n],
        )
        for n, (ref, row, first) in enumerate(sources)
    ]


def zero_copies(zeros, target, sems, at):
    return [
        pltpu.make_async_copy(zeros, target.at[pl.ds(n * TILE, TILE)], sems.at[at + n]) for n in (0, 1)
    ]


def start_if(condition, copies):
    @pl.when(condition)
    def _():
        for copy in copies:
            copy.start()


def tile_at(ref, entry, tile_count):
    return jnp.clip(ref[0, entry], 0, tile_count - 1)


def write_note(note, ref, tile_count):
    lane = lax.broadcasted_iota(jnp.int32, note.shape, 1)
    row = jnp.zeros(note.shape, jnp.float32)
    for entry in range(8):
        row = jnp.where(lane == entry, tile_at(ref, entry, tile_count).astype(jnp.float32), row)
    note[...] = row.astype(jnp.bfloat16)


def read_note(note, entry, tile_count):
    here = (lax.broadcasted_iota(jnp.int32, note.shape, 1) == entry) & (
        lax.broadcasted_iota(jnp.int32, note.shape, 0) == 0
    )
    value = jnp.sum(jnp.where(here, note.astype(jnp.float32), 0.0))
    return jnp.clip(value.astype(jnp.int32), 0, tile_count - 1)


def part_copies(k_ref, v_ref, first, width, target, sems, at):
    rows = k_ref.shape[0]
    return [
        pltpu.make_async_copy(
            ref.at[:, pl.ds(first, width)], target.at[pl.ds(n * rows, rows)], sems.at[at + n]
        )
        for n, ref in enumerate((k_ref, v_ref))
    ]


def begin(tile_lists, me, across_list, keys, values, width):
    rows, all_width = keys.shape
    tile_count = rows // TILE

    def build(me_ref, across_ref, list_hbm, k_ref, v_ref, meta, packed, to_across, list_ref, note, sems):
        read = pltpu.make_async_copy(list_hbm, list_ref, sems.at[5])
        read.start()
        me = me_ref[0]
        right = me % 4 >= 2
        copies = part_copies(k_ref, v_ref, 0, width, packed, sems, 0)
        tile = tile_at(across_ref, jnp.where(right, 5, 1), tile_count)
        copies += tile_copies(((k_ref, 0, 0), (v_ref, 0, 0)), tile, to_across, sems, 2)
        for copy in copies:
            copy.start()
        read.wait()
        write_note(note, list_ref, tile_count)
        last = pltpu.make_async_copy(
            note, packed.at[pl.ds(2 * rows, NOTE_ROWS), pl.ds(0, HD)], sems.at[4]
        )
        last.start()
        for entry in range(8):
            meta[entry] = tile_at(list_ref, entry, tile_count)
        meta[8] = me
        meta[9] = tile_at(across_ref, jnp.where(right, 1, 5), tile_count)
        for copy in copies + [last]:
            copy.wait()

    return move(
        "begin",
        build,
        (me, across_list, in_hbm(tile_lists), in_hbm(keys), in_hbm(values)),
        [SCALAR] * 2 + [WHOLE] * 3,
        [
            jax.ShapeDtypeStruct((10,), jnp.int32),
            jax.ShapeDtypeStruct((2 * rows + NOTE_ROWS, width), jnp.bfloat16),
            jax.ShapeDtypeStruct((2 * TILE, all_width), jnp.bfloat16),
        ],
        [SCALAR, WHOLE, WHOLE],
        6,
        8 * rows * width + 8 * TILE * all_width,
        [pltpu.SMEM(tile_lists.shape, jnp.int32), pltpu.VMEM((NOTE_ROWS, HD), jnp.bfloat16)],
    )


def choose_near(meta, beside_list, corner_list, keys, values):
    rows, width = keys.shape
    tile_count = rows // TILE

    def build(meta, beside_ref, corner_ref, k_ref, v_ref, wanted, to_beside, to_corner, zeros, sems):
        even = meta[8] % 2 == 0
        own = ((k_ref, 0, 0), (v_ref, 0, 0))
        copies = tile_copies(own, tile_at(beside_ref, jnp.where(even, 0, 4), tile_count), to_beside, sems, 0)
        for copy in copies:
            copy.start()
        wanted[0] = tile_at(corner_ref, jnp.where(even, 4, 0), tile_count)
        inside = (meta[8] % 4 == 1) | (meta[8] % 4 == 2)
        start_if(inside, tile_copies(own, wanted[0], to_corner, sems, 2))
        zeros[...] = jnp.zeros_like(zeros)
        blank = zero_copies(zeros, to_corner, sems, 2)
        start_if(jnp.logical_not(inside), blank)
        for copy in copies + blank:
            copy.wait()

    tile = jax.ShapeDtypeStruct((2 * TILE, width), jnp.bfloat16)
    return move(
        "choose_near",
        build,
        (meta, beside_list, corner_list, in_hbm(keys), in_hbm(values)),
        [SCALAR] * 3 + [WHOLE] * 2,
        [jax.ShapeDtypeStruct((1,), jnp.int32), tile, tile],
        [SCALAR, WHOLE, WHOLE],
        4,
        16 * TILE * width,
        [pltpu.VMEM((TILE, width), jnp.bfloat16)],
    )


def pack(keys, values, first, width, after):
    rows = keys.shape[0]

    def build(k_ref, v_ref, *refs):
        out_ref, stage, sems = refs[-3:]
        reads = part_copies(k_ref, v_ref, first, width, stage, sems, 0)
        writes = [
            pltpu.make_async_copy(
                stage.at[pl.ds(n * rows, rows)], out_ref.at[pl.ds(n * rows, rows)], sems.at[2 + n]
            )
            for n in (0, 1)
        ]
        for read in reads:
            read.start()
        for read, write in zip(reads, writes):
            read.wait()
            write.start()
        for write in writes:
            write.wait()

    return move(
        "pack",
        build,
        (in_hbm(keys), in_hbm(values), *after),
        [WHOLE] * (2 + len(after)),
        jax.ShapeDtypeStruct((2 * rows, width), jnp.bfloat16),
        WHOLE,
        4,
        8 * rows * width,
        [pltpu.VMEM((2 * rows, width), jnp.bfloat16)],
    )


def choose(meta, corner_tile, wants, outer, inner, after):
    rows, width = outer.shape[0] // 2 // TILE * TILE, outer.shape[1]
    tile_count = rows // TILE
    again = wants is not None

    def build(meta, corner_ref, *refs):
        if again:
            wants, outer, inner = refs[:3]
            to_two, to_one, to_outer, to_inner = refs[-6:-2]
        else:
            outer, inner, wants = refs[:2] + refs[-8:-7]
            to_two, to_one, to_outer, to_inner, notes = refs[-7:-2]
        zeros, sems = refs[-2:]
        spot, plane = meta[8] % 4, meta[8] // 4
        right, odd = spot >= 2, plane % 2 == 1
        from_outer = ((outer, 0, 0), (outer, rows, 0))
        from_inner = ((inner, 0, 0), (inner, rows, 0))
        if not again:
            reads = [
                pltpu.make_async_copy(
                    ref.at[pl.ds(2 * rows, NOTE_ROWS), pl.ds(0, HD)], notes.at[n], sems.at[8 + n]
                )
                for n, ref in enumerate((outer, inner))
            ]
            for read in reads:
                read.start()
        edge = (spot == 0) | (spot == 3)
        for source, here in ((from_outer, right == odd), (from_inner, right != odd)):
            start_if(here, tile_copies(source, meta[9], to_two, sems, 0))
            start_if(here & edge, tile_copies(source, corner_ref[0], to_one, sems, 2))
        zeros[...] = jnp.zeros_like(zeros)
        start_if(jnp.logical_not(edge), zero_copies(zeros, to_one, sems, 2))
        between = (plane == 1) | (plane == 2)
        start_if(
            jnp.logical_not(between),
            zero_copies(zeros, to_outer, sems, 4) + zero_copies(zeros, to_inner, sems, 6),
        )
        if not again:
            for read in reads:
                read.wait()
            wants[0] = read_note(notes[0], jnp.where(plane == 1, 7, 3), tile_count)
            wants[1] = read_note(notes[1], jnp.where(plane == 1, 3, 7), tile_count)
        start_if(
            between,
            tile_copies(from_inner, wants[0], to_outer, sems, 4)
            + tile_copies(from_outer, wants[1], to_inner, sems, 6),
        )
        for n, target in enumerate((to_two, to_one, to_outer, to_inner)):
            for copy in tile_copies(from_outer, 0, target, sems, 2 * n):
                copy.wait()

    sent = [jax.ShapeDtypeStruct((2 * TILE, width), jnp.bfloat16)] * 4
    return move(
        "choose_again" if again else "choose",
        build,
        (meta, corner_tile, *([wants] if again else []), outer, inner, *after),
        [SCALAR] * (2 + again) + [WHOLE] * (2 + len(after)),
        ([] if again else [jax.ShapeDtypeStruct((2,), jnp.int32)]) + sent,
        [SCALAR] * (not again) + [WHOLE] * 4,
        10,
        32 * TILE * width,
        ([] if again else [pltpu.VMEM((2, NOTE_ROWS, HD), jnp.bfloat16)])
        + [pltpu.VMEM((TILE, width), jnp.bfloat16)],
    )


def send(array, route):
    return lax.ppermute(array, "frame", route)


def fixed(block):
    return lambda meta: block


def body_direct(queries, key_heads, value_heads, tile_lists):
    frames = lax.axis_size("frame")
    levels = frames.bit_length() - 1
    rows, width = key_heads.shape
    me = lax.axis_index("frame")
    lists = jnp.clip(lax.all_gather(tile_lists, "frame", tiled=True), 0, rows // TILE - 1)
    meta = me.astype(jnp.int32).reshape(1)
    sources = [([(key_heads, rows, fixed(0), 0)], [(value_heads, rows, fixed(0), 0)], None)]
    for level in range(levels):
        for entry, distance in ((level, 1 << level), (levels + level, -(1 << level))):
            route = [(i, i + distance) for i in range(frames) if 0 <= i + distance < frames]
            start = lists[jnp.clip(me + distance, 0, frames - 1), entry] * TILE
            both = [lax.dynamic_slice_in_dim(a, start, TILE, 0) for a in (key_heads, value_heads)]
            both = send(jnp.concatenate(both, axis=0), route)

            def usable(meta, distance=distance):
                return (meta[0] >= distance) & (meta[0] - distance < frames)

            sources.append(([(both, TILE, fixed(0), 0)], [(both, TILE, fixed(1), 0)], usable))
    return attend(queries, meta, sources, 0, width // (2 * HD), 2, final=True)


def body_planes(queries, key_heads, value_heads, tile_lists):
    frames = 16
    rows, width = key_heads.shape
    tile_count = rows // TILE
    heads = 4
    block = heads * HD
    parts = ((0, 2), (2, 1))
    every = range(frames)
    beside = [(i, i ^ 1) for i in every]
    across = [(i, i ^ 2) for i in every]
    corner_in = [(i, i ^ 3 if i % 4 in (1, 2) else i) for i in every]
    corner_out = [(i, i ^ 3 if i % 4 in (0, 3) else i) for i in every]
    outer = [(i, i ^ 4) for i in every]
    inner = [(i, i ^ 12 if i // 4 in (1, 2) else i) for i in every]

    def right(meta):
        return meta[8] % 4 >= 2

    def two_there(meta):
        return jnp.where(right(meta), meta[8] + 2 < frames, meta[8] >= 2)

    def one_there(meta):
        return (meta[8] >= 1) & (meta[8] < frames - 1)

    def outer_tile(meta):
        return jnp.where(meta[8] // 4 % 2 == 1, meta[2], meta[6])

    def inner_tile(meta):
        return jnp.where(meta[8] // 4 % 2 == 1, meta[6], meta[2])

    def inner_there(meta):
        return (meta[8] >= 4) & (meta[8] < frames - 4)

    def own_frame():
        return [(key_heads, rows, fixed(0), 0)], [(value_heads, rows, fixed(0), 0)], None

    def tile_of(array, tile, usable=None):
        return [(array, TILE, tile, 0)], [(array, TILE, lambda meta: tile(meta) + tile_count, 0)], usable

    def sent_tile(arrays, usable=None):
        return (
            [(a, TILE, fixed(0), column) for a, column in arrays],
            [(a, TILE, fixed(1), column) for a, column in arrays],
            usable,
        )

    me = lax.axis_index("frame").astype(jnp.int32).reshape(1)
    across_list = send(tile_lists, across)
    beside_list = send(tile_lists, beside)
    corner_list = send(across_list, beside)
    first_width = parts[0][1] * block
    meta, first, to_across = begin(tile_lists, me, across_list, key_heads, value_heads, first_width)
    over = send(to_across, across)
    corner_tile, to_beside, to_corner = choose_near(meta, beside_list, corner_list, key_heads, value_heads)
    next_to = send(to_beside, beside)
    one_in = send(to_corner, corner_in)
    second = pack(key_heads, value_heads, first_width, width - first_width, [to_beside])
    near = [own_frame(), sent_tile([(next_to, 0)]), sent_tile([(over, 0)])]
    begun = attend(queries, meta, near, 0, width // block, heads)

    after, wants = [begun[0], one_in], None
    middles, finals = [], []
    for (at, steps), packed in zip(parts, (first, second)):
        from_outer = send(packed, outer)
        from_inner = send(packed, inner)
        sent = choose(meta, corner_tile, wants, from_outer, from_inner, after)
        if wants is None:
            wants, *sent = sent
        two = send(sent[0], across)
        one = send(sent[1], corner_out)
        far = [send(sent[2], outer), send(sent[3], inner)]
        middle = attend(
            queries,
            meta,
            [
                tile_of(from_outer, outer_tile),
                tile_of(from_inner, inner_tile, inner_there),
            ],
            at,
            steps,
            heads,
            begun,
            held=at,
        )
        after = [middle[0]]
        middles.append(middle)
        finals.append(
            [
                sent_tile([(two, 0)], two_there),
                sent_tile([(one_in, at), (one, 0)], one_there),
                sent_tile([(a, 0) for a in far]),
            ]
        )
    out = None
    for (at, steps), sources, middle in zip(parts, finals, middles):
        out = attend(queries, meta, sources, at, steps, heads, middle, True, out)
    return out


def solution(mesh):
    body = body_planes if mesh.shape["frame"] == 16 else body_direct
    in_specs = (
        P(("groups", "frame"), None),
        P(("groups", "frame"), None),
        P(("groups", "frame"), None),
        P("frame", None),
    )
    out_specs = P(("groups", "frame"), None)
    return jax.shard_map(body, mesh=mesh, in_specs=in_specs, out_specs=out_specs, check_vma=False)
```

```python
import functools
import math

import jax
import jax.numpy as jnp
from jax import lax
from jax.experimental import pallas as pl
from jax.experimental.pallas import tpu as pltpu
from jax.sharding import PartitionSpec as P

HD = 128
TILE = 128
NOTE_ROWS = 16
LOG2_SCALE = math.log2(math.e) / math.sqrt(HD)
VMEM_LIMIT = 24 * 1024 * 1024


def attend_kernel(plan, heads, carry_in, final, meta, *refs):
    refs = list(refs)
    q_ref = refs.pop(0)
    sources = []
    for parts, usable in plan:
        k_refs = [refs.pop(0) for _ in range(parts)]
        v_refs = [refs.pop(0) for _ in range(parts)]
        bias = None
        if usable is not None:
            bias = jnp.where(usable(meta), 0.0, -jnp.inf).astype(jnp.float32)
        sources.append((k_refs, v_refs, bias))
    if carry_in:
        acc_in, sum_in, max_in = refs.pop(0), refs.pop(0), refs.pop(0)
    outs = refs[-1:] if final else refs[-3:]
    rows = q_ref.shape[0]

    def load(some, cols):
        total = some[0][:, cols]
        for other in some[1:]:
            total = total + other[:, cols]
        return total

    groups = [[s] for s in sources if s[0][0].shape[0] > TILE]
    narrow = [s for s in sources if s[0][0].shape[0] == TILE]
    groups += [narrow[at : at + 2] for at in range(0, len(narrow), 2)]

    def columns(head):
        return slice(head * HD, (head + 1) * HD)

    def scores_of(head):
        cols = columns(head)
        scores = []
        for group in groups:
            key = jnp.concatenate([load(k, cols) for k, _, _ in group], axis=0)
            part = lax.dot_general(
                q_ref[:, cols], key, (((1,), (1,)), ((), ())), preferred_element_type=jnp.float32
            )
            pieces = []
            at = 0
            for k, _, bias in group:
                for _ in range(k[0].shape[0] // TILE):
                    piece = part[:, at : at + TILE] * LOG2_SCALE
                    pieces.append(piece if bias is None else piece + bias)
                    at += TILE
            scores.append(pieces)
        return scores

    def weigh(head, scores):
        peak = functools.reduce(jnp.maximum, [piece for pieces in scores for piece in pieces])
        peak = jnp.broadcast_to(jnp.max(peak, axis=1, keepdims=True), (rows, HD))
        if carry_in:
            peak = jnp.maximum(max_in[:, columns(head)], peak)
        weights = [
            jnp.concatenate([jnp.exp2(piece - peak).astype(jnp.bfloat16) for piece in pieces], axis=1)
            for pieces in scores
        ]
        return peak, weights

    def add_up(head, peak, weights):
        cols = columns(head)
        acc = total = None
        if carry_in:
            shrink = jnp.exp2(max_in[:, cols] - peak)
            acc = acc_in[:, cols] * shrink
            total = sum_in[:, cols] * shrink
        for group, weight in zip(groups, weights):
            value = jnp.concatenate([load(v, cols) for _, v, _ in group], axis=0)
            both = jnp.concatenate([value, jnp.ones_like(value)], axis=1)
            added = jnp.dot(weight, both, preferred_element_type=jnp.float32)
            acc = added[:, :HD] if acc is None else acc + added[:, :HD]
            total = added[:, HD:] if total is None else total + added[:, HD:]
        if final:
            outs[0][:, cols] = (acc / total).astype(jnp.bfloat16)
        else:
            outs[0][:, cols] = acc
            outs[1][:, cols] = total
            outs[2][:, cols] = peak

    scores = scores_of(0)
    last = None
    for head in range(heads):
        following = scores_of(head + 1) if head + 1 < heads else None
        weighed = weigh(head, scores)
        if last is not None:
            add_up(*last)
        last = (head, *weighed)
        scores = following
    add_up(*last)


def attend(queries, meta, sources, first, steps, heads, carry=None, final=False, into=None, held=0):
    rows, width = queries.shape
    block = heads * HD

    def spec(count, row, column):
        return pl.BlockSpec((count, block), lambda step, meta: (row(meta), column + step))

    def zero(meta):
        return 0

    operands, specs = [queries], [spec(rows, zero, first)]
    plan, keys_seen = [], 0
    for keys, values, usable in sources:
        for array, count, row, column in list(keys) + list(values):
            operands.append(array)
            specs.append(spec(count, row, column))
        keys_seen += keys[0][1]
        plan.append((len(keys), usable))
    if carry is not None:
        operands += list(carry)
        specs += [spec(rows, zero, held)] * 3
    aliases = {}
    if final:
        out_shape = jax.ShapeDtypeStruct((rows, width), jnp.bfloat16)
        out_specs = spec(rows, zero, first)
        if into is not None:
            aliases = {len(operands) + 1: 0}
            operands.append(into)
            specs.append(pl.BlockSpec(memory_space=pl.ANY))
    else:
        out_shape = [jax.ShapeDtypeStruct((rows, steps * block), jnp.float32)] * 3
        out_specs = [spec(rows, zero, 0)] * 3
    done = steps * block
    return pl.pallas_call(
        functools.partial(attend_kernel, plan, heads, carry is not None, final),
        name="attend_last" if final else "attend_more" if carry is not None else "attend_own",
        out_shape=out_shape,
        grid_spec=pltpu.PrefetchScalarGridSpec(
            num_scalar_prefetch=1, grid=(steps,), in_specs=specs, out_specs=out_specs
        ),
        input_output_aliases=aliases,
        compiler_params=pltpu.CompilerParams(vmem_limit_bytes=VMEM_LIMIT),
        cost_estimate=pl.CostEstimate(
            flops=4 * rows * keys_seen * done,
            bytes_accessed=4 * keys_seen * done + 2 * rows * done,
            transcendentals=rows * keys_seen * (done // HD),
        ),
    )(meta, *operands)


SCALAR = pl.BlockSpec(memory_space=pltpu.SMEM)
WHOLE = pl.BlockSpec(memory_space=pl.ANY)


def move(name, build, operands, specs, out_shape, out_specs, copies, moved, scratch=()):
    return pl.pallas_call(
        build,
        name=name,
        out_shape=out_shape,
        in_specs=specs,
        out_specs=out_specs,
        scratch_shapes=[*scratch, pltpu.SemaphoreType.DMA((copies,))],
        compiler_params=pltpu.CompilerParams(vmem_limit_bytes=VMEM_LIMIT),
        cost_estimate=pl.CostEstimate(flops=0, bytes_accessed=moved, transcendentals=0),
    )(*operands)


def in_hbm(array):
    return pltpu.with_memory_space_constraint(array, pltpu.HBM)


def tile_copies(sources, tile, target, sems, at):
    return [
        pltpu.make_async_copy(
            ref.at[pl.ds(pl.multiple_of(row + tile * TILE, TILE), TILE), pl.ds(first, target.shape[1])],
            target.at[pl.ds(n * TILE, TILE)],
            sems.at[at + n],
        )
        for n, (ref, row, first) in enumerate(sources)
    ]


def zero_copies(zeros, target, sems, at):
    return [
        pltpu.make_async_copy(zeros, target.at[pl.ds(n * TILE, TILE)], sems.at[at + n]) for n in (0, 1)
    ]


def start_if(condition, copies):
    @pl.when(condition)
    def _():
        for copy in copies:
            copy.start()


def tile_at(ref, entry, tile_count):
    return jnp.clip(ref[0, entry], 0, tile_count - 1)


def write_note(note, ref, tile_count):
    lane = lax.broadcasted_iota(jnp.int32, note.shape, 1)
    row = jnp.zeros(note.shape, jnp.float32)
    for entry in range(8):
        row = jnp.where(lane == entry, tile_at(ref, entry, tile_count).astype(jnp.float32), row)
    note[...] = row.astype(jnp.bfloat16)


def read_note(note, entry, tile_count):
    here = (lax.broadcasted_iota(jnp.int32, note.shape, 1) == entry) & (
        lax.broadcasted_iota(jnp.int32, note.shape, 0) == 0
    )
    value = jnp.sum(jnp.where(here, note.astype(jnp.float32), 0.0))
    return jnp.clip(value.astype(jnp.int32), 0, tile_count - 1)


def part_copies(k_ref, v_ref, first, width, target, sems, at):
    rows = k_ref.shape[0]
    return [
        pltpu.make_async_copy(
            ref.at[:, pl.ds(first, width)], target.at[pl.ds(n * rows, rows)], sems.at[at + n]
        )
        for n, ref in enumerate((k_ref, v_ref))
    ]


def begin(tile_lists, me, across_list, keys, values, width):
    rows, all_width = keys.shape
    tile_count = rows // TILE

    def build(me_ref, across_ref, list_hbm, k_ref, v_ref, meta, packed, to_across, list_ref, note, sems):
        read = pltpu.make_async_copy(list_hbm, list_ref, sems.at[5])
        read.start()
        me = me_ref[0]
        right = me % 4 >= 2
        copies = part_copies(k_ref, v_ref, 0, width, packed, sems, 0)
        tile = tile_at(across_ref, jnp.where(right, 5, 1), tile_count)
        copies += tile_copies(((k_ref, 0, 0), (v_ref, 0, 0)), tile, to_across, sems, 2)
        for copy in copies:
            copy.start()
        read.wait()
        write_note(note, list_ref, tile_count)
        last = pltpu.make_async_copy(
            note, packed.at[pl.ds(2 * rows, NOTE_ROWS), pl.ds(0, HD)], sems.at[4]
        )
        last.start()
        for entry in range(8):
            meta[entry] = tile_at(list_ref, entry, tile_count)
        meta[8] = me
        meta[9] = tile_at(across_ref, jnp.where(right, 1, 5), tile_count)
        for copy in copies + [last]:
            copy.wait()

    return move(
        "begin",
        build,
        (me, across_list, in_hbm(tile_lists), in_hbm(keys), in_hbm(values)),
        [SCALAR] * 2 + [WHOLE] * 3,
        [
            jax.ShapeDtypeStruct((10,), jnp.int32),
            jax.ShapeDtypeStruct((2 * rows + NOTE_ROWS, width), jnp.bfloat16),
            jax.ShapeDtypeStruct((2 * TILE, all_width), jnp.bfloat16),
        ],
        [SCALAR, WHOLE, WHOLE],
        6,
        8 * rows * width + 8 * TILE * all_width,
        [pltpu.SMEM(tile_lists.shape, jnp.int32), pltpu.VMEM((NOTE_ROWS, HD), jnp.bfloat16)],
    )


def choose_near(meta, beside_list, corner_list, keys, values, after):
    rows, width = keys.shape
    tile_count = rows // TILE

    def build(meta, beside_ref, corner_ref, k_ref, v_ref, *refs):
        wanted, to_beside, to_corner, zeros, sems = refs[-5:]
        even = meta[8] % 2 == 0
        own = ((k_ref, 0, 0), (v_ref, 0, 0))
        copies = tile_copies(own, tile_at(beside_ref, jnp.where(even, 0, 4), tile_count), to_beside, sems, 0)
        for copy in copies:
            copy.start()
        wanted[0] = tile_at(corner_ref, jnp.where(even, 4, 0), tile_count)
        inside = (meta[8] % 4 == 1) | (meta[8] % 4 == 2)
        start_if(inside, tile_copies(own, wanted[0], to_corner, sems, 2))
        zeros[...] = jnp.zeros_like(zeros)
        blank = zero_copies(zeros, to_corner, sems, 2)
        start_if(jnp.logical_not(inside), blank)
        for copy in copies + blank:
            copy.wait()

    tile = jax.ShapeDtypeStruct((2 * TILE, width), jnp.bfloat16)
    return move(
        "choose_near",
        build,
        (meta, beside_list, corner_list, in_hbm(keys), in_hbm(values), *after),
        [SCALAR] * 3 + [WHOLE] * (2 + len(after)),
        [jax.ShapeDtypeStruct((1,), jnp.int32), tile, tile],
        [SCALAR, WHOLE, WHOLE],
        4,
        16 * TILE * width,
        [pltpu.VMEM((TILE, width), jnp.bfloat16)],
    )


def pack(keys, values, first, width, after):
    rows = keys.shape[0]

    def build(k_ref, v_ref, *refs):
        out_ref, stage, sems = refs[-3:]
        reads = part_copies(k_ref, v_ref, first, width, stage, sems, 0)
        writes = [
            pltpu.make_async_copy(
                stage.at[pl.ds(n * rows, rows)], out_ref.at[pl.ds(n * rows, rows)], sems.at[2 + n]
            )
            for n in (0, 1)
        ]
        for read in reads:
            read.start()
        for read, write in zip(reads, writes):
            read.wait()
            write.start()
        for write in writes:
            write.wait()

    return move(
        "pack",
        build,
        (in_hbm(keys), in_hbm(values), *after),
        [WHOLE] * (2 + len(after)),
        jax.ShapeDtypeStruct((2 * rows, width), jnp.bfloat16),
        WHOLE,
        4,
        8 * rows * width,
        [pltpu.VMEM((2 * rows, width), jnp.bfloat16)],
    )


def halves_of(ref):
    rows = ref.shape[0] // 2 // TILE * TILE
    return (ref, 0, 0), (ref, rows, 0)


def start_far(plane, wants, outer, inner, to_outer, to_inner, zeros, sems, at):
    between = (plane == 1) | (plane == 2)
    start_if(
        between,
        tile_copies(halves_of(inner), wants[0], to_outer, sems, at)
        + tile_copies(halves_of(outer), wants[1], to_inner, sems, at + 2),
    )
    start_if(
        jnp.logical_not(between),
        zero_copies(zeros, to_outer, sems, at) + zero_copies(zeros, to_inner, sems, at + 2),
    )


def choose(meta, corner_tile, outer, inner, after, wants=None):
    width = outer.shape[1]
    count = 2 if wants is None else 4

    def build(meta, corner_ref, outer, inner, *refs):
        targets, zeros, sems = refs[-count - 2 : -2], refs[-2], refs[-1]
        spot, plane = meta[8] % 4, meta[8] // 4
        right, odd = spot >= 2, plane % 2 == 1
        edge = (spot == 0) | (spot == 3)
        for source, here in ((outer, right == odd), (inner, right != odd)):
            start_if(here, tile_copies(halves_of(source), meta[9], targets[0], sems, 0))
            start_if(here & edge, tile_copies(halves_of(source), corner_ref[0], targets[1], sems, 2))
        zeros[...] = jnp.zeros_like(zeros)
        start_if(jnp.logical_not(edge), zero_copies(zeros, targets[1], sems, 2))
        if count == 4:
            start_far(plane, refs[0], outer, inner, *targets[2:], zeros, sems, 4)
        for n, target in enumerate(targets):
            for copy in zero_copies(zeros, target, sems, 2 * n):
                copy.wait()

    extra = [] if wants is None else [wants]
    return move(
        "choose",
        build,
        (meta, corner_tile, outer, inner, *extra, *after),
        [SCALAR] * 2 + [WHOLE] * 2 + [SCALAR] * len(extra) + [WHOLE] * len(after),
        [jax.ShapeDtypeStruct((2 * TILE, width), jnp.bfloat16)] * count,
        [WHOLE] * count,
        2 * count,
        8 * count * TILE * width,
        [pltpu.VMEM((TILE, width), jnp.bfloat16)],
    )


def choose_far(meta, outer, inner, after):
    width = outer.shape[1]
    rows = outer.shape[0] - NOTE_ROWS
    tile_count = rows // 2 // TILE

    def build(meta, outer, inner, *refs):
        wants, to_outer, to_inner, zeros, notes, sems = refs[-6:]
        reads = [
            pltpu.make_async_copy(
                ref.at[pl.ds(rows, NOTE_ROWS), pl.ds(0, HD)], notes.at[n], sems.at[4 + n]
            )
            for n, ref in enumerate((outer, inner))
        ]
        for read in reads:
            read.start()
        plane = meta[8] // 4
        zeros[...] = jnp.zeros_like(zeros)
        for read in reads:
            read.wait()
        wants[0] = read_note(notes[0], jnp.where(plane == 1, 7, 3), tile_count)
        wants[1] = read_note(notes[1], jnp.where(plane == 1, 3, 7), tile_count)
        start_far(plane, wants, outer, inner, to_outer, to_inner, zeros, sems, 0)
        for copy in zero_copies(zeros, to_outer, sems, 0) + zero_copies(zeros, to_inner, sems, 2):
            copy.wait()

    sent = [jax.ShapeDtypeStruct((2 * TILE, width), jnp.bfloat16)] * 2
    return move(
        "choose_far",
        build,
        (meta, outer, inner, *after),
        [SCALAR] + [WHOLE] * (2 + len(after)),
        [jax.ShapeDtypeStruct((2,), jnp.int32)] + sent,
        [SCALAR] + [WHOLE] * 2,
        6,
        16 * TILE * width,
        [pltpu.VMEM((TILE, width), jnp.bfloat16), pltpu.VMEM((2, NOTE_ROWS, HD), jnp.bfloat16)],
    )


def send(array, route):
    return lax.ppermute(array, "frame", route)


def fixed(block):
    return lambda meta: block


def body_direct(queries, key_heads, value_heads, tile_lists):
    frames = lax.axis_size("frame")
    levels = frames.bit_length() - 1
    rows, width = key_heads.shape
    me = lax.axis_index("frame")
    lists = jnp.clip(lax.all_gather(tile_lists, "frame", tiled=True), 0, rows // TILE - 1)
    meta = me.astype(jnp.int32).reshape(1)
    sources = [([(key_heads, rows, fixed(0), 0)], [(value_heads, rows, fixed(0), 0)], None)]
    for level in range(levels):
        for entry, distance in ((level, 1 << level), (levels + level, -(1 << level))):
            route = [(i, i + distance) for i in range(frames) if 0 <= i + distance < frames]
            start = lists[jnp.clip(me + distance, 0, frames - 1), entry] * TILE
            both = [lax.dynamic_slice_in_dim(a, start, TILE, 0) for a in (key_heads, value_heads)]
            both = send(jnp.concatenate(both, axis=0), route)

            def usable(meta, distance=distance):
                return (meta[0] >= distance) & (meta[0] - distance < frames)

            sources.append(([(both, TILE, fixed(0), 0)], [(both, TILE, fixed(1), 0)], usable))
    return attend(queries, meta, sources, 0, width // (2 * HD), 2, final=True)


def body_planes(queries, key_heads, value_heads, tile_lists):
    frames = 16
    rows, width = key_heads.shape
    tile_count = rows // TILE
    heads = 3
    block = heads * HD
    parts = ((0, 2), (2, 2))
    every = range(frames)
    beside = [(i, i ^ 1) for i in every]
    across = [(i, i ^ 2) for i in every]
    corner_in = [(i, i ^ 3 if i % 4 in (1, 2) else i) for i in every]
    corner_out = [(i, i ^ 3 if i % 4 in (0, 3) else i) for i in every]
    outer = [(i, i ^ 4) for i in every]
    inner = [(i, i ^ 12 if i // 4 in (1, 2) else i) for i in every]

    def right(meta):
        return meta[8] % 4 >= 2

    def two_there(meta):
        return jnp.where(right(meta), meta[8] + 2 < frames, meta[8] >= 2)

    def one_there(meta):
        return (meta[8] >= 1) & (meta[8] < frames - 1)

    def outer_tile(meta):
        return jnp.where(meta[8] // 4 % 2 == 1, meta[2], meta[6])

    def inner_tile(meta):
        return jnp.where(meta[8] // 4 % 2 == 1, meta[6], meta[2])

    def inner_there(meta):
        return (meta[8] >= 4) & (meta[8] < frames - 4)

    def own_frame():
        return [(key_heads, rows, fixed(0), 0)], [(value_heads, rows, fixed(0), 0)], None

    def tile_of(array, tile, usable=None):
        return [(array, TILE, tile, 0)], [(array, TILE, lambda meta: tile(meta) + tile_count, 0)], usable

    def sent_tile(arrays, usable=None):
        return (
            [(a, TILE, fixed(0), column) for a, column in arrays],
            [(a, TILE, fixed(1), column) for a, column in arrays],
            usable,
        )

    me = lax.axis_index("frame").astype(jnp.int32).reshape(1)
    across_list = send(tile_lists, across)
    beside_list = send(tile_lists, beside)
    corner_list = send(across_list, beside)
    first_width = parts[0][1] * block
    meta, first, to_across = begin(tile_lists, me, across_list, key_heads, value_heads, first_width)
    over = send(to_across, across)
    begun = attend(queries, meta, [own_frame()], 0, width // block, heads)
    second = pack(key_heads, value_heads, first_width, width - first_width, [begun[0]])
    corner_tile, to_beside, to_corner = choose_near(
        meta, beside_list, corner_list, key_heads, value_heads, [over, second]
    )
    next_to = send(to_beside, beside)
    one_in = send(to_corner, corner_in)

    after, wants = [], None
    middles, finals = [], []
    for (at, steps), packed in zip(parts, (first, second)):
        from_outer = send(packed, outer)
        from_inner = send(packed, inner)
        to_two, to_one, *to_far = choose(meta, corner_tile, from_outer, from_inner, after, wants)
        z_tiles = [
            tile_of(from_outer, outer_tile),
            tile_of(from_inner, inner_tile, inner_there),
            sent_tile([(over, at)]),
            sent_tile([(next_to, at)]),
        ]
        two = send(to_two, across)
        one = send(to_one, corner_out)
        middle = attend(queries, meta, z_tiles, at, steps, heads, begun, held=at)
        if wants is None:
            wants, *to_far = choose_far(meta, from_outer, from_inner, [middle[0], one_in])
        far = [send(to_far[0], outer), send(to_far[1], inner)]
        after = [middle[0]]
        middles.append(middle)
        finals.append(
            [
                sent_tile([(two, 0)], two_there),
                sent_tile([(one_in, at), (one, 0)], one_there),
                sent_tile([(a, 0) for a in far]),
            ]
        )
    out = None
    for (at, steps), sources, middle in zip(parts, finals, middles):
        out = attend(queries, meta, sources, at, steps, heads, middle, True, out)
    return out


def solution(mesh):
    body = body_planes if mesh.shape["frame"] == 16 else body_direct
    in_specs = (
        P(("groups", "frame"), None),
        P(("groups", "frame"), None),
        P(("groups", "frame"), None),
        P("frame", None),
    )
    out_specs = P(("groups", "frame"), None)
    return jax.shard_map(body, mesh=mesh, in_specs=in_specs, out_specs=out_specs, check_vma=False)
```

```python
import functools
import math

import jax
import jax.numpy as jnp
from jax import lax
from jax.experimental import pallas as pl
from jax.experimental.pallas import tpu as pltpu
from jax.sharding import PartitionSpec as P

HD = 128
TILE = 128
LOG2_SCALE = math.log2(math.e) / math.sqrt(HD)
VMEM_LIMIT = 24 * 1024 * 1024


def attend_kernel(plan, heads, carry_in, final, meta, *refs):
    refs = list(refs)
    q_ref = refs.pop(0)
    sources = []
    for parts, usable in plan:
        k_refs = [refs.pop(0) for _ in range(parts)]
        v_refs = [refs.pop(0) for _ in range(parts)]
        bias = None
        if usable is not None:
            bias = jnp.where(usable(meta), 0.0, -jnp.inf).astype(jnp.float32)
        sources.append((k_refs, v_refs, bias))
    if carry_in:
        acc_in, sum_in, max_in = refs.pop(0), refs.pop(0), refs.pop(0)
    outs = refs[-1:] if final else refs[-3:]
    rows = q_ref.shape[0]

    def load(some, cols):
        total = some[0][:, cols]
        for other in some[1:]:
            total = total + other[:, cols]
        return total

    groups = [[s] for s in sources if s[0][0].shape[0] > TILE]
    narrow = [s for s in sources if s[0][0].shape[0] == TILE]
    groups += [narrow[at : at + 2] for at in range(0, len(narrow), 2)]

    def columns(head):
        return slice(head * HD, (head + 1) * HD)

    def scores_of(head):
        cols = columns(head)
        scores = []
        for group in groups:
            key = jnp.concatenate([load(k, cols) for k, _, _ in group], axis=0)
            part = lax.dot_general(
                q_ref[:, cols], key, (((1,), (1,)), ((), ())), preferred_element_type=jnp.float32
            )
            pieces = []
            at = 0
            for k, _, bias in group:
                for _ in range(k[0].shape[0] // TILE):
                    piece = part[:, at : at + TILE] * LOG2_SCALE
                    pieces.append(piece if bias is None else piece + bias)
                    at += TILE
            scores.append(pieces)
        return scores

    def weigh(head, scores):
        peak = functools.reduce(jnp.maximum, [piece for pieces in scores for piece in pieces])
        peak = jnp.broadcast_to(jnp.max(peak, axis=1, keepdims=True), (rows, HD))
        if carry_in:
            peak = jnp.maximum(max_in[:, columns(head)], peak)
        weights = [
            jnp.concatenate([jnp.exp2(piece - peak).astype(jnp.bfloat16) for piece in pieces], axis=1)
            for pieces in scores
        ]
        return peak, weights

    def add_up(head, peak, weights):
        cols = columns(head)
        acc = total = None
        if carry_in:
            shrink = jnp.exp2(max_in[:, cols] - peak)
            acc = acc_in[:, cols] * shrink
            total = sum_in[:, cols] * shrink
        for group, weight in zip(groups, weights):
            value = jnp.concatenate([load(v, cols) for _, v, _ in group], axis=0)
            both = jnp.concatenate([value, jnp.ones_like(value)], axis=1)
            added = jnp.dot(weight, both, preferred_element_type=jnp.float32)
            acc = added[:, :HD] if acc is None else acc + added[:, :HD]
            total = added[:, HD:] if total is None else total + added[:, HD:]
        if final:
            outs[0][:, cols] = (acc / total).astype(jnp.bfloat16)
        else:
            outs[0][:, cols] = acc
            outs[1][:, cols] = total
            outs[2][:, cols] = peak

    scores = scores_of(0)
    last = None
    for head in range(heads):
        following = scores_of(head + 1) if head + 1 < heads else None
        weighed = weigh(head, scores)
        if last is not None:
            add_up(*last)
        last = (head, *weighed)
        scores = following
    add_up(*last)


def attend(queries, meta, sources, first, steps, heads, carry=None, final=False, into=None, held=0):
    rows, width = queries.shape
    block = heads * HD

    def spec(count, row, column):
        return pl.BlockSpec((count, block), lambda step, meta: (row(meta), column + step))

    def zero(meta):
        return 0

    operands, specs = [queries], [spec(rows, zero, first)]
    plan, keys_seen = [], 0
    for keys, values, usable in sources:
        for array, count, row, column in list(keys) + list(values):
            operands.append(array)
            specs.append(spec(count, row, column))
        keys_seen += keys[0][1]
        plan.append((len(keys), usable))
    if carry is not None:
        operands += list(carry)
        specs += [spec(rows, zero, held)] * 3
    aliases = {}
    if final:
        out_shape = jax.ShapeDtypeStruct((rows, width), jnp.bfloat16)
        out_specs = spec(rows, zero, first)
        if into is not None:
            aliases = {len(operands) + 1: 0}
            operands.append(into)
            specs.append(pl.BlockSpec(memory_space=pl.ANY))
    else:
        out_shape = [jax.ShapeDtypeStruct((rows, steps * block), jnp.float32)] * 3
        out_specs = [spec(rows, zero, 0)] * 3
    done = steps * block
    return pl.pallas_call(
        functools.partial(attend_kernel, plan, heads, carry is not None, final),
        name="attend_last" if final else "attend_more" if carry is not None else "attend_own",
        out_shape=out_shape,
        grid_spec=pltpu.PrefetchScalarGridSpec(
            num_scalar_prefetch=1, grid=(steps,), in_specs=specs, out_specs=out_specs
        ),
        input_output_aliases=aliases,
        compiler_params=pltpu.CompilerParams(vmem_limit_bytes=VMEM_LIMIT),
        cost_estimate=pl.CostEstimate(
            flops=4 * rows * keys_seen * done,
            bytes_accessed=4 * keys_seen * done + 2 * rows * done,
            transcendentals=rows * keys_seen * (done // HD),
        ),
    )(meta, *operands)


SCALAR = pl.BlockSpec(memory_space=pltpu.SMEM)
WHOLE = pl.BlockSpec(memory_space=pl.ANY)


def move(name, build, operands, specs, out_shape, out_specs, copies, moved, scratch=()):
    return pl.pallas_call(
        build,
        name=name,
        out_shape=out_shape,
        in_specs=specs,
        out_specs=out_specs,
        scratch_shapes=[*scratch, pltpu.SemaphoreType.DMA((copies,))],
        compiler_params=pltpu.CompilerParams(vmem_limit_bytes=VMEM_LIMIT),
        cost_estimate=pl.CostEstimate(flops=0, bytes_accessed=moved, transcendentals=0),
    )(*operands)


def in_hbm(array):
    return pltpu.with_memory_space_constraint(array, pltpu.HBM)


def tile_copies(sources, tile, target, sems, at):
    return [
        pltpu.make_async_copy(
            ref.at[pl.ds(pl.multiple_of(row + tile * TILE, TILE), TILE), pl.ds(first, target.shape[1])],
            target.at[pl.ds(n * TILE, TILE)],
            sems.at[at + n],
        )
        for n, (ref, row, first) in enumerate(sources)
    ]


def zero_copies(zeros, target, sems, at):
    return [
        pltpu.make_async_copy(zeros, target.at[pl.ds(n * TILE, TILE)], sems.at[at + n]) for n in (0, 1)
    ]


def start_if(condition, copies):
    @pl.when(condition)
    def _():
        for copy in copies:
            copy.start()


def tile_at(ref, entry, tile_count):
    return jnp.clip(ref[0, entry], 0, tile_count - 1)


def part_copies(k_ref, v_ref, first, width, target, sems, at):
    rows = k_ref.shape[0]
    return [
        pltpu.make_async_copy(
            ref.at[:, pl.ds(first, width)], target.at[pl.ds(n * rows, rows)], sems.at[at + n]
        )
        for n, ref in enumerate((k_ref, v_ref))
    ]


def begin(tile_lists, me, across_list, keys, values, width):
    rows, all_width = keys.shape
    tile_count = rows // TILE

    def build(me_ref, across_ref, list_hbm, k_ref, v_ref, meta, packed, to_across, list_ref, sems):
        read = pltpu.make_async_copy(list_hbm, list_ref, sems.at[4])
        read.start()
        me = me_ref[0]
        right = me % 4 >= 2
        copies = part_copies(k_ref, v_ref, 0, width, packed, sems, 0)
        tile = tile_at(across_ref, jnp.where(right, 5, 1), tile_count)
        copies += tile_copies(((k_ref, 0, 0), (v_ref, 0, 0)), tile, to_across, sems, 2)
        for copy in copies:
            copy.start()
        read.wait()
        for entry in range(8):
            meta[entry] = tile_at(list_ref, entry, tile_count)
        meta[8] = me
        meta[9] = tile_at(across_ref, jnp.where(right, 1, 5), tile_count)
        for copy in copies:
            copy.wait()

    return move(
        "begin",
        build,
        (me, across_list, in_hbm(tile_lists), in_hbm(keys), in_hbm(values)),
        [SCALAR] * 2 + [WHOLE] * 3,
        [
            jax.ShapeDtypeStruct((10,), jnp.int32),
            jax.ShapeDtypeStruct((2 * rows, width), jnp.bfloat16),
            jax.ShapeDtypeStruct((2 * TILE, all_width), jnp.bfloat16),
        ],
        [SCALAR, WHOLE, WHOLE],
        5,
        8 * rows * width + 8 * TILE * all_width,
        [pltpu.SMEM(tile_lists.shape, jnp.int32)],
    )


def choose_near(meta, tile_lists, beside_list, corner_list, keys, values):
    rows, width = keys.shape
    tile_count = rows // TILE

    def build(meta, list_hbm, beside_ref, corner_ref, k_ref, v_ref, wanted, listing, to_beside, to_corner, zeros, sems):
        even = meta[8] % 2 == 0
        own = ((k_ref, 0, 0), (v_ref, 0, 0))
        copies = tile_copies(own, tile_at(beside_ref, jnp.where(even, 0, 4), tile_count), to_beside, sems, 0)
        copies.append(pltpu.make_async_copy(list_hbm, listing, sems.at[4]))
        for copy in copies:
            copy.start()
        wanted[0] = tile_at(corner_ref, jnp.where(even, 4, 0), tile_count)
        inside = (meta[8] % 4 == 1) | (meta[8] % 4 == 2)
        start_if(inside, tile_copies(own, wanted[0], to_corner, sems, 2))
        zeros[...] = jnp.zeros_like(zeros)
        blank = zero_copies(zeros, to_corner, sems, 2)
        start_if(jnp.logical_not(inside), blank)
        for copy in copies + blank:
            copy.wait()

    tile = jax.ShapeDtypeStruct((2 * TILE, width), jnp.bfloat16)
    return move(
        "choose_near",
        build,
        (meta, in_hbm(tile_lists), beside_list, corner_list, in_hbm(keys), in_hbm(values)),
        [SCALAR, WHOLE] + [SCALAR] * 2 + [WHOLE] * 2,
        [
            jax.ShapeDtypeStruct((1,), jnp.int32),
            jax.ShapeDtypeStruct(tile_lists.shape, jnp.int32),
            tile,
            tile,
        ],
        [SCALAR, WHOLE, WHOLE, WHOLE],
        5,
        16 * TILE * width,
        [pltpu.VMEM((TILE, width), jnp.bfloat16)],
    )


def pack(keys, values, first, width, after):
    rows = keys.shape[0]

    def build(k_ref, v_ref, *refs):
        out_ref, stage, sems = refs[-3:]
        reads = part_copies(k_ref, v_ref, first, width, stage, sems, 0)
        writes = [
            pltpu.make_async_copy(
                stage.at[pl.ds(n * rows, rows)], out_ref.at[pl.ds(n * rows, rows)], sems.at[2 + n]
            )
            for n in (0, 1)
        ]
        for read in reads:
            read.start()
        for read, write in zip(reads, writes):
            read.wait()
            write.start()
        for write in writes:
            write.wait()

    return move(
        "pack",
        build,
        (in_hbm(keys), in_hbm(values), *after),
        [WHOLE] * (2 + len(after)),
        jax.ShapeDtypeStruct((2 * rows, width), jnp.bfloat16),
        WHOLE,
        4,
        8 * rows * width,
        [pltpu.VMEM((2 * rows, width), jnp.bfloat16)],
    )


def choose(meta, corner_tile, far_list, keys, values, first, outer, inner, after):
    rows, width = keys.shape[0], outer.shape[1]
    tile_count = rows // TILE

    def build(meta, corner_ref, far_ref, k_ref, v_ref, outer, inner, *refs):
        to_two, to_one, to_far, zeros, sems = refs[-5:]
        spot, plane = meta[8] % 4, meta[8] // 4
        right, odd = spot >= 2, plane % 2 == 1
        edge = (spot == 0) | (spot == 3)
        between = (plane == 1) | (plane == 2)
        own = ((k_ref, 0, first), (v_ref, 0, first))
        from_outer = ((outer, 0, 0), (outer, rows, 0))
        from_inner = ((inner, 0, 0), (inner, rows, 0))
        for source, here in ((from_outer, right == odd), (from_inner, right != odd)):
            start_if(here, tile_copies(source, meta[9], to_two, sems, 0))
            start_if(here & edge, tile_copies(source, corner_ref[0], to_one, sems, 2))
        tile = tile_at(far_ref, jnp.where(odd, 7, 3), tile_count)
        start_if(between, tile_copies(from_inner, tile, to_far, sems, 4))
        start_if(jnp.logical_not(between), tile_copies(own, tile, to_far, sems, 4))
        zeros[...] = jnp.zeros_like(zeros)
        start_if(jnp.logical_not(edge), zero_copies(zeros, to_one, sems, 2))
        for n, target in enumerate((to_two, to_one, to_far)):
            for copy in zero_copies(zeros, target, sems, 2 * n):
                copy.wait()

    return move(
        "choose",
        build,
        (meta, corner_tile, far_list, in_hbm(keys), in_hbm(values), outer, inner, *after),
        [SCALAR] * 3 + [WHOLE] * (4 + len(after)),
        [jax.ShapeDtypeStruct((2 * TILE, width), jnp.bfloat16)] * 3,
        [WHOLE] * 3,
        6,
        24 * TILE * width,
        [pltpu.VMEM((TILE, width), jnp.bfloat16)],
    )


def send(array, route):
    return lax.ppermute(array, "frame", route)


def fixed(block):
    return lambda meta: block


def body_direct(queries, key_heads, value_heads, tile_lists):
    frames = lax.axis_size("frame")
    levels = frames.bit_length() - 1
    rows, width = key_heads.shape
    me = lax.axis_index("frame")
    lists = jnp.clip(lax.all_gather(tile_lists, "frame", tiled=True), 0, rows // TILE - 1)
    meta = me.astype(jnp.int32).reshape(1)
    sources = [([(key_heads, rows, fixed(0), 0)], [(value_heads, rows, fixed(0), 0)], None)]
    for level in range(levels):
        for entry, distance in ((level, 1 << level), (levels + level, -(1 << level))):
            route = [(i, i + distance) for i in range(frames) if 0 <= i + distance < frames]
            start = lists[jnp.clip(me + distance, 0, frames - 1), entry] * TILE
            both = [lax.dynamic_slice_in_dim(a, start, TILE, 0) for a in (key_heads, value_heads)]
            both = send(jnp.concatenate(both, axis=0), route)

            def usable(meta, distance=distance):
                return (meta[0] >= distance) & (meta[0] - distance < frames)

            sources.append(([(both, TILE, fixed(0), 0)], [(both, TILE, fixed(1), 0)], usable))
    return attend(queries, meta, sources, 0, width // (2 * HD), 2, final=True)


def body_planes(queries, key_heads, value_heads, tile_lists):
    frames = 16
    rows, width = key_heads.shape
    tile_count = rows // TILE
    heads = 4
    block = heads * HD
    parts = ((0, 2), (2, 1))
    every = range(frames)
    beside = [(i, i ^ 1) for i in every]
    across = [(i, i ^ 2) for i in every]
    corner_in = [(i, i ^ 3 if i % 4 in (1, 2) else i) for i in every]
    corner_out = [(i, i ^ 3 if i % 4 in (0, 3) else i) for i in every]
    outer = [(i, i ^ 4) for i in every]
    inner = [(i, i ^ 12 if i // 4 in (1, 2) else i) for i in every]
    far = [(i, i + (8, -4, 4, -8)[i // 4]) for i in every]

    def right(meta):
        return meta[8] % 4 >= 2

    def two_there(meta):
        return jnp.where(right(meta), meta[8] + 2 < frames, meta[8] >= 2)

    def one_there(meta):
        return (meta[8] >= 1) & (meta[8] < frames - 1)

    def outer_tile(meta):
        return jnp.where(meta[8] // 4 % 2 == 1, meta[2], meta[6])

    def inner_tile(meta):
        return jnp.where(meta[8] // 4 % 2 == 1, meta[6], meta[2])

    def inner_there(meta):
        return (meta[8] >= 4) & (meta[8] < frames - 4)

    def own_frame():
        return [(key_heads, rows, fixed(0), 0)], [(value_heads, rows, fixed(0), 0)], None

    def tile_of(array, tile, usable=None):
        return [(array, TILE, tile, 0)], [(array, TILE, lambda meta: tile(meta) + tile_count, 0)], usable

    def sent_tile(arrays, usable=None):
        return (
            [(a, TILE, fixed(0), column) for a, column in arrays],
            [(a, TILE, fixed(1), column) for a, column in arrays],
            usable,
        )

    me = lax.axis_index("frame").astype(jnp.int32).reshape(1)
    across_list = send(tile_lists, across)
    beside_list = send(tile_lists, beside)
    corner_list = send(across_list, beside)
    first_width = parts[0][1] * block
    meta, first, to_across = begin(tile_lists, me, across_list, key_heads, value_heads, first_width)
    over = send(to_across, across)
    corner_tile, listing, to_beside, to_corner = choose_near(
        meta, tile_lists, beside_list, corner_list, key_heads, value_heads
    )
    far_list = send(listing, [(j, i) for i, j in far])
    next_to = send(to_beside, beside)
    one_in = send(to_corner, corner_in)
    second = pack(key_heads, value_heads, first_width, width - first_width, [to_beside])
    near = [own_frame(), sent_tile([(next_to, 0)]), sent_tile([(over, 0)])]
    begun = attend(queries, meta, near, 0, width // block, heads)

    after = [begun[0], one_in]
    middles, finals = [], []
    for (at, steps), packed in zip(parts, (first, second)):
        from_outer = send(packed, outer)
        from_inner = send(packed, inner)
        to_two, to_one, to_far = choose(
            meta, corner_tile, far_list, key_heads, value_heads, at * block, from_outer, from_inner, after
        )
        two = send(to_two, across)
        one = send(to_one, corner_out)
        from_far = send(to_far, far)
        middle = attend(
            queries,
            meta,
            [
                tile_of(from_outer, outer_tile),
                tile_of(from_inner, inner_tile, inner_there),
            ],
            at,
            steps,
            heads,
            begun,
            held=at,
        )
        after = [middle[0]]
        middles.append(middle)
        finals.append(
            [
                sent_tile([(two, 0)], two_there),
                sent_tile([(one_in, at), (one, 0)], one_there),
                sent_tile([(from_far, 0)]),
            ]
        )
    out = None
    for (at, steps), sources, middle in zip(parts, finals, middles):
        out = attend(queries, meta, sources, at, steps, heads, middle, True, out)
    return out


def solution(mesh):
    body = body_planes if mesh.shape["frame"] == 16 else body_direct
    in_specs = (
        P(("groups", "frame"), None),
        P(("groups", "frame"), None),
        P(("groups", "frame"), None),
        P("frame", None),
    )
    out_specs = P(("groups", "frame"), None)
    return jax.shard_map(body, mesh=mesh, in_specs=in_specs, out_specs=out_specs, check_vma=False)
```

```python
import functools
import math

import jax
import jax.numpy as jnp
from jax import lax
from jax.experimental import pallas as pl
from jax.experimental.pallas import tpu as pltpu
from jax.sharding import PartitionSpec as P

HD = 128
TILE = 128
LOG2_SCALE = math.log2(math.e) / math.sqrt(HD)
VMEM_LIMIT = 24 * 1024 * 1024


def attend_kernel(plan, heads, carry_in, final, meta, *refs):
    refs = list(refs)
    q_ref = refs.pop(0)
    sources = []
    for parts, usable in plan:
        k_refs = [refs.pop(0) for _ in range(parts)]
        v_refs = [refs.pop(0) for _ in range(parts)]
        bias = None
        if usable is not None:
            bias = jnp.where(usable(meta), 0.0, -jnp.inf).astype(jnp.float32)
        sources.append((k_refs, v_refs, bias))
    if carry_in:
        acc_in, sum_in, max_in = refs.pop(0), refs.pop(0), refs.pop(0)
    outs = refs[-1:] if final else refs[-3:]
    rows = q_ref.shape[0]

    def load(some, cols):
        total = some[0][:, cols]
        for other in some[1:]:
            total = total + other[:, cols]
        return total

    groups = [[s] for s in sources if s[0][0].shape[0] > TILE]
    narrow = [s for s in sources if s[0][0].shape[0] == TILE]
    groups += [narrow[at : at + 2] for at in range(0, len(narrow), 2)]

    def columns(head):
        return slice(head * HD, (head + 1) * HD)

    def scores_of(head):
        cols = columns(head)
        scores = []
        for group in groups:
            key = jnp.concatenate([load(k, cols) for k, _, _ in group], axis=0)
            part = lax.dot_general(
                q_ref[:, cols], key, (((1,), (1,)), ((), ())), preferred_element_type=jnp.float32
            )
            pieces = []
            at = 0
            for k, _, bias in group:
                for _ in range(k[0].shape[0] // TILE):
                    piece = part[:, at : at + TILE] * LOG2_SCALE
                    pieces.append(piece if bias is None else piece + bias)
                    at += TILE
            scores.append(pieces)
        return scores

    def weigh(head, scores):
        peak = functools.reduce(jnp.maximum, [piece for pieces in scores for piece in pieces])
        peak = jnp.broadcast_to(jnp.max(peak, axis=1, keepdims=True), (rows, HD))
        if carry_in:
            peak = jnp.maximum(max_in[:, columns(head)], peak)
        weights = [
            jnp.concatenate([jnp.exp2(piece - peak).astype(jnp.bfloat16) for piece in pieces], axis=1)
            for pieces in scores
        ]
        return peak, weights

    def add_up(head, peak, weights):
        cols = columns(head)
        acc = total = None
        if carry_in:
            shrink = jnp.exp2(max_in[:, cols] - peak)
            acc = acc_in[:, cols] * shrink
            total = sum_in[:, cols] * shrink
        for group, weight in zip(groups, weights):
            value = jnp.concatenate([load(v, cols) for _, v, _ in group], axis=0)
            both = jnp.concatenate([value, jnp.ones_like(value)], axis=1)
            added = jnp.dot(weight, both, preferred_element_type=jnp.float32)
            acc = added[:, :HD] if acc is None else acc + added[:, :HD]
            total = added[:, HD:] if total is None else total + added[:, HD:]
        if final:
            outs[0][:, cols] = (acc / total).astype(jnp.bfloat16)
        else:
            outs[0][:, cols] = acc
            outs[1][:, cols] = total
            outs[2][:, cols] = peak

    scores = scores_of(0)
    last = None
    for head in range(heads):
        following = scores_of(head + 1) if head + 1 < heads else None
        weighed = weigh(head, scores)
        if last is not None:
            add_up(*last)
        last = (head, *weighed)
        scores = following
    add_up(*last)


def attend(queries, meta, sources, first, steps, heads, carry=None, final=False, into=None, held=0):
    rows, width = queries.shape
    block = heads * HD

    def spec(count, row, column):
        return pl.BlockSpec((count, block), lambda step, meta: (row(meta), column + step))

    def zero(meta):
        return 0

    operands, specs = [queries], [spec(rows, zero, first)]
    plan, keys_seen = [], 0
    for keys, values, usable in sources:
        for array, count, row, column in list(keys) + list(values):
            operands.append(array)
            specs.append(spec(count, row, column))
        keys_seen += keys[0][1]
        plan.append((len(keys), usable))
    if carry is not None:
        operands += list(carry)
        specs += [spec(rows, zero, held)] * 3
    aliases = {}
    if final:
        out_shape = jax.ShapeDtypeStruct((rows, width), jnp.bfloat16)
        out_specs = spec(rows, zero, first)
        if into is not None:
            aliases = {len(operands) + 1: 0}
            operands.append(into)
            specs.append(pl.BlockSpec(memory_space=pl.ANY))
    else:
        out_shape = [jax.ShapeDtypeStruct((rows, steps * block), jnp.float32)] * 3
        out_specs = [spec(rows, zero, 0)] * 3
    done = steps * block
    return pl.pallas_call(
        functools.partial(attend_kernel, plan, heads, carry is not None, final),
        name="attend_last" if final else "attend_more" if carry is not None else "attend_own",
        out_shape=out_shape,
        grid_spec=pltpu.PrefetchScalarGridSpec(
            num_scalar_prefetch=1, grid=(steps,), in_specs=specs, out_specs=out_specs
        ),
        input_output_aliases=aliases,
        compiler_params=pltpu.CompilerParams(vmem_limit_bytes=VMEM_LIMIT),
        cost_estimate=pl.CostEstimate(
            flops=4 * rows * keys_seen * done,
            bytes_accessed=4 * keys_seen * done + 2 * rows * done,
            transcendentals=rows * keys_seen * (done // HD),
        ),
    )(meta, *operands)


SCALAR = pl.BlockSpec(memory_space=pltpu.SMEM)
WHOLE = pl.BlockSpec(memory_space=pl.ANY)


def move(name, build, operands, specs, out_shape, out_specs, copies, moved, scratch=()):
    return pl.pallas_call(
        build,
        name=name,
        out_shape=out_shape,
        in_specs=specs,
        out_specs=out_specs,
        scratch_shapes=[*scratch, pltpu.SemaphoreType.DMA((copies,))],
        compiler_params=pltpu.CompilerParams(vmem_limit_bytes=VMEM_LIMIT),
        cost_estimate=pl.CostEstimate(flops=0, bytes_accessed=moved, transcendentals=0),
    )(*operands)


def in_hbm(array):
    return pltpu.with_memory_space_constraint(array, pltpu.HBM)


def tile_copies(sources, tile, target, sems, at):
    return [
        pltpu.make_async_copy(
            ref.at[pl.ds(pl.multiple_of(row + tile * TILE, TILE), TILE), pl.ds(first, target.shape[1])],
            target.at[pl.ds(n * TILE, TILE)],
            sems.at[at + n],
        )
        for n, (ref, row, first) in enumerate(sources)
    ]


def zero_copies(zeros, target, sems, at):
    return [
        pltpu.make_async_copy(zeros, target.at[pl.ds(n * TILE, TILE)], sems.at[at + n]) for n in (0, 1)
    ]


def start_if(condition, copies):
    @pl.when(condition)
    def _():
        for copy in copies:
            copy.start()


def tile_at(ref, entry, tile_count):
    return jnp.clip(ref[0, entry], 0, tile_count - 1)


def part_copies(k_ref, v_ref, first, width, target, sems, at):
    rows = k_ref.shape[0]
    return [
        pltpu.make_async_copy(
            ref.at[:, pl.ds(first, width)], target.at[pl.ds(n * rows, rows)], sems.at[at + n]
        )
        for n, ref in enumerate((k_ref, v_ref))
    ]


def begin(tile_lists, me, across_list, keys, values, width, after):
    rows, all_width = keys.shape
    tile_count = rows // TILE

    def build(me_ref, across_ref, list_hbm, k_ref, v_ref, *refs):
        meta, packed, to_across, list_ref, sems = refs[-5:]
        read = pltpu.make_async_copy(list_hbm, list_ref, sems.at[4])
        read.start()
        me = me_ref[0]
        right = me % 4 >= 2
        copies = part_copies(k_ref, v_ref, 0, width, packed, sems, 0)
        tile = tile_at(across_ref, jnp.where(right, 5, 1), tile_count)
        copies += tile_copies(((k_ref, 0, 0), (v_ref, 0, 0)), tile, to_across, sems, 2)
        for copy in copies:
            copy.start()
        read.wait()
        for entry in range(8):
            meta[entry] = tile_at(list_ref, entry, tile_count)
        meta[8] = me
        meta[9] = tile_at(across_ref, jnp.where(right, 1, 5), tile_count)
        for copy in copies:
            copy.wait()

    return move(
        "begin",
        build,
        (me, across_list, in_hbm(tile_lists), in_hbm(keys), in_hbm(values), *after),
        [SCALAR] * 2 + [WHOLE] * (3 + len(after)),
        [
            jax.ShapeDtypeStruct((10,), jnp.int32),
            jax.ShapeDtypeStruct((2 * rows, width), jnp.bfloat16),
            jax.ShapeDtypeStruct((2 * TILE, all_width), jnp.bfloat16),
        ],
        [SCALAR, WHOLE, WHOLE],
        5,
        8 * rows * width + 8 * TILE * all_width,
        [pltpu.SMEM(tile_lists.shape, jnp.int32)],
    )


def choose_near(meta, beside_list, corner_list, keys, values):
    rows, width = keys.shape
    tile_count = rows // TILE

    def build(meta, beside_ref, corner_ref, k_ref, v_ref, wanted, to_beside, to_corner, zeros, sems):
        even = meta[8] % 2 == 0
        own = ((k_ref, 0, 0), (v_ref, 0, 0))
        copies = tile_copies(own, tile_at(beside_ref, jnp.where(even, 0, 4), tile_count), to_beside, sems, 0)
        for copy in copies:
            copy.start()
        wanted[0] = tile_at(corner_ref, jnp.where(even, 4, 0), tile_count)
        inside = (meta[8] % 4 == 1) | (meta[8] % 4 == 2)
        start_if(inside, tile_copies(own, wanted[0], to_corner, sems, 2))
        zeros[...] = jnp.zeros_like(zeros)
        blank = zero_copies(zeros, to_corner, sems, 2)
        start_if(jnp.logical_not(inside), blank)
        for copy in copies + blank:
            copy.wait()

    tile = jax.ShapeDtypeStruct((2 * TILE, width), jnp.bfloat16)
    return move(
        "choose_near",
        build,
        (meta, beside_list, corner_list, in_hbm(keys), in_hbm(values)),
        [SCALAR] * 3 + [WHOLE] * 2,
        [jax.ShapeDtypeStruct((1,), jnp.int32), tile, tile],
        [SCALAR, WHOLE, WHOLE],
        4,
        16 * TILE * width,
        [pltpu.VMEM((TILE, width), jnp.bfloat16)],
    )


def pack(keys, values, first, width, after):
    rows = keys.shape[0]

    def build(k_ref, v_ref, *refs):
        out_ref, stage, sems = refs[-3:]
        reads = part_copies(k_ref, v_ref, first, width, stage, sems, 0)
        writes = [
            pltpu.make_async_copy(
                stage.at[pl.ds(n * rows, rows)], out_ref.at[pl.ds(n * rows, rows)], sems.at[2 + n]
            )
            for n in (0, 1)
        ]
        for read in reads:
            read.start()
        for read, write in zip(reads, writes):
            read.wait()
            write.start()
        for write in writes:
            write.wait()

    return move(
        "pack",
        build,
        (in_hbm(keys), in_hbm(values), *after),
        [WHOLE] * (2 + len(after)),
        jax.ShapeDtypeStruct((2 * rows, width), jnp.bfloat16),
        WHOLE,
        4,
        8 * rows * width,
        [pltpu.VMEM((2 * rows, width), jnp.bfloat16)],
    )


def choose(meta, corner_tile, far_list, keys, values, first, outer, inner, after):
    rows, width = keys.shape[0], outer.shape[1]
    tile_count = rows // TILE

    def build(meta, corner_ref, far_ref, k_ref, v_ref, outer, inner, *refs):
        to_two, to_one, to_far, zeros, sems = refs[-5:]
        spot, plane = meta[8] % 4, meta[8] // 4
        right, odd = spot >= 2, plane % 2 == 1
        edge = (spot == 0) | (spot == 3)
        between = (plane == 1) | (plane == 2)
        own = ((k_ref, 0, first), (v_ref, 0, first))
        from_outer = ((outer, 0, 0), (outer, rows, 0))
        from_inner = ((inner, 0, 0), (inner, rows, 0))
        for source, here in ((from_outer, right == odd), (from_inner, right != odd)):
            start_if(here, tile_copies(source, meta[9], to_two, sems, 0))
            start_if(here & edge, tile_copies(source, corner_ref[0], to_one, sems, 2))
        tile = tile_at(far_ref, jnp.where(odd, 7, 3), tile_count)
        start_if(between, tile_copies(from_inner, tile, to_far, sems, 4))
        start_if(jnp.logical_not(between), tile_copies(own, tile, to_far, sems, 4))
        zeros[...] = jnp.zeros_like(zeros)
        start_if(jnp.logical_not(edge), zero_copies(zeros, to_one, sems, 2))
        for n, target in enumerate((to_two, to_one, to_far)):
            for copy in zero_copies(zeros, target, sems, 2 * n):
                copy.wait()

    return move(
        "choose",
        build,
        (meta, corner_tile, far_list, in_hbm(keys), in_hbm(values), outer, inner, *after),
        [SCALAR] * 3 + [WHOLE] * (4 + len(after)),
        [jax.ShapeDtypeStruct((2 * TILE, width), jnp.bfloat16)] * 3,
        [WHOLE] * 3,
        6,
        24 * TILE * width,
        [pltpu.VMEM((TILE, width), jnp.bfloat16)],
    )


def send(array, route):
    return lax.ppermute(array, "frame", route)


def fixed(block):
    return lambda meta: block


def body_direct(queries, key_heads, value_heads, tile_lists):
    frames = lax.axis_size("frame")
    levels = frames.bit_length() - 1
    rows, width = key_heads.shape
    me = lax.axis_index("frame")
    lists = jnp.clip(lax.all_gather(tile_lists, "frame", tiled=True), 0, rows // TILE - 1)
    meta = me.astype(jnp.int32).reshape(1)
    sources = [([(key_heads, rows, fixed(0), 0)], [(value_heads, rows, fixed(0), 0)], None)]
    for level in range(levels):
        for entry, distance in ((level, 1 << level), (levels + level, -(1 << level))):
            route = [(i, i + distance) for i in range(frames) if 0 <= i + distance < frames]
            start = lists[jnp.clip(me + distance, 0, frames - 1), entry] * TILE
            both = [lax.dynamic_slice_in_dim(a, start, TILE, 0) for a in (key_heads, value_heads)]
            both = send(jnp.concatenate(both, axis=0), route)

            def usable(meta, distance=distance):
                return (meta[0] >= distance) & (meta[0] - distance < frames)

            sources.append(([(both, TILE, fixed(0), 0)], [(both, TILE, fixed(1), 0)], usable))
    return attend(queries, meta, sources, 0, width // (2 * HD), 2, final=True)


def body_planes(queries, key_heads, value_heads, tile_lists):
    frames = 16
    rows, width = key_heads.shape
    tile_count = rows // TILE
    heads = 4
    block = heads * HD
    parts = ((0, 2), (2, 1))
    every = range(frames)
    beside = [(i, i ^ 1) for i in every]
    across = [(i, i ^ 2) for i in every]
    corner_in = [(i, i ^ 3 if i % 4 in (1, 2) else i) for i in every]
    corner_out = [(i, i ^ 3 if i % 4 in (0, 3) else i) for i in every]
    outer = [(i, i ^ 4) for i in every]
    inner = [(i, i ^ 12 if i // 4 in (1, 2) else i) for i in every]
    far = [(i, i + (8, -4, 4, -8)[i // 4]) for i in every]

    def right(meta):
        return meta[8] % 4 >= 2

    def two_there(meta):
        return jnp.where(right(meta), meta[8] + 2 < frames, meta[8] >= 2)

    def one_there(meta):
        return (meta[8] >= 1) & (meta[8] < frames - 1)

    def outer_tile(meta):
        return jnp.where(meta[8] // 4 % 2 == 1, meta[2], meta[6])

    def inner_tile(meta):
        return jnp.where(meta[8] // 4 % 2 == 1, meta[6], meta[2])

    def inner_there(meta):
        return (meta[8] >= 4) & (meta[8] < frames - 4)

    def own_frame():
        return [(key_heads, rows, fixed(0), 0)], [(value_heads, rows, fixed(0), 0)], None

    def tile_of(array, tile, usable=None):
        return [(array, TILE, tile, 0)], [(array, TILE, lambda meta: tile(meta) + tile_count, 0)], usable

    def sent_tile(arrays, usable=None):
        return (
            [(a, TILE, fixed(0), column) for a, column in arrays],
            [(a, TILE, fixed(1), column) for a, column in arrays],
            usable,
        )

    me = lax.axis_index("frame").astype(jnp.int32).reshape(1)
    across_list = send(tile_lists, across)
    far_list = send(tile_lists, [(j, i) for i, j in far])
    beside_list = send(tile_lists, beside)
    corner_list = send(across_list, beside)
    first_width = parts[0][1] * block
    meta, first, to_across = begin(tile_lists, me, across_list, key_heads, value_heads, first_width, [far_list])
    over = send(to_across, across)
    corner_tile, to_beside, to_corner = choose_near(meta, beside_list, corner_list, key_heads, value_heads)
    next_to = send(to_beside, beside)
    one_in = send(to_corner, corner_in)
    second = pack(key_heads, value_heads, first_width, width - first_width, [over])
    near = [own_frame(), sent_tile([(next_to, 0)]), sent_tile([(over, 0)])]
    begun = attend(queries, meta, near, 0, width // block, heads)

    after = [begun[0]]
    middles, finals = [], []
    for (at, steps), packed in zip(parts, (first, second)):
        from_outer = send(packed, outer)
        from_inner = send(packed, inner)
        to_two, to_one, to_far = choose(
            meta, corner_tile, far_list, key_heads, value_heads, at * block, from_outer, from_inner, after
        )
        two = send(to_two, across)
        one = send(to_one, corner_out)
        from_far = send(to_far, far)
        middle = attend(
            queries,
            meta,
            [
                tile_of(from_outer, outer_tile),
                tile_of(from_inner, inner_tile, inner_there),
            ],
            at,
            steps,
            heads,
            begun,
            held=at,
        )
        after = [middle[0]]
        middles.append(middle)
        finals.append(
            [
                sent_tile([(two, 0)], two_there),
                sent_tile([(one_in, at), (one, 0)], one_there),
                sent_tile([(from_far, 0)]),
            ]
        )
    out = None
    for (at, steps), sources, middle in zip(parts, finals, middles):
        out = attend(queries, meta, sources, at, steps, heads, middle, True, out)
    return out


def solution(mesh):
    body = body_planes if mesh.shape["frame"] == 16 else body_direct
    in_specs = (
        P(("groups", "frame"), None),
        P(("groups", "frame"), None),
        P(("groups", "frame"), None),
        P("frame", None),
    )
    out_specs = P(("groups", "frame"), None)
    return jax.shard_map(body, mesh=mesh, in_specs=in_specs, out_specs=out_specs, check_vma=False)
```

```python
import functools
import math

import jax
import jax.numpy as jnp
from jax import lax
from jax.experimental import pallas as pl
from jax.experimental.pallas import tpu as pltpu
from jax.sharding import PartitionSpec as P

HD = 128
TILE = 128
NOTE_ROWS = 16
LOG2_SCALE = math.log2(math.e) / math.sqrt(HD)
VMEM_LIMIT = 24 * 1024 * 1024


def attend_kernel(plan, heads, carry_in, final, meta, *refs):
    refs = list(refs)
    q_ref = refs.pop(0)
    sources = []
    for parts, usable in plan:
        k_refs = [refs.pop(0) for _ in range(parts)]
        v_refs = [refs.pop(0) for _ in range(parts)]
        bias = None
        if usable is not None:
            bias = jnp.where(usable(meta), 0.0, -jnp.inf).astype(jnp.float32)
        sources.append((k_refs, v_refs, bias))
    if carry_in:
        acc_in, sum_in, max_in = refs.pop(0), refs.pop(0), refs.pop(0)
    outs = refs[-1:] if final else refs[-3:]
    rows = q_ref.shape[0]

    def load(some, cols):
        total = some[0][:, cols]
        for other in some[1:]:
            total = total + other[:, cols]
        return total

    groups = [[s] for s in sources if s[0][0].shape[0] > TILE]
    narrow = [s for s in sources if s[0][0].shape[0] == TILE]
    groups += [narrow[at : at + 2] for at in range(0, len(narrow), 2)]

    def columns(head):
        return slice(head * HD, (head + 1) * HD)

    def scores_of(head):
        cols = columns(head)
        scores = []
        for group in groups:
            key = jnp.concatenate([load(k, cols) for k, _, _ in group], axis=0)
            part = lax.dot_general(
                q_ref[:, cols], key, (((1,), (1,)), ((), ())), preferred_element_type=jnp.float32
            )
            pieces = []
            at = 0
            for k, _, bias in group:
                for _ in range(k[0].shape[0] // TILE):
                    piece = part[:, at : at + TILE] * LOG2_SCALE
                    pieces.append(piece if bias is None else piece + bias)
                    at += TILE
            scores.append(pieces)
        return scores

    def weigh(head, scores):
        peak = functools.reduce(jnp.maximum, [piece for pieces in scores for piece in pieces])
        peak = jnp.broadcast_to(jnp.max(peak, axis=1, keepdims=True), (rows, HD))
        if carry_in:
            peak = jnp.maximum(max_in[:, columns(head)], peak)
        weights = [
            jnp.concatenate([jnp.exp2(piece - peak).astype(jnp.bfloat16) for piece in pieces], axis=1)
            for pieces in scores
        ]
        return peak, weights

    def add_up(head, peak, weights):
        cols = columns(head)
        acc = total = None
        if carry_in:
            shrink = jnp.exp2(max_in[:, cols] - peak)
            acc = acc_in[:, cols] * shrink
            total = sum_in[:, cols] * shrink
        for group, weight in zip(groups, weights):
            value = jnp.concatenate([load(v, cols) for _, v, _ in group], axis=0)
            both = jnp.concatenate([value, jnp.ones_like(value)], axis=1)
            added = jnp.dot(weight, both, preferred_element_type=jnp.float32)
            acc = added[:, :HD] if acc is None else acc + added[:, :HD]
            total = added[:, HD:] if total is None else total + added[:, HD:]
        if final:
            outs[0][:, cols] = (acc / total).astype(jnp.bfloat16)
        else:
            outs[0][:, cols] = acc
            outs[1][:, cols] = total
            outs[2][:, cols] = peak

    scores = scores_of(0)
    last = None
    for head in range(heads):
        following = scores_of(head + 1) if head + 1 < heads else None
        weighed = weigh(head, scores)
        if last is not None:
            add_up(*last)
        last = (head, *weighed)
        scores = following
    add_up(*last)


def attend(queries, meta, sources, first, steps, heads, carry=None, final=False, into=None, held=0):
    rows, width = queries.shape
    block = heads * HD

    def spec(count, row, column):
        return pl.BlockSpec((count, block), lambda step, meta: (row(meta), column + step))

    def zero(meta):
        return 0

    operands, specs = [queries], [spec(rows, zero, first)]
    plan, keys_seen = [], 0
    for keys, values, usable in sources:
        for array, count, row, column in list(keys) + list(values):
            operands.append(array)
            specs.append(spec(count, row, column))
        keys_seen += keys[0][1]
        plan.append((len(keys), usable))
    if carry is not None:
        operands += list(carry)
        specs += [spec(rows, zero, held)] * 3
    aliases = {}
    if final:
        out_shape = jax.ShapeDtypeStruct((rows, width), jnp.bfloat16)
        out_specs = spec(rows, zero, first)
        if into is not None:
            aliases = {len(operands) + 1: 0}
            operands.append(into)
            specs.append(pl.BlockSpec(memory_space=pl.ANY))
    else:
        out_shape = [jax.ShapeDtypeStruct((rows, steps * block), jnp.float32)] * 3
        out_specs = [spec(rows, zero, 0)] * 3
    done = steps * block
    return pl.pallas_call(
        functools.partial(attend_kernel, plan, heads, carry is not None, final),
        name="attend_last" if final else "attend_more" if carry is not None else "attend_own",
        out_shape=out_shape,
        grid_spec=pltpu.PrefetchScalarGridSpec(
            num_scalar_prefetch=1, grid=(steps,), in_specs=specs, out_specs=out_specs
        ),
        input_output_aliases=aliases,
        compiler_params=pltpu.CompilerParams(vmem_limit_bytes=VMEM_LIMIT),
        cost_estimate=pl.CostEstimate(
            flops=4 * rows * keys_seen * done,
            bytes_accessed=4 * keys_seen * done + 2 * rows * done,
            transcendentals=rows * keys_seen * (done // HD),
        ),
    )(meta, *operands)


SCALAR = pl.BlockSpec(memory_space=pltpu.SMEM)
WHOLE = pl.BlockSpec(memory_space=pl.ANY)


def move(name, build, operands, specs, out_shape, out_specs, copies, moved, scratch=()):
    return pl.pallas_call(
        build,
        name=name,
        out_shape=out_shape,
        in_specs=specs,
        out_specs=out_specs,
        scratch_shapes=[*scratch, pltpu.SemaphoreType.DMA((copies,))],
        compiler_params=pltpu.CompilerParams(vmem_limit_bytes=VMEM_LIMIT),
        cost_estimate=pl.CostEstimate(flops=0, bytes_accessed=moved, transcendentals=0),
    )(*operands)


def in_hbm(array):
    return pltpu.with_memory_space_constraint(array, pltpu.HBM)


def tile_copies(sources, tile, target, sems, at):
    return [
        pltpu.make_async_copy(
            ref.at[pl.ds(pl.multiple_of(row + tile * TILE, TILE), TILE), pl.ds(first, target.shape[1])],
            target.at[pl.ds(n * TILE, TILE)],
            sems.at[at + n],
        )
        for n, (ref, row, first) in enumerate(sources)
    ]


def zero_copies(zeros, target, sems, at):
    return [
        pltpu.make_async_copy(zeros, target.at[pl.ds(n * TILE, TILE)], sems.at[at + n]) for n in (0, 1)
    ]


def start_if(condition, copies):
    @pl.when(condition)
    def _():
        for copy in copies:
            copy.start()


def tile_at(ref, entry, tile_count):
    return jnp.clip(ref[0, entry], 0, tile_count - 1)


def write_note(note, ref, tile_count):
    lane = lax.broadcasted_iota(jnp.int32, note.shape, 1)
    row = jnp.zeros(note.shape, jnp.float32)
    for entry in range(8):
        row = jnp.where(lane == entry, tile_at(ref, entry, tile_count).astype(jnp.float32), row)
    note[...] = row.astype(jnp.bfloat16)


def read_note(note, entry, tile_count):
    here = (lax.broadcasted_iota(jnp.int32, note.shape, 1) == entry) & (
        lax.broadcasted_iota(jnp.int32, note.shape, 0) == 0
    )
    value = jnp.sum(jnp.where(here, note.astype(jnp.float32), 0.0))
    return jnp.clip(value.astype(jnp.int32), 0, tile_count - 1)


def part_copies(k_ref, v_ref, first, width, target, sems, at):
    rows = k_ref.shape[0]
    return [
        pltpu.make_async_copy(
            ref.at[:, pl.ds(first, width)], target.at[pl.ds(n * rows, rows)], sems.at[at + n]
        )
        for n, ref in enumerate((k_ref, v_ref))
    ]


def begin(tile_lists, me, across_list, keys, values, width):
    rows, all_width = keys.shape
    tile_count = rows // TILE

    def build(me_ref, across_ref, list_hbm, k_ref, v_ref, meta, packed, to_across, list_ref, note, sems):
        read = pltpu.make_async_copy(list_hbm, list_ref, sems.at[5])
        read.start()
        me = me_ref[0]
        right = me % 4 >= 2
        copies = part_copies(k_ref, v_ref, 0, width, packed, sems, 0)
        tile = tile_at(across_ref, jnp.where(right, 5, 1), tile_count)
        copies += tile_copies(((k_ref, 0, 0), (v_ref, 0, 0)), tile, to_across, sems, 2)
        for copy in copies:
            copy.start()
        read.wait()
        write_note(note, list_ref, tile_count)
        last = pltpu.make_async_copy(
            note, packed.at[pl.ds(2 * rows, NOTE_ROWS), pl.ds(0, HD)], sems.at[4]
        )
        last.start()
        for entry in range(8):
            meta[entry] = tile_at(list_ref, entry, tile_count)
        meta[8] = me
        meta[9] = tile_at(across_ref, jnp.where(right, 1, 5), tile_count)
        for copy in copies + [last]:
            copy.wait()

    return move(
        "begin",
        build,
        (me, across_list, in_hbm(tile_lists), in_hbm(keys), in_hbm(values)),
        [SCALAR] * 2 + [WHOLE] * 3,
        [
            jax.ShapeDtypeStruct((10,), jnp.int32),
            jax.ShapeDtypeStruct((2 * rows + NOTE_ROWS, width), jnp.bfloat16),
            jax.ShapeDtypeStruct((2 * TILE, all_width), jnp.bfloat16),
        ],
        [SCALAR, WHOLE, WHOLE],
        6,
        8 * rows * width + 8 * TILE * all_width,
        [pltpu.SMEM(tile_lists.shape, jnp.int32), pltpu.VMEM((NOTE_ROWS, HD), jnp.bfloat16)],
    )


def choose_near(meta, beside_list, corner_list, keys, values):
    rows, width = keys.shape
    tile_count = rows // TILE

    def build(meta, beside_ref, corner_ref, k_ref, v_ref, wanted, to_beside, to_corner, zeros, sems):
        even = meta[8] % 2 == 0
        own = ((k_ref, 0, 0), (v_ref, 0, 0))
        copies = tile_copies(own, tile_at(beside_ref, jnp.where(even, 0, 4), tile_count), to_beside, sems, 0)
        for copy in copies:
            copy.start()
        wanted[0] = tile_at(corner_ref, jnp.where(even, 4, 0), tile_count)
        inside = (meta[8] % 4 == 1) | (meta[8] % 4 == 2)
        start_if(inside, tile_copies(own, wanted[0], to_corner, sems, 2))
        zeros[...] = jnp.zeros_like(zeros)
        blank = zero_copies(zeros, to_corner, sems, 2)
        start_if(jnp.logical_not(inside), blank)
        for copy in copies + blank:
            copy.wait()

    tile = jax.ShapeDtypeStruct((2 * TILE, width), jnp.bfloat16)
    return move(
        "choose_near",
        build,
        (meta, beside_list, corner_list, in_hbm(keys), in_hbm(values)),
        [SCALAR] * 3 + [WHOLE] * 2,
        [jax.ShapeDtypeStruct((1,), jnp.int32), tile, tile],
        [SCALAR, WHOLE, WHOLE],
        4,
        16 * TILE * width,
        [pltpu.VMEM((TILE, width), jnp.bfloat16)],
    )


def pack(keys, values, first, width, after):
    rows = keys.shape[0]

    def build(k_ref, v_ref, *refs):
        out_ref, stage, sems = refs[-3:]
        reads = part_copies(k_ref, v_ref, first, width, stage, sems, 0)
        writes = [
            pltpu.make_async_copy(
                stage.at[pl.ds(n * rows, rows)], out_ref.at[pl.ds(n * rows, rows)], sems.at[2 + n]
            )
            for n in (0, 1)
        ]
        for read in reads:
            read.start()
        for read, write in zip(reads, writes):
            read.wait()
            write.start()
        for write in writes:
            write.wait()

    return move(
        "pack",
        build,
        (in_hbm(keys), in_hbm(values), *after),
        [WHOLE] * (2 + len(after)),
        jax.ShapeDtypeStruct((2 * rows, width), jnp.bfloat16),
        WHOLE,
        4,
        8 * rows * width,
        [pltpu.VMEM((2 * rows, width), jnp.bfloat16)],
    )


def choose(meta, corner_tile, wants, outer, inner, after):
    rows, width = outer.shape[0] // 2 // TILE * TILE, outer.shape[1]
    tile_count = rows // TILE
    again = wants is not None

    def build(meta, corner_ref, *refs):
        if again:
            wants, outer, inner = refs[:3]
            to_two, to_one, to_outer, to_inner = refs[-6:-2]
        else:
            outer, inner, wants = refs[:2] + refs[-8:-7]
            to_two, to_one, to_outer, to_inner, notes = refs[-7:-2]
        zeros, sems = refs[-2:]
        spot, plane = meta[8] % 4, meta[8] // 4
        right, odd = spot >= 2, plane % 2 == 1
        from_outer = ((outer, 0, 0), (outer, rows, 0))
        from_inner = ((inner, 0, 0), (inner, rows, 0))
        if not again:
            reads = [
                pltpu.make_async_copy(
                    ref.at[pl.ds(2 * rows, NOTE_ROWS), pl.ds(0, HD)], notes.at[n], sems.at[8 + n]
                )
                for n, ref in enumerate((outer, inner))
            ]
            for read in reads:
                read.start()
        edge = (spot == 0) | (spot == 3)
        for source, here in ((from_outer, right == odd), (from_inner, right != odd)):
            start_if(here, tile_copies(source, meta[9], to_two, sems, 0))
            start_if(here & edge, tile_copies(source, corner_ref[0], to_one, sems, 2))
        zeros[...] = jnp.zeros_like(zeros)
        start_if(jnp.logical_not(edge), zero_copies(zeros, to_one, sems, 2))
        between = (plane == 1) | (plane == 2)
        start_if(
            jnp.logical_not(between),
            zero_copies(zeros, to_outer, sems, 4) + zero_copies(zeros, to_inner, sems, 6),
        )
        if not again:
            for read in reads:
                read.wait()
            wants[0] = read_note(notes[0], jnp.where(plane == 1, 7, 3), tile_count)
            wants[1] = read_note(notes[1], jnp.where(plane == 1, 3, 7), tile_count)
        start_if(
            between,
            tile_copies(from_inner, wants[0], to_outer, sems, 4)
            + tile_copies(from_outer, wants[1], to_inner, sems, 6),
        )
        for n, target in enumerate((to_two, to_one, to_outer, to_inner)):
            for copy in tile_copies(from_outer, 0, target, sems, 2 * n):
                copy.wait()

    sent = [jax.ShapeDtypeStruct((2 * TILE, width), jnp.bfloat16)] * 4
    return move(
        "choose_again" if again else "choose",
        build,
        (meta, corner_tile, *([wants] if again else []), outer, inner, *after),
        [SCALAR] * (2 + again) + [WHOLE] * (2 + len(after)),
        ([] if again else [jax.ShapeDtypeStruct((2,), jnp.int32)]) + sent,
        [SCALAR] * (not again) + [WHOLE] * 4,
        10,
        32 * TILE * width,
        ([] if again else [pltpu.VMEM((2, NOTE_ROWS, HD), jnp.bfloat16)])
        + [pltpu.VMEM((TILE, width), jnp.bfloat16)],
    )


def send(array, route):
    return lax.ppermute(array, "frame", route)


def fixed(block):
    return lambda meta: block


def body_direct(queries, key_heads, value_heads, tile_lists):
    frames = lax.axis_size("frame")
    levels = frames.bit_length() - 1
    rows, width = key_heads.shape
    me = lax.axis_index("frame")
    lists = jnp.clip(lax.all_gather(tile_lists, "frame", tiled=True), 0, rows // TILE - 1)
    meta = me.astype(jnp.int32).reshape(1)
    sources = [([(key_heads, rows, fixed(0), 0)], [(value_heads, rows, fixed(0), 0)], None)]
    for level in range(levels):
        for entry, distance in ((level, 1 << level), (levels + level, -(1 << level))):
            route = [(i, i + distance) for i in range(frames) if 0 <= i + distance < frames]
            start = lists[jnp.clip(me + distance, 0, frames - 1), entry] * TILE
            both = [lax.dynamic_slice_in_dim(a, start, TILE, 0) for a in (key_heads, value_heads)]
            both = send(jnp.concatenate(both, axis=0), route)

            def usable(meta, distance=distance):
                return (meta[0] >= distance) & (meta[0] - distance < frames)

            sources.append(([(both, TILE, fixed(0), 0)], [(both, TILE, fixed(1), 0)], usable))
    return attend(queries, meta, sources, 0, width // (2 * HD), 2, final=True)


def body_planes(queries, key_heads, value_heads, tile_lists):
    frames = 16
    rows, width = key_heads.shape
    tile_count = rows // TILE
    heads = 4
    block = heads * HD
    parts = ((0, 2), (2, 1))
    every = range(frames)
    beside = [(i, i ^ 1) for i in every]
    across = [(i, i ^ 2) for i in every]
    corner_in = [(i, i ^ 3 if i % 4 in (1, 2) else i) for i in every]
    corner_out = [(i, i ^ 3 if i % 4 in (0, 3) else i) for i in every]
    outer = [(i, i ^ 4) for i in every]
    inner = [(i, i ^ 12 if i // 4 in (1, 2) else i) for i in every]

    def right(meta):
        return meta[8] % 4 >= 2

    def two_there(meta):
        return jnp.where(right(meta), meta[8] + 2 < frames, meta[8] >= 2)

    def one_there(meta):
        return (meta[8] >= 1) & (meta[8] < frames - 1)

    def outer_tile(meta):
        return jnp.where(meta[8] // 4 % 2 == 1, meta[2], meta[6])

    def inner_tile(meta):
        return jnp.where(meta[8] // 4 % 2 == 1, meta[6], meta[2])

    def inner_there(meta):
        return (meta[8] >= 4) & (meta[8] < frames - 4)

    def own_frame():
        return [(key_heads, rows, fixed(0), 0)], [(value_heads, rows, fixed(0), 0)], None

    def tile_of(array, tile, usable=None):
        return [(array, TILE, tile, 0)], [(array, TILE, lambda meta: tile(meta) + tile_count, 0)], usable

    def sent_tile(arrays, usable=None):
        return (
            [(a, TILE, fixed(0), column) for a, column in arrays],
            [(a, TILE, fixed(1), column) for a, column in arrays],
            usable,
        )

    me = lax.axis_index("frame").astype(jnp.int32).reshape(1)
    across_list = send(tile_lists, across)
    beside_list = send(tile_lists, beside)
    corner_list = send(across_list, beside)
    first_width = parts[0][1] * block
    meta, first, to_across = begin(tile_lists, me, across_list, key_heads, value_heads, first_width)
    over = send(to_across, across)
    corner_tile, to_beside, to_corner = choose_near(meta, beside_list, corner_list, key_heads, value_heads)
    next_to = send(to_beside, beside)
    one_in = send(to_corner, corner_in)
    second = pack(key_heads, value_heads, first_width, width - first_width, [to_beside])
    near = [own_frame(), sent_tile([(next_to, 0)]), sent_tile([(over, 0)])]
    begun = attend(queries, meta, near, 0, width // block, heads)

    after, wants = [begun[0], one_in], None
    calls = []
    for (at, steps), packed in zip(parts, (first, second)):
        from_outer = send(packed, outer)
        from_inner = send(packed, inner)
        sent = choose(meta, corner_tile, wants, from_outer, from_inner, after)
        if wants is None:
            wants, *sent = sent
        two = send(sent[0], across)
        one = send(sent[1], corner_out)
        far = [send(sent[2], outer), send(sent[3], inner)]
        z_tiles = [tile_of(from_outer, outer_tile), tile_of(from_inner, inner_tile, inner_there)]
        late_tiles = [
            sent_tile([(two, 0)], two_there),
            sent_tile([(one_in, at), (one, 0)], one_there),
            sent_tile([(a, 0) for a in far]),
        ]
        after = []
        calls.append((at, steps, z_tiles, late_tiles))
    at, steps, z_tiles, late_tiles = calls[0]
    out = attend(queries, meta, z_tiles + late_tiles, at, steps, heads, begun, True, held=at)
    at, steps, z_tiles, late_tiles = calls[1]
    middle = attend(queries, meta, z_tiles, at, steps, heads, begun, held=at)
    return attend(queries, meta, late_tiles, at, steps, heads, middle, True, out)


def solution(mesh):
    body = body_planes if mesh.shape["frame"] == 16 else body_direct
    in_specs = (
        P(("groups", "frame"), None),
        P(("groups", "frame"), None),
        P(("groups", "frame"), None),
        P("frame", None),
    )
    out_specs = P(("groups", "frame"), None)
    return jax.shard_map(body, mesh=mesh, in_specs=in_specs, out_specs=out_specs, check_vma=False)
```

```python
import functools
import math

import jax
import jax.numpy as jnp
from jax import lax
from jax.experimental import pallas as pl
from jax.experimental.pallas import tpu as pltpu
from jax.sharding import PartitionSpec as P

HD = 128
TILE = 128
NOTE_ROWS = 16
LOG2_SCALE = math.log2(math.e) / math.sqrt(HD)
VMEM_LIMIT = 24 * 1024 * 1024


def attend_kernel(plan, heads, carry_in, final, meta, *refs):
    refs = list(refs)
    q_ref = refs.pop(0)
    sources = []
    for parts, usable in plan:
        k_refs = [refs.pop(0) for _ in range(parts)]
        v_refs = [refs.pop(0) for _ in range(parts)]
        bias = None
        if usable is not None:
            bias = jnp.where(usable(meta), 0.0, -jnp.inf).astype(jnp.float32)
        sources.append((k_refs, v_refs, bias))
    if carry_in:
        acc_in, sum_in, max_in = refs.pop(0), refs.pop(0), refs.pop(0)
    outs = refs[-1:] if final else refs[-3:]
    rows = q_ref.shape[0]

    def load(some, cols):
        total = some[0][:, cols]
        for other in some[1:]:
            total = total + other[:, cols]
        return total

    groups = [[s] for s in sources if s[0][0].shape[0] > TILE]
    narrow = [s for s in sources if s[0][0].shape[0] == TILE]
    groups += [narrow[at : at + 2] for at in range(0, len(narrow), 2)]

    def columns(head):
        return slice(head * HD, (head + 1) * HD)

    def scores_of(head):
        cols = columns(head)
        scores = []
        for group in groups:
            key = jnp.concatenate([load(k, cols) for k, _, _ in group], axis=0)
            part = lax.dot_general(
                q_ref[:, cols], key, (((1,), (1,)), ((), ())), preferred_element_type=jnp.float32
            )
            pieces = []
            at = 0
            for k, _, bias in group:
                for _ in range(k[0].shape[0] // TILE):
                    piece = part[:, at : at + TILE] * LOG2_SCALE
                    pieces.append(piece if bias is None else piece + bias)
                    at += TILE
            scores.append(pieces)
        return scores

    def weigh(head, scores):
        peak = functools.reduce(jnp.maximum, [piece for pieces in scores for piece in pieces])
        peak = jnp.broadcast_to(jnp.max(peak, axis=1, keepdims=True), (rows, HD))
        if carry_in:
            peak = jnp.maximum(max_in[:, columns(head)], peak)
        weights = [
            jnp.concatenate([jnp.exp2(piece - peak).astype(jnp.bfloat16) for piece in pieces], axis=1)
            for pieces in scores
        ]
        return peak, weights

    def add_up(head, peak, weights):
        cols = columns(head)
        acc = total = None
        if carry_in:
            shrink = jnp.exp2(max_in[:, cols] - peak)
            acc = acc_in[:, cols] * shrink
            total = sum_in[:, cols] * shrink
        for group, weight in zip(groups, weights):
            value = jnp.concatenate([load(v, cols) for _, v, _ in group], axis=0)
            both = jnp.concatenate([value, jnp.ones_like(value)], axis=1)
            added = jnp.dot(weight, both, preferred_element_type=jnp.float32)
            acc = added[:, :HD] if acc is None else acc + added[:, :HD]
            total = added[:, HD:] if total is None else total + added[:, HD:]
        if final:
            outs[0][:, cols] = (acc / total).astype(jnp.bfloat16)
        else:
            outs[0][:, cols] = acc
            outs[1][:, cols] = total
            outs[2][:, cols] = peak

    scores = scores_of(0)
    last = None
    for head in range(heads):
        following = scores_of(head + 1) if head + 1 < heads else None
        weighed = weigh(head, scores)
        if last is not None:
            add_up(*last)
        last = (head, *weighed)
        scores = following
    add_up(*last)


def attend(queries, meta, sources, first, steps, heads, carry=None, final=False, into=None, held=0):
    rows, width = queries.shape
    block = heads * HD

    def spec(count, row, column):
        return pl.BlockSpec((count, block), lambda step, meta: (row(meta), column + step))

    def zero(meta):
        return 0

    operands, specs = [queries], [spec(rows, zero, first)]
    plan, keys_seen = [], 0
    for keys, values, usable in sources:
        for array, count, row, column in list(keys) + list(values):
            operands.append(array)
            specs.append(spec(count, row, column))
        keys_seen += keys[0][1]
        plan.append((len(keys), usable))
    if carry is not None:
        operands += list(carry)
        specs += [spec(rows, zero, held)] * 3
    aliases = {}
    if final:
        out_shape = jax.ShapeDtypeStruct((rows, width), jnp.bfloat16)
        out_specs = spec(rows, zero, first)
        if into is not None:
            aliases = {len(operands) + 1: 0}
            operands.append(into)
            specs.append(pl.BlockSpec(memory_space=pl.ANY))
    else:
        out_shape = [jax.ShapeDtypeStruct((rows, steps * block), jnp.float32)] * 3
        out_specs = [spec(rows, zero, 0)] * 3
    done = steps * block
    return pl.pallas_call(
        functools.partial(attend_kernel, plan, heads, carry is not None, final),
        name="attend_last" if final else "attend_more" if carry is not None else "attend_own",
        out_shape=out_shape,
        grid_spec=pltpu.PrefetchScalarGridSpec(
            num_scalar_prefetch=1, grid=(steps,), in_specs=specs, out_specs=out_specs
        ),
        input_output_aliases=aliases,
        compiler_params=pltpu.CompilerParams(vmem_limit_bytes=VMEM_LIMIT),
        cost_estimate=pl.CostEstimate(
            flops=4 * rows * keys_seen * done,
            bytes_accessed=4 * keys_seen * done + 2 * rows * done,
            transcendentals=rows * keys_seen * (done // HD),
        ),
    )(meta, *operands)


SCALAR = pl.BlockSpec(memory_space=pltpu.SMEM)
WHOLE = pl.BlockSpec(memory_space=pl.ANY)


def move(name, build, operands, specs, out_shape, out_specs, copies, moved, scratch=()):
    return pl.pallas_call(
        build,
        name=name,
        out_shape=out_shape,
        in_specs=specs,
        out_specs=out_specs,
        scratch_shapes=[*scratch, pltpu.SemaphoreType.DMA((copies,))],
        compiler_params=pltpu.CompilerParams(vmem_limit_bytes=VMEM_LIMIT),
        cost_estimate=pl.CostEstimate(flops=0, bytes_accessed=moved, transcendentals=0),
    )(*operands)


def in_hbm(array):
    return pltpu.with_memory_space_constraint(array, pltpu.HBM)


def tile_copies(sources, tile, target, sems, at):
    return [
        pltpu.make_async_copy(
            ref.at[pl.ds(pl.multiple_of(row + tile * TILE, TILE), TILE), pl.ds(first, target.shape[1])],
            target.at[pl.ds(n * TILE, TILE)],
            sems.at[at + n],
        )
        for n, (ref, row, first) in enumerate(sources)
    ]


def zero_copies(zeros, target, sems, at):
    return [
        pltpu.make_async_copy(zeros, target.at[pl.ds(n * TILE, TILE)], sems.at[at + n]) for n in (0, 1)
    ]


def start_if(condition, copies):
    @pl.when(condition)
    def _():
        for copy in copies:
            copy.start()


def tile_at(ref, entry, tile_count):
    return jnp.clip(ref[0, entry], 0, tile_count - 1)


def write_note(note, ref, tile_count):
    lane = lax.broadcasted_iota(jnp.int32, note.shape, 1)
    row = jnp.zeros(note.shape, jnp.float32)
    for entry in range(8):
        row = jnp.where(lane == entry, tile_at(ref, entry, tile_count).astype(jnp.float32), row)
    note[...] = row.astype(jnp.bfloat16)


def read_note(note, entry, tile_count):
    here = (lax.broadcasted_iota(jnp.int32, note.shape, 1) == entry) & (
        lax.broadcasted_iota(jnp.int32, note.shape, 0) == 0
    )
    value = jnp.sum(jnp.where(here, note.astype(jnp.float32), 0.0))
    return jnp.clip(value.astype(jnp.int32), 0, tile_count - 1)


def part_copies(k_ref, v_ref, first, width, target, sems, at):
    rows = k_ref.shape[0]
    return [
        pltpu.make_async_copy(
            ref.at[:, pl.ds(first, width)], target.at[pl.ds(n * rows, rows)], sems.at[at + n]
        )
        for n, ref in enumerate((k_ref, v_ref))
    ]


def begin(tile_lists, me, across_list, keys, values, width):
    rows, all_width = keys.shape
    tile_count = rows // TILE

    def build(me_ref, across_ref, list_hbm, k_ref, v_ref, meta, packed, to_across, list_ref, note, sems):
        read = pltpu.make_async_copy(list_hbm, list_ref, sems.at[5])
        read.start()
        me = me_ref[0]
        right = me % 4 >= 2
        copies = part_copies(k_ref, v_ref, 0, width, packed, sems, 0)
        tile = tile_at(across_ref, jnp.where(right, 5, 1), tile_count)
        copies += tile_copies(((k_ref, 0, 0), (v_ref, 0, 0)), tile, to_across, sems, 2)
        for copy in copies:
            copy.start()
        read.wait()
        write_note(note, list_ref, tile_count)
        last = pltpu.make_async_copy(
            note, packed.at[pl.ds(2 * rows, NOTE_ROWS), pl.ds(0, HD)], sems.at[4]
        )
        last.start()
        for entry in range(8):
            meta[entry] = tile_at(list_ref, entry, tile_count)
        meta[8] = me
        meta[9] = tile_at(across_ref, jnp.where(right, 1, 5), tile_count)
        for copy in copies + [last]:
            copy.wait()

    return move(
        "begin",
        build,
        (me, across_list, in_hbm(tile_lists), in_hbm(keys), in_hbm(values)),
        [SCALAR] * 2 + [WHOLE] * 3,
        [
            jax.ShapeDtypeStruct((10,), jnp.int32),
            jax.ShapeDtypeStruct((2 * rows + NOTE_ROWS, width), jnp.bfloat16),
            jax.ShapeDtypeStruct((2 * TILE, all_width), jnp.bfloat16),
        ],
        [SCALAR, WHOLE, WHOLE],
        6,
        8 * rows * width + 8 * TILE * all_width,
        [pltpu.SMEM(tile_lists.shape, jnp.int32), pltpu.VMEM((NOTE_ROWS, HD), jnp.bfloat16)],
    )


def choose_near(meta, beside_list, corner_list, keys, values):
    rows, width = keys.shape
    tile_count = rows // TILE

    def build(meta, beside_ref, corner_ref, k_ref, v_ref, known, to_beside, to_corner, zeros, sems):
        even = meta[8] % 2 == 0
        own = ((k_ref, 0, 0), (v_ref, 0, 0))
        copies = tile_copies(own, tile_at(beside_ref, jnp.where(even, 0, 4), tile_count), to_beside, sems, 0)
        for copy in copies:
            copy.start()
        for entry in range(10):
            known[entry] = meta[entry]
        tile = tile_at(corner_ref, jnp.where(even, 4, 0), tile_count)
        known[10] = tile
        inside = (meta[8] % 4 == 1) | (meta[8] % 4 == 2)
        start_if(inside, tile_copies(own, tile, to_corner, sems, 2))
        zeros[...] = jnp.zeros_like(zeros)
        blank = zero_copies(zeros, to_corner, sems, 2)
        start_if(jnp.logical_not(inside), blank)
        for copy in copies + blank:
            copy.wait()

    sent = jax.ShapeDtypeStruct((2 * TILE, width), jnp.bfloat16)
    return move(
        "choose_near",
        build,
        (meta, beside_list, corner_list, in_hbm(keys), in_hbm(values)),
        [SCALAR] * 3 + [WHOLE] * 2,
        [jax.ShapeDtypeStruct((11,), jnp.int32), sent, sent],
        [SCALAR, WHOLE, WHOLE],
        4,
        16 * TILE * width,
        [pltpu.VMEM((TILE, width), jnp.bfloat16)],
    )


def pack(keys, values, first, width, after):
    rows = keys.shape[0]

    def build(k_ref, v_ref, *refs):
        out_ref, stage, sems = refs[-3:]
        reads = part_copies(k_ref, v_ref, first, width, stage, sems, 0)
        writes = [
            pltpu.make_async_copy(
                stage.at[pl.ds(n * rows, rows)], out_ref.at[pl.ds(n * rows, rows)], sems.at[2 + n]
            )
            for n in (0, 1)
        ]
        for read in reads:
            read.start()
        for read, write in zip(reads, writes):
            read.wait()
            write.start()
        for write in writes:
            write.wait()

    return move(
        "pack",
        build,
        (in_hbm(keys), in_hbm(values), *after),
        [WHOLE] * (2 + len(after)),
        jax.ShapeDtypeStruct((2 * rows, width), jnp.bfloat16),
        WHOLE,
        4,
        8 * rows * width,
        [pltpu.VMEM((2 * rows, width), jnp.bfloat16)],
    )


def choose(meta, again, outer, inner, after):
    rows, width = outer.shape[0] // 2 // TILE * TILE, outer.shape[1]
    tile_count = rows // TILE

    def build(meta, outer, inner, *refs):
        if again:
            to_two, to_one, to_outer, to_inner = refs[-6:-2]
            wants = meta[11], meta[12]
        else:
            known, to_two, to_one, to_outer, to_inner, notes = refs[-8:-2]
        zeros, sems = refs[-2:]
        spot, plane = meta[8] % 4, meta[8] // 4
        right, odd = spot >= 2, plane % 2 == 1
        from_outer = ((outer, 0, 0), (outer, rows, 0))
        from_inner = ((inner, 0, 0), (inner, rows, 0))
        if not again:
            reads = [
                pltpu.make_async_copy(
                    ref.at[pl.ds(2 * rows, NOTE_ROWS), pl.ds(0, HD)], notes.at[n], sems.at[8 + n]
                )
                for n, ref in enumerate((outer, inner))
            ]
            for read in reads:
                read.start()
        edge = (spot == 0) | (spot == 3)
        for source, here in ((from_outer, right == odd), (from_inner, right != odd)):
            start_if(here, tile_copies(source, meta[9], to_two, sems, 0))
            start_if(here & edge, tile_copies(source, meta[10], to_one, sems, 2))
        zeros[...] = jnp.zeros_like(zeros)
        start_if(jnp.logical_not(edge), zero_copies(zeros, to_one, sems, 2))
        between = (plane == 1) | (plane == 2)
        start_if(
            jnp.logical_not(between),
            zero_copies(zeros, to_outer, sems, 4) + zero_copies(zeros, to_inner, sems, 6),
        )
        if not again:
            for read in reads:
                read.wait()
            wants = (
                read_note(notes[0], jnp.where(plane == 1, 7, 3), tile_count),
                read_note(notes[1], jnp.where(plane == 1, 3, 7), tile_count),
            )
            for entry in range(11):
                known[entry] = meta[entry]
            known[11], known[12] = wants
        start_if(
            between,
            tile_copies(from_inner, wants[0], to_outer, sems, 4)
            + tile_copies(from_outer, wants[1], to_inner, sems, 6),
        )
        for n, target in enumerate((to_two, to_one, to_outer, to_inner)):
            for copy in tile_copies(from_outer, 0, target, sems, 2 * n):
                copy.wait()

    sent = [jax.ShapeDtypeStruct((2 * TILE, width), jnp.bfloat16)] * 4
    return move(
        "choose_again" if again else "choose",
        build,
        (meta, outer, inner, *after),
        [SCALAR] + [WHOLE] * (2 + len(after)),
        ([] if again else [jax.ShapeDtypeStruct((13,), jnp.int32)]) + sent,
        [SCALAR] * (not again) + [WHOLE] * 4,
        10,
        32 * TILE * width,
        ([] if again else [pltpu.VMEM((2, NOTE_ROWS, HD), jnp.bfloat16)])
        + [pltpu.VMEM((TILE, width), jnp.bfloat16)],
    )


def send(array, route):
    return lax.ppermute(array, "frame", route)


def fixed(block):
    return lambda meta: block


def body_direct(queries, key_heads, value_heads, tile_lists):
    frames = lax.axis_size("frame")
    levels = frames.bit_length() - 1
    rows, width = key_heads.shape
    me = lax.axis_index("frame")
    lists = jnp.clip(lax.all_gather(tile_lists, "frame", tiled=True), 0, rows // TILE - 1)
    meta = me.astype(jnp.int32).reshape(1)
    sources = [([(key_heads, rows, fixed(0), 0)], [(value_heads, rows, fixed(0), 0)], None)]
    for level in range(levels):
        for entry, distance in ((level, 1 << level), (levels + level, -(1 << level))):
            route = [(i, i + distance) for i in range(frames) if 0 <= i + distance < frames]
            start = lists[jnp.clip(me + distance, 0, frames - 1), entry] * TILE
            both = [lax.dynamic_slice_in_dim(a, start, TILE, 0) for a in (key_heads, value_heads)]
            both = send(jnp.concatenate(both, axis=0), route)

            def usable(meta, distance=distance):
                return (meta[0] >= distance) & (meta[0] - distance < frames)

            sources.append(([(both, TILE, fixed(0), 0)], [(both, TILE, fixed(1), 0)], usable))
    return attend(queries, meta, sources, 0, width // (2 * HD), 2, final=True)


def body_planes(queries, key_heads, value_heads, tile_lists):
    frames = 16
    rows, width = key_heads.shape
    tile_count = rows // TILE
    heads = 4
    block = heads * HD
    parts = ((0, 2), (2, 1))
    every = range(frames)
    beside = [(i, i ^ 1) for i in every]
    across = [(i, i ^ 2) for i in every]
    corner_in = [(i, i ^ 3 if i % 4 in (1, 2) else i) for i in every]
    corner_out = [(i, i ^ 3 if i % 4 in (0, 3) else i) for i in every]
    outer = [(i, i ^ 4) for i in every]
    inner = [(i, i ^ 12 if i // 4 in (1, 2) else i) for i in every]

    def right(meta):
        return meta[8] % 4 >= 2

    def two_there(meta):
        return jnp.where(right(meta), meta[8] + 2 < frames, meta[8] >= 2)

    def one_there(meta):
        return (meta[8] >= 1) & (meta[8] < frames - 1)

    def outer_tile(meta):
        return jnp.where(meta[8] // 4 % 2 == 1, meta[2], meta[6])

    def inner_tile(meta):
        return jnp.where(meta[8] // 4 % 2 == 1, meta[6], meta[2])

    def inner_there(meta):
        return (meta[8] >= 4) & (meta[8] < frames - 4)

    def own_frame():
        return [(key_heads, rows, fixed(0), 0)], [(value_heads, rows, fixed(0), 0)], None

    def tile_of(array, tile, usable=None):
        return [(array, TILE, tile, 0)], [(array, TILE, lambda meta: tile(meta) + tile_count, 0)], usable

    def sent_tile(arrays, usable=None):
        return (
            [(a, TILE, fixed(0), column) for a, column in arrays],
            [(a, TILE, fixed(1), column) for a, column in arrays],
            usable,
        )

    me = lax.axis_index("frame").astype(jnp.int32).reshape(1)
    across_list = send(tile_lists, across)
    beside_list = send(tile_lists, beside)
    corner_list = send(across_list, beside)
    first_width = parts[0][1] * block
    meta, first, to_across = begin(tile_lists, me, across_list, key_heads, value_heads, first_width)
    over = send(to_across, across)
    known, to_beside, to_corner = choose_near(meta, beside_list, corner_list, key_heads, value_heads)
    next_to = send(to_beside, beside)
    one_in = send(to_corner, corner_in)
    second = pack(key_heads, value_heads, first_width, width - first_width, [to_beside])
    near = [own_frame(), sent_tile([(next_to, 0)]), sent_tile([(over, 0)])]
    begun = attend(queries, meta, near, 0, width // block, heads)

    after, again = [begun[0], one_in], False
    calls = []
    for (at, steps), packed in zip(parts, (first, second)):
        from_outer = send(packed, outer)
        from_inner = send(packed, inner)
        sent = choose(known, again, from_outer, from_inner, after)
        if not again:
            known, *sent = sent
        again = True
        two = send(sent[0], across)
        one = send(sent[1], corner_out)
        far = [send(sent[2], outer), send(sent[3], inner)]
        z_tiles = [tile_of(from_outer, outer_tile), tile_of(from_inner, inner_tile, inner_there)]
        late_tiles = [
            sent_tile([(two, 0)], two_there),
            sent_tile([(one_in, at), (one, 0)], one_there),
            sent_tile([(a, 0) for a in far]),
        ]
        after = []
        calls.append((at, steps, z_tiles, late_tiles))
    at, steps, z_tiles, late_tiles = calls[0]
    out = attend(queries, meta, z_tiles + late_tiles, at, steps, heads, begun, True, held=at)
    at, steps, z_tiles, late_tiles = calls[1]
    middle = attend(queries, meta, z_tiles, at, steps, heads, begun, held=at)
    return attend(queries, meta, late_tiles, at, steps, heads, middle, True, out)


def solution(mesh):
    body = body_planes if mesh.shape["frame"] == 16 else body_direct
    in_specs = (
        P(("groups", "frame"), None),
        P(("groups", "frame"), None),
        P(("groups", "frame"), None),
        P("frame", None),
    )
    out_specs = P(("groups", "frame"), None)
    return jax.shard_map(body, mesh=mesh, in_specs=in_specs, out_specs=out_specs, check_vma=False)
```

```python
import functools
import math

import jax
import jax.numpy as jnp
from jax import lax
from jax.experimental import pallas as pl
from jax.experimental.pallas import tpu as pltpu
from jax.sharding import PartitionSpec as P

HD = 128
TILE = 128
NOTE_ROWS = 16
LOG2_SCALE = math.log2(math.e) / math.sqrt(HD)
VMEM_LIMIT = 24 * 1024 * 1024


def attend_kernel(plan, heads, carry_in, final, meta, *refs):
    refs = list(refs)
    q_ref = refs.pop(0)
    sources = []
    for parts, usable in plan:
        k_refs = [refs.pop(0) for _ in range(parts)]
        v_refs = [refs.pop(0) for _ in range(parts)]
        bias = None
        if usable is not None:
            bias = jnp.where(usable(meta), 0.0, -jnp.inf).astype(jnp.float32)
        sources.append((k_refs, v_refs, bias))
    if carry_in:
        acc_in, sum_in, max_in = refs.pop(0), refs.pop(0), refs.pop(0)
    outs = refs[-1:] if final else refs[-3:]
    rows = q_ref.shape[0]

    def load(some, cols):
        total = some[0][:, cols]
        for other in some[1:]:
            total = total + other[:, cols]
        return total

    groups = [[s] for s in sources if s[0][0].shape[0] > TILE]
    narrow = [s for s in sources if s[0][0].shape[0] == TILE]
    groups += [narrow[at : at + 2] for at in range(0, len(narrow), 2)]

    def columns(head):
        return slice(head * HD, (head + 1) * HD)

    def scores_of(head):
        cols = columns(head)
        scores = []
        for group in groups:
            key = jnp.concatenate([load(k, cols) for k, _, _ in group], axis=0)
            part = lax.dot_general(
                q_ref[:, cols], key, (((1,), (1,)), ((), ())), preferred_element_type=jnp.float32
            )
            pieces = []
            at = 0
            for k, _, bias in group:
                for _ in range(k[0].shape[0] // TILE):
                    piece = part[:, at : at + TILE] * LOG2_SCALE
                    pieces.append(piece if bias is None else piece + bias)
                    at += TILE
            scores.append(pieces)
        return scores

    def weigh(head, scores):
        peak = functools.reduce(jnp.maximum, [piece for pieces in scores for piece in pieces])
        peak = jnp.broadcast_to(jnp.max(peak, axis=1, keepdims=True), (rows, HD))
        if carry_in:
            peak = jnp.maximum(max_in[:, columns(head)], peak)
        weights = [
            jnp.concatenate([jnp.exp2(piece - peak).astype(jnp.bfloat16) for piece in pieces], axis=1)
            for pieces in scores
        ]
        return peak, weights

    def add_up(head, peak, weights):
        cols = columns(head)
        acc = total = None
        if carry_in:
            shrink = jnp.exp2(max_in[:, cols] - peak)
            acc = acc_in[:, cols] * shrink
            total = sum_in[:, cols] * shrink
        for group, weight in zip(groups, weights):
            value = jnp.concatenate([load(v, cols) for _, v, _ in group], axis=0)
            both = jnp.concatenate([value, jnp.ones_like(value)], axis=1)
            added = jnp.dot(weight, both, preferred_element_type=jnp.float32)
            acc = added[:, :HD] if acc is None else acc + added[:, :HD]
            total = added[:, HD:] if total is None else total + added[:, HD:]
        if final:
            outs[0][:, cols] = (acc / total).astype(jnp.bfloat16)
        else:
            outs[0][:, cols] = acc
            outs[1][:, cols] = total
            outs[2][:, cols] = peak

    scores = scores_of(0)
    last = None
    for head in range(heads):
        following = scores_of(head + 1) if head + 1 < heads else None
        weighed = weigh(head, scores)
        if last is not None:
            add_up(*last)
        last = (head, *weighed)
        scores = following
    add_up(*last)


def attend(queries, meta, sources, first, steps, heads, carry=None, final=False, into=None, held=0):
    rows, width = queries.shape
    block = heads * HD

    def spec(count, row, column):
        return pl.BlockSpec((count, block), lambda step, meta: (row(meta), column + step))

    def zero(meta):
        return 0

    operands, specs = [queries], [spec(rows, zero, first)]
    plan, keys_seen = [], 0
    for keys, values, usable in sources:
        for array, count, row, column in list(keys) + list(values):
            operands.append(array)
            specs.append(spec(count, row, column))
        keys_seen += keys[0][1]
        plan.append((len(keys), usable))
    if carry is not None:
        operands += list(carry)
        specs += [spec(rows, zero, held)] * 3
    aliases = {}
    if final:
        out_shape = jax.ShapeDtypeStruct((rows, width), jnp.bfloat16)
        out_specs = spec(rows, zero, first)
        if into is not None:
            aliases = {len(operands) + 1: 0}
            operands.append(into)
            specs.append(pl.BlockSpec(memory_space=pl.ANY))
    else:
        out_shape = [jax.ShapeDtypeStruct((rows, steps * block), jnp.float32)] * 3
        out_specs = [spec(rows, zero, 0)] * 3
    done = steps * block
    return pl.pallas_call(
        functools.partial(attend_kernel, plan, heads, carry is not None, final),
        name="attend_last" if final else "attend_more" if carry is not None else "attend_own",
        out_shape=out_shape,
        grid_spec=pltpu.PrefetchScalarGridSpec(
            num_scalar_prefetch=1, grid=(steps,), in_specs=specs, out_specs=out_specs
        ),
        input_output_aliases=aliases,
        compiler_params=pltpu.CompilerParams(vmem_limit_bytes=VMEM_LIMIT),
        cost_estimate=pl.CostEstimate(
            flops=4 * rows * keys_seen * done,
            bytes_accessed=4 * keys_seen * done + 2 * rows * done,
            transcendentals=rows * keys_seen * (done // HD),
        ),
    )(meta, *operands)


SCALAR = pl.BlockSpec(memory_space=pltpu.SMEM)
WHOLE = pl.BlockSpec(memory_space=pl.ANY)


def move(name, build, operands, specs, out_shape, out_specs, copies, moved, scratch=()):
    return pl.pallas_call(
        build,
        name=name,
        out_shape=out_shape,
        in_specs=specs,
        out_specs=out_specs,
        scratch_shapes=[*scratch, pltpu.SemaphoreType.DMA((copies,))],
        compiler_params=pltpu.CompilerParams(vmem_limit_bytes=VMEM_LIMIT),
        cost_estimate=pl.CostEstimate(flops=0, bytes_accessed=moved, transcendentals=0),
    )(*operands)


def in_hbm(array):
    return pltpu.with_memory_space_constraint(array, pltpu.HBM)


def tile_copies(sources, tile, target, sems, at):
    return [
        pltpu.make_async_copy(
            ref.at[pl.ds(pl.multiple_of(row + tile * TILE, TILE), TILE), pl.ds(first, target.shape[1])],
            target.at[pl.ds(n * TILE, TILE)],
            sems.at[at + n],
        )
        for n, (ref, row, first) in enumerate(sources)
    ]


def zero_copies(zeros, target, sems, at):
    return [
        pltpu.make_async_copy(zeros, target.at[pl.ds(n * TILE, TILE)], sems.at[at + n]) for n in (0, 1)
    ]


def start_if(condition, copies):
    @pl.when(condition)
    def _():
        for copy in copies:
            copy.start()


def tile_at(ref, entry, tile_count):
    return jnp.clip(ref[0, entry], 0, tile_count - 1)


def write_note(note, ref, tile_count):
    lane = lax.broadcasted_iota(jnp.int32, note.shape, 1)
    row = jnp.zeros(note.shape, jnp.float32)
    for entry in range(8):
        row = jnp.where(lane == entry, tile_at(ref, entry, tile_count).astype(jnp.float32), row)
    note[...] = row.astype(jnp.bfloat16)


def read_note(note, entry, tile_count):
    here = (lax.broadcasted_iota(jnp.int32, note.shape, 1) == entry) & (
        lax.broadcasted_iota(jnp.int32, note.shape, 0) == 0
    )
    value = jnp.sum(jnp.where(here, note.astype(jnp.float32), 0.0))
    return jnp.clip(value.astype(jnp.int32), 0, tile_count - 1)


def part_copies(k_ref, v_ref, first, width, target, sems, at):
    rows = k_ref.shape[0]
    return [
        pltpu.make_async_copy(
            ref.at[:, pl.ds(first, width)], target.at[pl.ds(n * rows, rows)], sems.at[at + n]
        )
        for n, ref in enumerate((k_ref, v_ref))
    ]


def begin(tile_lists, me, across_list, keys, values, width):
    rows, all_width = keys.shape
    tile_count = rows // TILE

    def build(me_ref, across_any, list_hbm, k_ref, v_ref, meta, packed, to_across, list_ref, across_ref, note, sems):
        read = pltpu.make_async_copy(list_hbm, list_ref, sems.at[5])
        read_across = pltpu.make_async_copy(across_any, across_ref, sems.at[6])
        read_across.start()
        read.start()
        me = me_ref[0]
        right = me % 4 >= 2
        copies = part_copies(k_ref, v_ref, 0, width, packed, sems, 0)
        for copy in copies:
            copy.start()
        read_across.wait()
        tile = tile_at(across_ref, jnp.where(right, 5, 1), tile_count)
        tiles = tile_copies(((k_ref, 0, 0), (v_ref, 0, 0)), tile, to_across, sems, 2)
        for copy in tiles:
            copy.start()
        copies += tiles
        read.wait()
        write_note(note, list_ref, tile_count)
        last = pltpu.make_async_copy(
            note, packed.at[pl.ds(2 * rows, NOTE_ROWS), pl.ds(0, HD)], sems.at[4]
        )
        last.start()
        for entry in range(8):
            meta[entry] = tile_at(list_ref, entry, tile_count)
        meta[8] = me
        meta[9] = tile_at(across_ref, jnp.where(right, 1, 5), tile_count)
        for copy in copies + [last]:
            copy.wait()

    return move(
        "begin",
        build,
        (me, across_list, in_hbm(tile_lists), in_hbm(keys), in_hbm(values)),
        [SCALAR] + [WHOLE] * 4,
        [
            jax.ShapeDtypeStruct((10,), jnp.int32),
            jax.ShapeDtypeStruct((2 * rows + NOTE_ROWS, width), jnp.bfloat16),
            jax.ShapeDtypeStruct((2 * TILE, all_width), jnp.bfloat16),
        ],
        [SCALAR, WHOLE, WHOLE],
        7,
        8 * rows * width + 8 * TILE * all_width,
        [pltpu.SMEM(tile_lists.shape, jnp.int32)] * 2 + [pltpu.VMEM((NOTE_ROWS, HD), jnp.bfloat16)],
    )


def choose_near(meta, beside_list, corner_list, keys, values):
    rows, width = keys.shape
    tile_count = rows // TILE

    def build(meta, beside_ref, corner_ref, k_ref, v_ref, known, to_beside, to_corner, zeros, sems):
        even = meta[8] % 2 == 0
        own = ((k_ref, 0, 0), (v_ref, 0, 0))
        copies = tile_copies(own, tile_at(beside_ref, jnp.where(even, 0, 4), tile_count), to_beside, sems, 0)
        for copy in copies:
            copy.start()
        for entry in range(10):
            known[entry] = meta[entry]
        tile = tile_at(corner_ref, jnp.where(even, 4, 0), tile_count)
        known[10] = tile
        inside = (meta[8] % 4 == 1) | (meta[8] % 4 == 2)
        start_if(inside, tile_copies(own, tile, to_corner, sems, 2))
        zeros[...] = jnp.zeros_like(zeros)
        blank = zero_copies(zeros, to_corner, sems, 2)
        start_if(jnp.logical_not(inside), blank)
        for copy in copies + blank:
            copy.wait()

    sent = jax.ShapeDtypeStruct((2 * TILE, width), jnp.bfloat16)
    return move(
        "choose_near",
        build,
        (meta, beside_list, corner_list, in_hbm(keys), in_hbm(values)),
        [SCALAR] * 3 + [WHOLE] * 2,
        [jax.ShapeDtypeStruct((11,), jnp.int32), sent, sent],
        [SCALAR, WHOLE, WHOLE],
        4,
        16 * TILE * width,
        [pltpu.VMEM((TILE, width), jnp.bfloat16)],
    )


def pack(keys, values, first, width, after):
    rows = keys.shape[0]

    def build(k_ref, v_ref, *refs):
        out_ref, stage, sems = refs[-3:]
        reads = part_copies(k_ref, v_ref, first, width, stage, sems, 0)
        writes = [
            pltpu.make_async_copy(
                stage.at[pl.ds(n * rows, rows)], out_ref.at[pl.ds(n * rows, rows)], sems.at[2 + n]
            )
            for n in (0, 1)
        ]
        for read in reads:
            read.start()
        for read, write in zip(reads, writes):
            read.wait()
            write.start()
        for write in writes:
            write.wait()

    return move(
        "pack",
        build,
        (in_hbm(keys), in_hbm(values), *after),
        [WHOLE] * (2 + len(after)),
        jax.ShapeDtypeStruct((2 * rows, width), jnp.bfloat16),
        WHOLE,
        4,
        8 * rows * width,
        [pltpu.VMEM((2 * rows, width), jnp.bfloat16)],
    )


def choose(meta, again, outer, inner, after):
    rows, width = outer.shape[0] // 2 // TILE * TILE, outer.shape[1]
    tile_count = rows // TILE

    def build(meta, outer, inner, *refs):
        if again:
            to_two, to_one, to_outer, to_inner = refs[-6:-2]
            wants = meta[11], meta[12]
        else:
            known, to_two, to_one, to_outer, to_inner, notes = refs[-8:-2]
        zeros, sems = refs[-2:]
        spot, plane = meta[8] % 4, meta[8] // 4
        right, odd = spot >= 2, plane % 2 == 1
        from_outer = ((outer, 0, 0), (outer, rows, 0))
        from_inner = ((inner, 0, 0), (inner, rows, 0))
        if not again:
            reads = [
                pltpu.make_async_copy(
                    ref.at[pl.ds(2 * rows, NOTE_ROWS), pl.ds(0, HD)], notes.at[n], sems.at[8 + n]
                )
                for n, ref in enumerate((outer, inner))
            ]
            for read in reads:
                read.start()
        edge = (spot == 0) | (spot == 3)
        for source, here in ((from_outer, right == odd), (from_inner, right != odd)):
            start_if(here, tile_copies(source, meta[9], to_two, sems, 0))
            start_if(here & edge, tile_copies(source, meta[10], to_one, sems, 2))
        zeros[...] = jnp.zeros_like(zeros)
        start_if(jnp.logical_not(edge), zero_copies(zeros, to_one, sems, 2))
        between = (plane == 1) | (plane == 2)
        start_if(
            jnp.logical_not(between),
            zero_copies(zeros, to_outer, sems, 4) + zero_copies(zeros, to_inner, sems, 6),
        )
        if not again:
            for read in reads:
                read.wait()
            wants = (
                read_note(notes[0], jnp.where(plane == 1, 7, 3), tile_count),
                read_note(notes[1], jnp.where(plane == 1, 3, 7), tile_count),
            )
            for entry in range(11):
                known[entry] = meta[entry]
            known[11], known[12] = wants
        start_if(
            between,
            tile_copies(from_inner, wants[0], to_outer, sems, 4)
            + tile_copies(from_outer, wants[1], to_inner, sems, 6),
        )
        for n, target in enumerate((to_two, to_one, to_outer, to_inner)):
            for copy in tile_copies(from_outer, 0, target, sems, 2 * n):
                copy.wait()

    sent = [jax.ShapeDtypeStruct((2 * TILE, width), jnp.bfloat16)] * 4
    return move(
        "choose_again" if again else "choose",
        build,
        (meta, outer, inner, *after),
        [SCALAR] + [WHOLE] * (2 + len(after)),
        ([] if again else [jax.ShapeDtypeStruct((13,), jnp.int32)]) + sent,
        [SCALAR] * (not again) + [WHOLE] * 4,
        10,
        32 * TILE * width,
        ([] if again else [pltpu.VMEM((2, NOTE_ROWS, HD), jnp.bfloat16)])
        + [pltpu.VMEM((TILE, width), jnp.bfloat16)],
    )


def send(array, route):
    return lax.ppermute(array, "frame", route)


def fixed(block):
    return lambda meta: block


def body_direct(queries, key_heads, value_heads, tile_lists):
    frames = lax.axis_size("frame")
    levels = frames.bit_length() - 1
    rows, width = key_heads.shape
    me = lax.axis_index("frame")
    lists = jnp.clip(lax.all_gather(tile_lists, "frame", tiled=True), 0, rows // TILE - 1)
    meta = me.astype(jnp.int32).reshape(1)
    sources = [([(key_heads, rows, fixed(0), 0)], [(value_heads, rows, fixed(0), 0)], None)]
    for level in range(levels):
        for entry, distance in ((level, 1 << level), (levels + level, -(1 << level))):
            route = [(i, i + distance) for i in range(frames) if 0 <= i + distance < frames]
            start = lists[jnp.clip(me + distance, 0, frames - 1), entry] * TILE
            both = [lax.dynamic_slice_in_dim(a, start, TILE, 0) for a in (key_heads, value_heads)]
            both = send(jnp.concatenate(both, axis=0), route)

            def usable(meta, distance=distance):
                return (meta[0] >= distance) & (meta[0] - distance < frames)

            sources.append(([(both, TILE, fixed(0), 0)], [(both, TILE, fixed(1), 0)], usable))
    return attend(queries, meta, sources, 0, width // (2 * HD), 2, final=True)


def body_planes(queries, key_heads, value_heads, tile_lists):
    frames = 16
    rows, width = key_heads.shape
    tile_count = rows // TILE
    heads = 4
    block = heads * HD
    parts = ((0, 2), (2, 1))
    every = range(frames)
    beside = [(i, i ^ 1) for i in every]
    across = [(i, i ^ 2) for i in every]
    corner_in = [(i, i ^ 3 if i % 4 in (1, 2) else i) for i in every]
    corner_out = [(i, i ^ 3 if i % 4 in (0, 3) else i) for i in every]
    outer = [(i, i ^ 4) for i in every]
    inner = [(i, i ^ 12 if i // 4 in (1, 2) else i) for i in every]

    def right(meta):
        return meta[8] % 4 >= 2

    def two_there(meta):
        return jnp.where(right(meta), meta[8] + 2 < frames, meta[8] >= 2)

    def one_there(meta):
        return (meta[8] >= 1) & (meta[8] < frames - 1)

    def outer_tile(meta):
        return jnp.where(meta[8] // 4 % 2 == 1, meta[2], meta[6])

    def inner_tile(meta):
        return jnp.where(meta[8] // 4 % 2 == 1, meta[6], meta[2])

    def inner_there(meta):
        return (meta[8] >= 4) & (meta[8] < frames - 4)

    def own_frame():
        return [(key_heads, rows, fixed(0), 0)], [(value_heads, rows, fixed(0), 0)], None

    def tile_of(array, tile, usable=None):
        return [(array, TILE, tile, 0)], [(array, TILE, lambda meta: tile(meta) + tile_count, 0)], usable

    def sent_tile(arrays, usable=None):
        return (
            [(a, TILE, fixed(0), column) for a, column in arrays],
            [(a, TILE, fixed(1), column) for a, column in arrays],
            usable,
        )

    me = lax.axis_index("frame").astype(jnp.int32).reshape(1)
    across_list = send(tile_lists, across)
    beside_list = send(tile_lists, beside)
    corner_list = send(across_list, beside)
    first_width = parts[0][1] * block
    meta, first, to_across = begin(tile_lists, me, across_list, key_heads, value_heads, first_width)
    over = send(to_across, across)
    known, to_beside, to_corner = choose_near(meta, beside_list, corner_list, key_heads, value_heads)
    next_to = send(to_beside, beside)
    one_in = send(to_corner, corner_in)
    second = pack(key_heads, value_heads, first_width, width - first_width, [to_beside])
    near = [own_frame(), sent_tile([(next_to, 0)]), sent_tile([(over, 0)])]
    begun = attend(queries, meta, near, 0, width // block, heads)

    after, again = [begun[0], one_in], False
    calls = []
    for (at, steps), packed in zip(parts, (first, second)):
        from_outer = send(packed, outer)
        from_inner = send(packed, inner)
        sent = choose(known, again, from_outer, from_inner, after)
        if not again:
            known, *sent = sent
        again = True
        two = send(sent[0], across)
        one = send(sent[1], corner_out)
        far = [send(sent[2], outer), send(sent[3], inner)]
        z_tiles = [tile_of(from_outer, outer_tile), tile_of(from_inner, inner_tile, inner_there)]
        late_tiles = [
            sent_tile([(two, 0)], two_there),
            sent_tile([(one_in, at), (one, 0)], one_there),
            sent_tile([(a, 0) for a in far]),
        ]
        after = []
        calls.append((at, steps, z_tiles, late_tiles))
    at, steps, z_tiles, late_tiles = calls[0]
    out = attend(queries, meta, z_tiles + late_tiles, at, steps, heads, begun, True, held=at)
    at, steps, z_tiles, late_tiles = calls[1]
    middle = attend(queries, meta, z_tiles, at, steps, heads, begun, held=at)
    return attend(queries, meta, late_tiles, at, steps, heads, middle, True, out)


def solution(mesh):
    body = body_planes if mesh.shape["frame"] == 16 else body_direct
    in_specs = (
        P(("groups", "frame"), None),
        P(("groups", "frame"), None),
        P(("groups", "frame"), None),
        P("frame", None),
    )
    out_specs = P(("groups", "frame"), None)
    return jax.shard_map(body, mesh=mesh, in_specs=in_specs, out_specs=out_specs, check_vma=False)
```
